32 devices in a mesh: section: 4 (over y, x), expert: 8 (over z, core).
Axes of the slice: x: 2, y: 2, z: 4, core: 2. Of those that a mesh axis runs over, the one named last changes fastest.
Arguments:
- tokens_in: bfloat16 [4, 256, 3584], P('section', 'expert'), may hold values from -6 to 6
- cotangent: bfloat16 [4, 256, 3584], P('section', 'expert'), may hold values from -6 to 6
- norm_gain: float32 [4, 3584], P('section'), may hold values from 0.1 to 1.9
- w_gate: bfloat16 [4, 8, 3584, 512], P('section', 'expert'), may hold values from -0.09375 to 0.09375
- w_up: bfloat16 [4, 8, 3584, 512], P('section', 'expert'), may hold values from -0.09375 to 0.09375
- w_down: bfloat16 [4, 8, 512, 3584], P('section', 'expert'), may hold values from -0.1875 to 0.1875
- expert_ids: int32 [4, 4, 256, 1], P('section', None, 'expert'), may hold values from 0 to 3; in each aligned block of 32 rows (0 to 31, 32 to 63, ..., all dimensions but the last counted through in order) at most 16 rows name the same one
- gate_weights: float32 [4, 4, 256, 1], P('section', None, 'expert'), may hold values from 0.2 to 1
Outputs:
- grad_inputs: bfloat16 [4, 4, 256, 3584], P('section', None, 'expert')
- grad_gates: float32 [4, 4, 256, 1], P('section', None, 'expert')
The draws below stay inside these ranges and needn't reach their ends.
Inputs may be any that keep to these rules, and one draw needn't show every extreme that they name: `expert_ids`: within each aligned block of 32 tokens of one layer and micro-batch no expert is named more than 16 times, a bound that some block reaches; each token names one expert.
All inputs are finite; a program needn't handle non-finite values.
Results may differ from the reference program's by a relative error of at most 0.025.
Values may be sent and summed in bfloat16 or wider, within the bound.
No kernel may reach another device: no remote copies, remote signals or barrier semaphores. Data moves between devices by JAX's collectives and lax.ppermute only.
A program may use at most 192 MiB of HBM per device.

```python
import math
import jax
import jax.numpy as jnp
import numpy as np
from jax import lax

D = 3584
FF = 1024
TOP = 1
TOK_DEV = 32
EXPERTS = 4
FF_DEV = 512
CAP = 16
MICRO = 4
TOKENS = 256
N_SECTION = 4
N_EXPERT = 8


def block_levels(stream_key, dims, cuts, smallest, largest):
    def one(dim, parts):
        heights = jax.random.uniform(jax.random.fold_in(jax.random.fold_in(stream_key, 6), dim), (parts,), jnp.float32, smallest / len(cuts), largest / len(cuts))
        return jnp.repeat(jnp.exp(heights), dims[dim] // parts).reshape((-1,) + (1,) * (len(dims) - dim - 1))

    loudness = one(*cuts[0])
    for cut in cuts[1:]:
        loudness = loudness * one(*cut)
    return loudness


def routed_block(key, own, number, rows, amount, top, bound, slope):
    ranking = jax.random.permutation(key, amount)
    crowded, common = load_shares(amount, rows * top, bound, slope, True), load_shares(amount, rows * top, bound, slope, False)
    places = jnp.arange(amount)

    def named(sizes, rotation):
        used = int((sizes > 0).sum())
        fixed = max(1, used // 4)
        passed = fixed + (places - fixed + rotation * (used - fixed)) % max(1, amount - fixed)
        return jnp.zeros((amount,), jnp.int32).at[ranking[jnp.where(places < fixed, places, passed)]].set(jnp.asarray(sizes, jnp.int32))

    sizes = jnp.where(number % 4 == 0, named(crowded, number // 4), named(common, number - number // 4 - 1))
    mixed = jax.random.permutation(jax.random.fold_in(own, 3), amount)
    giver, taker = mixed[0:amount // 2 * 2:2], mixed[1:amount // 2 * 2:2]
    slack = jnp.minimum(sizes[giver] - 1, bound - sizes[taker]) // 2
    slack = jnp.where((giver == ranking[0]) | (taker == ranking[0]) | (sizes[taker] == 0), 0, jnp.maximum(slack, 0))
    passed = jax.random.randint(jax.random.fold_in(own, 4), (amount // 2,), 0, 1 << 20) % (slack + 1)
    sizes = sizes.at[giver].add(-passed).at[taker].add(passed)
    items = jnp.searchsorted(jnp.cumsum(sizes), jnp.arange(rows * top), side="right").astype(jnp.int32)
    listing = items.reshape(top, rows).T
    listing = listing[jax.random.permutation(jax.random.fold_in(own, 1), rows)]
    rotation = jax.random.randint(jax.random.fold_in(own, 2), (rows, 1), 0, top)
    return jnp.take_along_axis(listing, (jnp.arange(top)[None, :] + rotation) % top, axis=1)


def load_shares(count, total, most, slope, full):
    weights = [(1 << 20) // math.isqrt(standing ** slope) + 1 for standing in range(1, count + 1)]
    largest = most if full else min(most, max(-(-total // count), total * weights[0] // sum(weights)))
    least = 1 if total - largest >= count - 1 else 0
    given, rest = [largest] + [least] * (count - 1), total - largest - least * (count - 1)
    while rest > 0:
        candidates = [i for i in range(1, count) if given[i] < largest] or [i for i in range(1, count) if given[i] < most]
        pool, remaining = sum([weights[i] for i in candidates]), rest
        for i in candidates:
            more = min(most - given[i], max(1, remaining * weights[i] // pool), rest)
            given[i] = given[i] + more
            rest = rest - more
    return np.array(given)


def normal_values(key, shape, width, most, pieces=(), kind=jnp.bfloat16):
    factor_of = block_levels(key, shape, pieces, -0.22, 0.18) if pieces else 1.0
    entries = jax.random.normal(key, shape, jnp.float32) * width * factor_of
    return jnp.minimum(jnp.maximum(entries, -most), most).astype(kind)


def setup_inputs(seed: int = 0) -> dict:
    key_list = jax.random.split(jax.random.key(seed), 9)
    tokens_in = normal_values(key_list[0], (MICRO, TOKENS, D), 1.0, 6.0, ((0, 4), (1, 8)))
    cotangent = normal_values(key_list[1], (MICRO, TOKENS, D), 1.0, 6.0, ((0, 4), (1, 8)))
    norm_gain = jnp.clip(1.0 + 0.18 * jax.random.normal(key_list[2], (N_SECTION, D), jnp.float32), 0.1, 1.9)
    w_gate = normal_values(key_list[3], (N_SECTION, N_EXPERT, D, FF_DEV), D ** -0.5, 0.09375, ((0, 4), (1, 8)))
    w_up = normal_values(key_list[4], (N_SECTION, N_EXPERT, D, FF_DEV), D ** -0.5, 0.09375, ((0, 4), (1, 8)))
    w_down = normal_values(key_list[5], (N_SECTION, N_EXPERT, FF_DEV, D), FF ** -0.5, 0.1875, ((0, 4), (1, 8)))
    expert_ids_keys = jax.random.split(jax.random.fold_in(key_list[6], 1), N_SECTION * MICRO * TOKENS // TOK_DEV)
    expert_ids_turns = jax.random.permutation(jax.random.fold_in(key_list[6], 3), N_SECTION * MICRO * TOKENS // TOK_DEV)
    expert_ids = jax.vmap(lambda own, number: routed_block(jax.random.fold_in(key_list[6], 2), own, number, TOK_DEV, EXPERTS, TOP, CAP, 1))(expert_ids_keys, expert_ids_turns).reshape((N_SECTION, MICRO, TOKENS, TOP))
    gate_weights = jnp.clip(0.2 + 0.8 * jax.random.uniform(key_list[7], (N_SECTION, MICRO, TOKENS, TOP), jnp.float32) ** block_levels(key_list[7], (N_SECTION, MICRO, TOKENS, TOP), ((0, 4), (2, 8)), -0.2, 0.2), 0.2, 1.0)
    return dict(tokens_in=tokens_in, cotangent=cotangent, norm_gain=norm_gain, w_gate=w_gate, w_up=w_up, w_down=w_down, expert_ids=expert_ids, gate_weights=gate_weights)


epsilon = 1e-06

def norm_rows(layer_in, gain_row):
    values = layer_in.astype(jnp.float32)
    inv_rms = lax.rsqrt(lax.optimization_barrier(jnp.mean(values * values, axis=-1, keepdims=True)) + epsilon)
    normed = (values * inv_rms * gain_row).astype(jnp.bfloat16)
    return (values, inv_rms, normed)

def slot_tables(route_ids):
    flat_ids = route_ids.reshape(N_EXPERT, TOK_DEV * TOP).astype(jnp.int32)
    one_hot = (flat_ids[:, :, None] == jnp.arange(EXPERTS, dtype=jnp.int32)[None, None, :]).astype(jnp.int32)
    position = lax.optimization_barrier(jnp.sum((jnp.cumsum(one_hot, axis=1, dtype=jnp.int32) - 1) * one_hot, axis=-1, dtype=jnp.int32))
    source = jnp.broadcast_to(jnp.arange(N_EXPERT, dtype=jnp.int32)[:, None], flat_ids.shape)
    return (flat_ids.reshape(-1), source.reshape(-1), position.reshape(-1))

def scatter_rows(row_block, expert_of, source, position):
    buffer = jnp.zeros((EXPERTS, N_EXPERT, CAP, D), row_block.dtype)
    buffer = buffer.at[expert_of, source, position].set(row_block)
    return buffer.reshape(EXPERTS, N_EXPERT * CAP, D)

def expert_forward(operands):
    row_block, gate_pair, up_pair, down_pair = operands
    total = jnp.zeros((row_block.shape[0], D), jnp.float32)
    for half_index in range(2):
        gate_pre = jnp.dot(row_block, gate_pair[half_index], preferred_element_type=jnp.float32)
        up_pre = jnp.dot(row_block, up_pair[half_index], preferred_element_type=jnp.float32)
        hidden = (jax.nn.silu(gate_pre) * up_pre).astype(jnp.bfloat16)
        half_out = jnp.dot(hidden, down_pair[half_index], preferred_element_type=jnp.float32).astype(jnp.bfloat16)
        total = total + lax.optimization_barrier(half_out).astype(jnp.float32)
    return total

def expert_backward(operands):
    row_block, grad_block, gate_pair, up_pair, down_pair = operands
    total = jnp.zeros((row_block.shape[0], D), jnp.float32)
    for half_index in range(2):
        gate_pre = jnp.dot(row_block, gate_pair[half_index], preferred_element_type=jnp.float32)
        up_pre = jnp.dot(row_block, up_pair[half_index], preferred_element_type=jnp.float32)
        sigma = jax.nn.sigmoid(gate_pre)
        grad_hidden = jnp.dot(grad_block, down_pair[half_index].T, preferred_element_type=jnp.float32)
        grad_gate = (grad_hidden * up_pre * sigma * (1.0 + gate_pre * (1.0 - sigma))).astype(jnp.bfloat16)
        grad_up = (grad_hidden * gate_pre * sigma).astype(jnp.bfloat16)
        half_grad = jnp.dot(grad_gate, gate_pair[half_index].T, preferred_element_type=jnp.float32)
        half_grad = half_grad + jnp.dot(grad_up, up_pair[half_index].T, preferred_element_type=jnp.float32)
        total = total + lax.optimization_barrier(half_grad.astype(jnp.bfloat16)).astype(jnp.float32)
    return total

def reference(tokens_in, cotangent, norm_gain, w_gate, w_up, w_down, expert_ids, gate_weights):
    gate_sets = [w_gate[layer].reshape(EXPERTS, 2, D, FF_DEV) for layer in range(N_SECTION)]
    up_sets = [w_up[layer].reshape(EXPERTS, 2, D, FF_DEV) for layer in range(N_SECTION)]
    down_sets = [w_down[layer].reshape(EXPERTS, 2, FF_DEV, D) for layer in range(N_SECTION)]
    grad_table = [[None] * MICRO for layer in range(N_SECTION)]
    gate_table = [[None] * MICRO for layer in range(N_SECTION)]
    for micro_index in range(MICRO):
        layer_in = tokens_in[micro_index]
        saved = []
        for layer in range(N_SECTION):
            values, inv_rms, normed = norm_rows(layer_in, norm_gain[layer])
            expert_of, source, position = slot_tables(expert_ids[layer, micro_index])
            dispatched = scatter_rows(jnp.repeat(normed, TOP, axis=0), expert_of, source, position)
            combined = lax.map(expert_forward, (dispatched, gate_sets[layer], up_sets[layer], down_sets[layer]))
            combined = combined.reshape(EXPERTS, N_EXPERT, CAP, D)
            expert_rows = combined[expert_of, source, position].reshape(TOKENS, TOP, D)
            mixed = lax.optimization_barrier(jnp.sum(gate_weights[layer, micro_index][:, :, None] * expert_rows, axis=1))
            saved.append((values, inv_rms, dispatched, expert_rows, expert_of, source, position))
            layer_in = (values + mixed).astype(jnp.bfloat16)
        grad_next = cotangent[micro_index]
        for layer in range(N_SECTION - 1, -1, -1):
            values, inv_rms, dispatched, expert_rows, expert_of, source, position = saved[layer]
            grad_f = grad_next.astype(jnp.float32)
            gate_table[layer][micro_index] = lax.optimization_barrier(jnp.sum(grad_f[:, None, :] * expert_rows, axis=-1))
            grad_rows = (gate_weights[layer, micro_index][:, :, None] * grad_f[:, None, :]).astype(jnp.bfloat16)
            grad_disp = scatter_rows(grad_rows.reshape(TOKENS * TOP, D), expert_of, source, position)
            returned = lax.map(expert_backward, (dispatched, grad_disp, gate_sets[layer], up_sets[layer], down_sets[layer]))
            returned = returned.reshape(EXPERTS, N_EXPERT, CAP, D)
            grad_norm = lax.optimization_barrier(jnp.sum(returned[expert_of, source, position].reshape(TOKENS, TOP, D), axis=1))
            scaled = grad_norm * norm_gain[layer]
            grad_in = grad_f + inv_rms * scaled - values * (inv_rms * inv_rms * inv_rms) * lax.optimization_barrier(jnp.mean(values * scaled, axis=-1, keepdims=True))
            grad_next = grad_in.astype(jnp.bfloat16)
            grad_table[layer][micro_index] = grad_next
    grad_inputs = jnp.stack([jnp.stack(grad_table[layer]) for layer in range(N_SECTION)])
    grad_gates = jnp.stack([jnp.stack(gate_table[layer]) for layer in range(N_SECTION)])
    return (grad_inputs, grad_gates)
```

```python
from functools import partial

import jax
import jax.numpy as jnp
from jax import lax
from jax.experimental import pallas as pl
from jax.experimental.pallas import tpu as pltpu
from jax.sharding import PartitionSpec as P

epsilon = 1e-06
both = ("section", "expert")
last_with_last = (((1,), (1,)), ((), ()))

in_vmem = pl.BlockSpec(memory_space=pltpu.VMEM)
in_smem = pl.BlockSpec(memory_space=pltpu.SMEM)
anywhere = pl.BlockSpec(memory_space=pl.ANY)


def spans(total, size):
    size = size if total % size == 0 else total
    return [pl.ds(start, size) for start in range(0, total, size)]


def params(mib):
    return pltpu.CompilerParams(vmem_limit_bytes=mib * 2**20)


def product(left, right):
    return jnp.dot(left, right, preferred_element_type=jnp.float32)


def product_t(left, right):
    return lax.dot_general(left, right, last_with_last, preferred_element_type=jnp.float32)


def weight_copies(half_refs, buffers, sems):
    return [
        [
            pltpu.make_async_copy(half_refs[half][which], buffers[which].at[half], sems.at[which, half])
            for half in range(2)
        ]
        for which in range(3)
    ]


def forward_kernel(slot, micro_count, parts, *refs):
    sec_ref, gain_ref, route_ref = refs[:3]
    x_refs = refs[3 : 3 + parts]
    rest = refs[3 + parts :]
    half_refs = [rest[0:3], rest[3:6]]
    out_refs = rest[6 : 6 + parts]
    save_x, save_gate, save_up, save_rows = rest[6 + parts : 10 + parts]
    gate_buf, up_buf, down_buf, normed, hidden, sems = rest[10 + parts :]
    micro = slot - sec_ref[0]
    width = gain_ref.shape[1]
    hidden_dim = gate_buf.shape[2]
    rows = x_refs[0].shape[0]

    @pl.when((micro >= 0) & (micro < micro_count))
    def _():
        copies = weight_copies(half_refs, (gate_buf, up_buf, down_buf), sems)
        for half in range(2):
            copies[0][half].start()
            copies[1][half].start()
        for half in range(2):
            copies[2][half].start()
        for part in range(parts):
            block = x_refs[part][...]
            values = block.astype(jnp.float32)
            inv_rms = lax.rsqrt(jnp.mean(values * values, axis=-1, keepdims=True) + epsilon)
            here = pl.ds(part * rows, rows)
            normed[here, :] = (values * inv_rms * gain_ref[...]).astype(jnp.bfloat16)
            save_x[here, :] = block
        for half in range(2):
            side = pl.ds(half * hidden_dim, hidden_dim)
            copies[0][half].wait()
            gate_pre = product(normed[...], gate_buf[half])
            copies[1][half].wait()
            up_pre = product(normed[...], up_buf[half])
            save_gate[:, side] = gate_pre
            save_up[:, side] = up_pre
            hidden[half] = (gate_pre * jax.nn.sigmoid(gate_pre) * up_pre).astype(jnp.bfloat16)
        copies[2][0].wait()
        copies[2][1].wait()
        route = route_ref[micro]
        for span in spans(width, 256):
            made = product(hidden[0], down_buf[0, :, span])
            made = made + product(hidden[1], down_buf[1, :, span])
            save_rows[:, span] = made
            added = route * made
            for part in range(parts):
                here = slice(part * rows, (part + 1) * rows)
                values = x_refs[part][:, span].astype(jnp.float32)
                out_refs[part][:, span] = (values + added[here]).astype(jnp.bfloat16)


def backward_kernel(slot, counts, candidates, parts, *refs):
    section_count, micro_count = counts
    sec_ref, gain_ref, route_ref = refs[:3]
    rest = refs[3:]
    arrived = rest[:parts]
    first = rest[parts : 2 * parts]
    rest = rest[2 * parts :]
    half_refs = [rest[0:3], rest[3:6]]
    rest = rest[6:]
    saved = {}
    for section in candidates:
        saved[section] = rest[:4]
        rest = rest[4:]
    out_refs = rest[:parts]
    gate_out = rest[parts]
    (gate_buf, up_buf, down_buf, grad_buf, x_buf, pre_gate, pre_up, rows_buf, grad_rows, scaled_buf,
     sems, state_sems, grad_sems) = rest[parts + 1 :]
    sec = sec_ref[0]
    micro = slot - 2 * (section_count - 1) + sec
    width = gain_ref.shape[1]
    hidden_dim = gate_buf.shape[2]
    slots = grad_buf.shape[0]
    rows = slots // parts

    @pl.when((micro >= 0) & (micro < micro_count))
    def _():
        def for_section(section, act):
            @pl.when(sec == section)
            def _():
                for part in range(parts):
                    if section == section_count - 1:
                        source = first[part].at[slot - (section_count - 1)]
                    else:
                        source = arrived[part]
                    act(pltpu.make_async_copy(
                        source, grad_buf.at[pl.ds(part * rows, rows), :], grad_sems.at[part]
                    ))
                targets = (rows_buf, x_buf, pre_gate, pre_up)
                for number, target in enumerate(targets):
                    act(pltpu.make_async_copy(
                        saved[section][number], target, state_sems.at[number]
                    ))

        for section in candidates:
            for_section(section, lambda copy: copy.start())
        copies = weight_copies(half_refs, (gate_buf, up_buf, down_buf), sems)
        for half in range(2):
            copies[2][half].start()
        for half in range(2):
            copies[0][half].start()
            copies[1][half].start()
        for section in candidates:
            for_section(section, lambda copy: copy.wait())
        route = route_ref[micro]
        gate_grad = jnp.zeros((slots, 1), jnp.float32)
        square = jnp.zeros((slots, 1), jnp.float32)
        for span in spans(width, 512):
            grad_f = grad_buf[:, span].astype(jnp.float32)
            gate_grad += jnp.sum(grad_f * rows_buf[:, span], axis=-1, keepdims=True)
            grad_rows[:, span] = (route * grad_f).astype(jnp.bfloat16)
            values = x_buf[:, span].astype(jnp.float32)
            square += jnp.sum(values * values, axis=-1, keepdims=True)
        gate_out[...] = jnp.broadcast_to(gate_grad, gate_out.shape)
        inv_rms = lax.rsqrt(square / width + epsilon)
        grads = []
        for half in range(2):
            side = pl.ds(half * hidden_dim, hidden_dim)
            copies[2][half].wait()
            grad_hidden = product_t(grad_rows[...], down_buf[half])
            gate_pre = pre_gate[:, side]
            sigma = jax.nn.sigmoid(gate_pre)
            grad_gate = grad_hidden * pre_up[:, side] * sigma * (1.0 + gate_pre * (1.0 - sigma))
            grad_up = grad_hidden * gate_pre * sigma
            grads.append((grad_gate.astype(jnp.bfloat16), grad_up.astype(jnp.bfloat16)))
        for half in range(2):
            copies[0][half].wait()
            copies[1][half].wait()
        dotted = jnp.zeros((slots, 1), jnp.float32)
        for span in spans(width, 256):
            total = product_t(grads[0][0], gate_buf[0, span, :])
            total = total + product_t(grads[0][1], up_buf[0, span, :])
            total = total + product_t(grads[1][0], gate_buf[1, span, :])
            total = total + product_t(grads[1][1], up_buf[1, span, :])
            scaled = total * gain_ref[:, span]
            scaled_buf[:, span] = scaled
            dotted += jnp.sum(x_buf[:, span].astype(jnp.float32) * scaled, axis=-1, keepdims=True)
        back = inv_rms * inv_rms * inv_rms * (dotted / width)
        for span in spans(width, 512):
            grad_in = (
                grad_buf[:, span].astype(jnp.float32)
                + inv_rms * scaled_buf[:, span]
                - x_buf[:, span].astype(jnp.float32) * back
            ).astype(jnp.bfloat16)
            for part in range(parts):
                out_refs[part][:, span] = grad_in[part * rows : (part + 1) * rows]


def forward_router(slot, micro_count, parts, has_first, has_rest, *refs):
    sec_ref, place_ref, move_ref = refs[:3]
    rest = refs[3:]
    tokens_ref = rest[0] if has_first else None
    rest = rest[1:] if has_first else rest
    arrived = rest[:parts] if has_rest else None
    rest = rest[parts:] if has_rest else rest
    out_refs = rest[:parts]
    sec = sec_ref[0]
    micro = slot - sec
    width = out_refs[0].shape[1]
    rows = out_refs[0].shape[0]

    def put(table, source):
        for span in spans(width, 512):
            made = product(table, source(span)).astype(jnp.bfloat16)
            for part in range(parts):
                out_refs[part][:, span] = made[part * rows : (part + 1) * rows]

    if has_first:

        @pl.when(sec == 0)
        def _():
            put(place_ref[slot], lambda span: tokens_ref[:, span])

    if has_rest:

        @pl.when((sec > 0) & (micro >= 0) & (micro < micro_count))
        def _():
            put(
                move_ref[micro],
                lambda span: jnp.concatenate([ref[:, span] for ref in arrived], axis=0),
            )


def backward_router(slot, counts, parts, has_former, onward, *refs):
    section_count, micro_count = counts
    sec_ref, take_ref, move_ref = refs[:3]
    arrived = refs[3 : 3 + parts]
    rest = refs[3 + parts + (1 if has_former else 0) :]
    result = rest[0]
    out_refs = rest[1 : 1 + parts] if onward else []
    ordered, sem = rest[1 + len(out_refs) :]
    sec = sec_ref[0]
    micro = slot - 2 * (section_count - 1) + sec
    width = arrived[0].shape[1]
    rows = arrived[0].shape[0]

    @pl.when((micro >= 0) & (micro < micro_count))
    def _():
        def source(span):
            return jnp.concatenate([ref[:, span] for ref in arrived], axis=0)

        if onward:

            @pl.when(sec > 0)
            def _():
                for span in spans(width, 512):
                    made = product(move_ref[micro], source(span)).astype(jnp.bfloat16)
                    for part in range(parts):
                        out_refs[part][:, span] = made[part * rows : (part + 1) * rows]

        for span in spans(width, 512):
            ordered[:, span] = product(take_ref[micro], source(span)).astype(jnp.bfloat16)
        copy = pltpu.make_async_copy(ordered, result.at[micro], sem)
        copy.start()
        copy.wait()


def slots_of(route_ids, expert_count, capacity, turn):
    one_hot = (route_ids[:, :, None] == jnp.arange(expert_count, dtype=jnp.int32)).astype(jnp.int32)
    position = jnp.sum((jnp.cumsum(one_hot, axis=1, dtype=jnp.int32) - 1) * one_hot, axis=-1)
    return lax.rem(route_ids - turn + expert_count, expert_count) * capacity + position


def body(tokens_in, cotangent, norm_gain, w_gate, w_up, w_down, expert_ids, gate_weights):
    section_count = lax.axis_size("section")
    device_count = lax.axis_size("expert")
    section = lax.axis_index("section")
    place = lax.axis_index("expert") // 2
    expert_count = device_count // 2
    micro_count = expert_ids.shape[1]
    tok_rows = expert_ids.shape[2]
    model_dim = tokens_in.shape[2]
    hidden_dim = w_gate.shape[3]
    capacity = 2 * ((tok_rows + expert_count - 1) // expert_count)
    slots = expert_count * capacity
    by_permute = capacity % 16 == 0
    parts = expert_count if by_permute else 1
    rows = slots // parts
    turn = place if by_permute else jnp.int32(0)
    counts = (section_count, micro_count)
    first_back = section_count - 1
    slot_count = micro_count + 2 * (section_count - 1)
    sections = range(section_count)

    def exchange(chunks, jobs, direction):
        if by_permute:
            moved = [None] * parts
            for step in sorted(range(parts), key=lambda k: -min(k, parts - k)):
                if step == 0 and all(a == b for a, b in jobs):
                    moved[0] = chunks[0]
                    continue
                pairs = [
                    (
                        a * device_count + 2 * z + core,
                        b * device_count + 2 * ((z + direction * step) % expert_count) + core,
                    )
                    for a, b in jobs
                    for z in range(expert_count)
                    for core in range(2)
                ]
                moved[step] = lax.ppermute(chunks[step], both, pairs)
            return moved
        (block,) = chunks
        shape = block.shape
        spread = block.reshape(-1, expert_count, capacity, shape[-1])
        groups = [[2 * z + core for z in range(expert_count)] for core in range(2)]
        spread = lax.all_to_all(
            spread, "expert", split_axis=1, concat_axis=1, tiled=True, axis_index_groups=groups
        )
        block = spread.reshape(shape)
        if any(a != b for a, b in jobs):
            block = lax.ppermute(block, "section", jobs)
        return [block]

    def cut(block):
        return [block[:, part * rows : (part + 1) * rows] for part in range(parts)]

    own = (w_gate[0, 0], w_up[0, 0], w_down[0, 0])
    swap = [(i, i ^ 1) for i in range(device_count)]
    other = tuple(lax.ppermute(matrix, "expert", swap) for matrix in own)
    weights = (*own, *other)

    sec = section.reshape(1).astype(jnp.int32)
    gain = norm_gain
    ids = expert_ids[0, :, :, 0]
    former_ids = lax.ppermute(ids, "section", [(s, s + 1) for s in sections[:-1]])
    slot_own = slots_of(ids, expert_count, capacity, turn)
    slot_former = slots_of(former_ids, expert_count, capacity, turn)
    numbers = jnp.arange(slots, dtype=jnp.int32)
    is_own = numbers[None, :, None] == slot_own[:, None, :]
    place_own = is_own.astype(jnp.bfloat16)
    place_former = (numbers[None, :, None] == slot_former[:, None, :]).astype(jnp.bfloat16)
    take_own = place_own.transpose(0, 2, 1)
    move_forward = jnp.einsum("mjt,mit->mji", place_own, place_former)
    move_back = jnp.einsum("mjt,mit->mji", place_former, place_own)
    route_slots = jnp.sum(jnp.where(is_own, gate_weights[0, :, None, :, 0], 0.0), axis=-1)
    route_parts = exchange(cut(route_slots[:, :, None]), [(s, s) for s in sections], 1)
    route = jnp.concatenate(route_parts, axis=1)

    tokens_all = [tokens_in[0]]
    cotangent_all = []
    for step in range(1, section_count):
        sent = jnp.where(section == step, tokens_in[0], cotangent[0])
        came = lax.ppermute(sent, "section", [(step, 0), (step - 1, section_count - 1)])
        tokens_all.append(came)
        cotangent_all.append(came)
    cotangent_all.append(cotangent[0])
    packed = jnp.einsum(
        "mjt,mtd->mjd", place_own, jnp.stack(cotangent_all), preferred_element_type=jnp.float32
    ).astype(jnp.bfloat16)
    first_grads = exchange(cut(packed), [(first_back, first_back)], 1)

    chunk = jax.ShapeDtypeStruct((rows, model_dim), jnp.bfloat16)
    weight_scratch = [
        pltpu.VMEM((2, model_dim, hidden_dim), jnp.bfloat16),
        pltpu.VMEM((2, model_dim, hidden_dim), jnp.bfloat16),
        pltpu.VMEM((2, hidden_dim, model_dim), jnp.bfloat16),
    ]
    weight_bytes = 6 * model_dim * hidden_dim * 2
    flops = 2 * slots * 6 * model_dim * hidden_dim
    heavy = pl.CostEstimate(flops=flops, bytes_accessed=weight_bytes, transcendentals=0)
    state_shapes = [
        jax.ShapeDtypeStruct((slots, model_dim), jnp.bfloat16),
        jax.ShapeDtypeStruct((slots, 2 * hidden_dim), jnp.float32),
        jax.ShapeDtypeStruct((slots, 2 * hidden_dim), jnp.float32),
        jax.ShapeDtypeStruct((slots, model_dim), jnp.float32),
    ]

    saved = {}
    ahead = None
    behind = None
    gate_slots = []
    result = None
    for slot in range(slot_count):
        forward_on = [s for s in sections if 0 <= slot - s < micro_count]
        if forward_on:
            has_first = 0 in forward_on
            has_rest = ahead is not None
            packed = pl.pallas_call(
                partial(forward_router, slot, micro_count, parts, has_first, has_rest),
                out_shape=[chunk] * parts,
                in_specs=[in_smem, in_vmem, in_vmem]
                + [in_vmem] * ((1 if has_first else 0) + (parts if has_rest else 0)),
                out_specs=[in_vmem] * parts,
                compiler_params=params(16),
                name=f"route_forward_{slot}",
            )(
                sec,
                place_own,
                move_forward,
                *([tokens_all[slot]] if has_first else []),
                *(ahead if has_rest else []),
            )
            moved = exchange(packed, [(s, s) for s in forward_on], 1)
            outs = pl.pallas_call(
                partial(forward_kernel, slot, micro_count, parts),
                out_shape=[chunk] * parts + state_shapes,
                in_specs=[in_smem, in_vmem, in_vmem] + [in_vmem] * parts + [anywhere] * 6,
                out_specs=[in_vmem] * (parts + 4),
                scratch_shapes=weight_scratch
                + [
                    pltpu.VMEM((slots, model_dim), jnp.bfloat16),
                    pltpu.VMEM((2, slots, hidden_dim), jnp.bfloat16),
                    pltpu.SemaphoreType.DMA((3, 2)),
                ],
                compiler_params=params(40),
                cost_estimate=heavy,
                name=f"expert_forward_{slot}",
            )(sec, gain, route, *moved, *weights)
            x_rows, pre_gate, pre_up, made = outs[parts:]
            saved[slot] = (made, x_rows, pre_gate, pre_up)
            jobs = [(s, s + 1) for s in forward_on if s + 1 < section_count]
            ahead = exchange(outs[:parts], jobs, -1) if jobs else None
        backward_on = [s for s in sections if 0 <= slot - 2 * first_back + s < micro_count]
        if backward_on:
            jobs = [(s + 1, s) for s in backward_on if s < first_back]
            grads = exchange(behind, jobs, 1) if jobs else [part[0] for part in first_grads]
            states = []
            for s in backward_on:
                states += list(saved[slot - 2 * first_back + 2 * s])
            outs = pl.pallas_call(
                partial(backward_kernel, slot, counts, backward_on, parts),
                out_shape=[chunk] * parts + [jax.ShapeDtypeStruct((slots, 128), jnp.float32)],
                in_specs=[in_smem, in_vmem, in_vmem]
                + [anywhere] * (2 * parts + 6 + len(states)),
                out_specs=[in_vmem] * (parts + 1),
                scratch_shapes=weight_scratch
                + [
                    pltpu.VMEM((slots, model_dim), jnp.bfloat16),
                    pltpu.VMEM((slots, model_dim), jnp.bfloat16),
                    pltpu.VMEM((slots, 2 * hidden_dim), jnp.float32),
                    pltpu.VMEM((slots, 2 * hidden_dim), jnp.float32),
                    pltpu.VMEM((slots, model_dim), jnp.float32),
                    pltpu.VMEM((slots, model_dim), jnp.bfloat16),
                    pltpu.VMEM((slots, model_dim), jnp.float32),
                    pltpu.SemaphoreType.DMA((3, 2)),
                    pltpu.SemaphoreType.DMA((4,)),
                    pltpu.SemaphoreType.DMA((parts,)),
                ],
                compiler_params=params(40),
                cost_estimate=heavy,
                name=f"expert_backward_{slot}",
            )(sec, gain, route, *grads, *first_grads, *weights, *states)
            gate_slots.append(outs[parts][:, 0])
            home = exchange(outs[:parts], [(s, s) for s in backward_on], -1)
            onward = slot + 1 < slot_count
            has_former = result is not None
            outs = pl.pallas_call(
                partial(backward_router, slot, counts, parts, has_former, onward),
                out_shape=[jax.ShapeDtypeStruct((micro_count, tok_rows, model_dim), jnp.bfloat16)]
                + [chunk] * (parts if onward else 0),
                in_specs=[in_smem, in_vmem, in_vmem]
                + [in_vmem] * parts
                + [anywhere] * (1 if has_former else 0),
                out_specs=[anywhere] + [in_vmem] * (parts if onward else 0),
                scratch_shapes=[
                    pltpu.VMEM((tok_rows, model_dim), jnp.bfloat16),
                    pltpu.SemaphoreType.DMA,
                ],
                input_output_aliases={3 + parts: 0} if has_former else {},
                compiler_params=params(16),
                name=f"route_backward_{slot}",
            )(sec, take_own, move_back, *home, *([result] if has_former else []))
            result = outs[0]
            behind = outs[1:]

    gates = lax.dynamic_slice_in_dim(jnp.stack(gate_slots), first_back - section, micro_count, 0)
    gate_parts = exchange(cut(gates[:, :, None]), [(s, s) for s in sections], -1)
    gates = jnp.concatenate(gate_parts, axis=1)
    gate_out = jnp.sum(jnp.where(is_own, gates, 0.0), axis=1)
    return (result[None], gate_out[None, :, :, None])


def solution(mesh):
    return jax.shard_map(
        body,
        mesh=mesh,
        in_specs=(
            P("section", "expert", None),
            P("section", "expert", None),
            P("section", None),
            P("section", "expert", None, None),
            P("section", "expert", None, None),
            P("section", "expert", None, None),
            P("section", None, "expert", None),
            P("section", None, "expert", None),
        ),
        out_specs=(P("section", None, "expert", None), P("section", None, "expert", None)),
        check_vma=False,
    )
```

```python
from functools import partial

import jax
import jax.numpy as jnp
from jax import lax
from jax.experimental import pallas as pl
from jax.experimental.pallas import tpu as pltpu
from jax.sharding import PartitionSpec as P

epsilon = 1e-06
both = ("section", "expert")
last_with_last = (((1,), (1,)), ((), ()))

in_vmem = pl.BlockSpec(memory_space=pltpu.VMEM)
in_smem = pl.BlockSpec(memory_space=pltpu.SMEM)
in_hbm = pl.BlockSpec(memory_space=pltpu.HBM)
lanes = 128


def spans(total, size):
    size = size if total % size == 0 else total
    return [pl.ds(start, size) for start in range(0, total, size)]


def params(mib):
    return pltpu.CompilerParams(vmem_limit_bytes=mib * 2**20)


def product(left, right):
    return jnp.dot(left, right, preferred_element_type=jnp.float32)


def product_t(left, right):
    return lax.dot_general(left, right, last_with_last, preferred_element_type=jnp.float32)


def coded(column):
    high = column.astype(jnp.bfloat16).astype(jnp.float32)
    left = column - high
    middle = left.astype(jnp.bfloat16).astype(jnp.float32)
    lane = lax.broadcasted_iota(jnp.int32, (column.shape[0], lanes), 1)
    spread = jnp.where(lane == 1, middle, jnp.where(lane == 2, left - middle, 0.0))
    return jnp.where(lane == 0, high, spread).astype(jnp.bfloat16)


def decoded(columns):
    return jnp.sum(columns.astype(jnp.float32), axis=-1, keepdims=True)


def weight_copies(half_refs, buffers, sems):
    return [
        [
            pltpu.make_async_copy(half_refs[half][which], buffers[which].at[half], sems.at[which, half])
            for half in range(2)
        ]
        for which in range(3)
    ]


def forward_kernel(slot, micro_count, parts, *refs):
    sec_ref, gain_ref = refs[:2]
    x_refs = refs[2 : 2 + parts]
    rest = refs[2 + parts :]
    half_refs = [rest[0:3], rest[3:6]]
    out_refs = rest[6 : 6 + parts]
    save_x, save_gate, save_up, save_rows = rest[6 + parts : 10 + parts]
    gate_buf, up_buf, down_buf, normed, hidden, sems = rest[10 + parts :]
    micro = slot - sec_ref[0]
    width = gain_ref.shape[1]
    hidden_dim = gate_buf.shape[2]
    rows = x_refs[0].shape[0]

    @pl.when((micro >= 0) & (micro < micro_count))
    def _():
        copies = weight_copies(half_refs, (gate_buf, up_buf, down_buf), sems)
        for half in range(2):
            copies[0][half].start()
            copies[1][half].start()
        for half in range(2):
            copies[2][half].start()
        for part in range(parts):
            values = x_refs[part][:, :width].astype(jnp.float32)
            inv_rms = lax.rsqrt(jnp.mean(values * values, axis=-1, keepdims=True) + epsilon)
            here = pl.ds(part * rows, rows)
            normed[here, :] = (values * inv_rms * gain_ref[...]).astype(jnp.bfloat16)
            save_x[here, :] = x_refs[part][...]
        for half in range(2):
            side = pl.ds(half * hidden_dim, hidden_dim)
            copies[0][half].wait()
            gate_pre = product(normed[...], gate_buf[half])
            copies[1][half].wait()
            up_pre = product(normed[...], up_buf[half])
            save_gate[:, side] = gate_pre
            save_up[:, side] = up_pre
            hidden[half] = (gate_pre * jax.nn.sigmoid(gate_pre) * up_pre).astype(jnp.bfloat16)
        copies[2][0].wait()
        copies[2][1].wait()
        route = [decoded(x_refs[part][:, width:]) for part in range(parts)]
        for span in spans(width, 256):
            made = product(hidden[0], down_buf[0, :, span])
            made = made + product(hidden[1], down_buf[1, :, span])
            save_rows[:, span] = made
            for part in range(parts):
                added = route[part] * made[part * rows : (part + 1) * rows]
                values = x_refs[part][:, span].astype(jnp.float32)
                out_refs[part][:, span] = (values + added).astype(jnp.bfloat16)


def backward_kernel(slot, counts, candidates, parts, *refs):
    section_count, micro_count = counts
    sec_ref, gain_ref = refs[:2]
    rest = refs[2:]
    arrived = rest[:parts]
    first = rest[parts : 2 * parts]
    rest = rest[2 * parts :]
    half_refs = [rest[0:3], rest[3:6]]
    rest = rest[6:]
    saved = {}
    for section in candidates:
        saved[section] = rest[:4]
        rest = rest[4:]
    out_refs = rest[:parts]
    (gate_buf, up_buf, down_buf, grad_buf, x_buf, pre_gate, pre_up, rows_buf, grad_rows, scaled_buf,
     sems, state_sems, grad_sems) = rest[parts:]
    sec = sec_ref[0]
    micro = slot - 2 * (section_count - 1) + sec
    width = gain_ref.shape[1]
    hidden_dim = gate_buf.shape[2]
    slots = grad_buf.shape[0]
    rows = slots // parts

    @pl.when((micro >= 0) & (micro < micro_count))
    def _():
        def for_section(section, act):
            @pl.when(sec == section)
            def _():
                for part in range(parts):
                    if section == section_count - 1:
                        source = first[part].at[slot - (section_count - 1)]
                    else:
                        source = arrived[part]
                    act(pltpu.make_async_copy(
                        source, grad_buf.at[pl.ds(part * rows, rows), :], grad_sems.at[part]
                    ))
                targets = (rows_buf, x_buf, pre_gate, pre_up)
                for number, target in enumerate(targets):
                    act(pltpu.make_async_copy(
                        saved[section][number], target, state_sems.at[number]
                    ))

        for section in candidates:
            for_section(section, lambda copy: copy.start())
        copies = weight_copies(half_refs, (gate_buf, up_buf, down_buf), sems)
        for half in range(2):
            copies[2][half].start()
        for half in range(2):
            copies[0][half].start()
            copies[1][half].start()
        for section in candidates:
            for_section(section, lambda copy: copy.wait())
        route = decoded(x_buf[:, width:])
        gate_grad = jnp.zeros((slots, 1), jnp.float32)
        square = jnp.zeros((slots, 1), jnp.float32)
        for span in spans(width, 512):
            grad_f = grad_buf[:, span].astype(jnp.float32)
            gate_grad += jnp.sum(grad_f * rows_buf[:, span], axis=-1, keepdims=True)
            grad_rows[:, span] = (route * grad_f).astype(jnp.bfloat16)
            values = x_buf[:, span].astype(jnp.float32)
            square += jnp.sum(values * values, axis=-1, keepdims=True)
        gate_columns = coded(gate_grad)
        for part in range(parts):
            out_refs[part][:, width:] = gate_columns[part * rows : (part + 1) * rows]
        inv_rms = lax.rsqrt(square / width + epsilon)
        grads = []
        for half in range(2):
            side = pl.ds(half * hidden_dim, hidden_dim)
            copies[2][half].wait()
            grad_hidden = product_t(down_buf[half], grad_rows[...]).T
            gate_pre = pre_gate[:, side]
            sigma = jax.nn.sigmoid(gate_pre)
            grad_gate = grad_hidden * pre_up[:, side] * sigma * (1.0 + gate_pre * (1.0 - sigma))
            grad_up = grad_hidden * gate_pre * sigma
            grads.append((grad_gate.astype(jnp.bfloat16), grad_up.astype(jnp.bfloat16)))
        for half in range(2):
            copies[0][half].wait()
            copies[1][half].wait()
        dotted = jnp.zeros((slots, 1), jnp.float32)
        for span in spans(width, 256):
            total = product_t(gate_buf[0, span, :], grads[0][0])
            total = total + product_t(up_buf[0, span, :], grads[0][1])
            total = total + product_t(gate_buf[1, span, :], grads[1][0])
            total = total + product_t(up_buf[1, span, :], grads[1][1])
            scaled = total.T * gain_ref[:, span]
            scaled_buf[:, span] = scaled
            dotted += jnp.sum(x_buf[:, span].astype(jnp.float32) * scaled, axis=-1, keepdims=True)
        back = inv_rms * inv_rms * inv_rms * (dotted / width)
        for span in spans(width, 512):
            grad_in = (
                grad_buf[:, span].astype(jnp.float32)
                + inv_rms * scaled_buf[:, span]
                - x_buf[:, span].astype(jnp.float32) * back
            ).astype(jnp.bfloat16)
            for part in range(parts):
                out_refs[part][:, span] = grad_in[part * rows : (part + 1) * rows]


def forward_router(slot, micro_count, parts, has_first, has_rest, *refs):
    sec_ref, route_ref, place_ref, move_ref = refs[:4]
    rest = refs[4:]
    tokens_ref = rest[0] if has_first else None
    rest = rest[1:] if has_first else rest
    arrived = rest[:parts] if has_rest else None
    rest = rest[parts:] if has_rest else rest
    out_refs = rest[:parts]
    sec = sec_ref[0]
    micro = slot - sec
    width = out_refs[0].shape[1] - lanes
    rows = out_refs[0].shape[0]

    def put(number, table, source):
        columns = coded(route_ref[number])
        for part in range(parts):
            out_refs[part][:, width:] = columns[part * rows : (part + 1) * rows]
        for span in spans(width, 512):
            made = product(table, source(span)).astype(jnp.bfloat16)
            for part in range(parts):
                out_refs[part][:, span] = made[part * rows : (part + 1) * rows]

    if has_first:

        @pl.when(sec == 0)
        def _():
            put(slot, place_ref[slot], lambda span: tokens_ref[:, span])

    if has_rest:

        @pl.when((sec > 0) & (micro >= 0) & (micro < micro_count))
        def _():
            put(
                micro,
                move_ref[micro],
                lambda span: jnp.concatenate([ref[:, span] for ref in arrived], axis=0),
            )


def backward_router(slot, counts, parts, has_former, onward, *refs):
    section_count, micro_count = counts
    sec_ref, take_ref, move_ref = refs[:3]
    arrived = refs[3 : 3 + parts]
    rest = refs[3 + parts + (2 if has_former else 0) :]
    result, gates = rest[:2]
    out_refs = rest[2 : 2 + parts] if onward else []
    ordered, gate_rows, sems = rest[2 + len(out_refs) :]
    sec = sec_ref[0]
    micro = slot - 2 * (section_count - 1) + sec
    width = arrived[0].shape[1] - lanes
    rows = arrived[0].shape[0]

    @pl.when((micro >= 0) & (micro < micro_count))
    def _():
        def source(span):
            return jnp.concatenate([ref[:, span] for ref in arrived], axis=0)

        if onward:

            @pl.when(sec > 0)
            def _():
                for span in spans(width, 512):
                    made = product(move_ref[micro], source(span)).astype(jnp.bfloat16)
                    for part in range(parts):
                        out_refs[part][:, span] = made[part * rows : (part + 1) * rows]

        for span in spans(width, 512):
            ordered[:, span] = product(take_ref[micro], source(span)).astype(jnp.bfloat16)
        copy = pltpu.make_async_copy(ordered, result.at[micro], sems.at[0])
        copy.start()
        columns = decoded(product(take_ref[micro], source(pl.ds(width, lanes))))
        gate_rows[...] = jnp.broadcast_to(columns, gate_rows.shape)
        gate_copy = pltpu.make_async_copy(gate_rows, gates.at[micro], sems.at[1])
        gate_copy.start()
        copy.wait()
        gate_copy.wait()


def slots_of(route_ids, expert_count, capacity, turn):
    one_hot = (route_ids[:, :, None] == jnp.arange(expert_count, dtype=jnp.int32)).astype(jnp.int32)
    position = jnp.sum((jnp.cumsum(one_hot, axis=1, dtype=jnp.int32) - 1) * one_hot, axis=-1)
    return lax.rem(route_ids - turn + expert_count, expert_count) * capacity + position


def body(tokens_in, cotangent, norm_gain, w_gate, w_up, w_down, expert_ids, gate_weights):
    section_count = lax.axis_size("section")
    device_count = lax.axis_size("expert")
    section = lax.axis_index("section")
    place = lax.axis_index("expert") // 2
    expert_count = device_count // 2
    micro_count = expert_ids.shape[1]
    tok_rows = expert_ids.shape[2]
    model_dim = tokens_in.shape[2]
    hidden_dim = w_gate.shape[3]
    capacity = 2 * ((tok_rows + expert_count - 1) // expert_count)
    slots = expert_count * capacity
    by_permute = capacity % 16 == 0
    parts = expert_count if by_permute else 1
    rows = slots // parts
    turn = place if by_permute else jnp.int32(0)
    counts = (section_count, micro_count)
    first_back = section_count - 1
    slot_count = micro_count + 2 * (section_count - 1)
    sections = range(section_count)

    def exchange(chunks, jobs, direction):
        if by_permute:
            moved = [None] * parts
            for step in sorted(range(parts), key=lambda k: -min(k, parts - k)):
                if step == 0 and all(a == b for a, b in jobs):
                    moved[0] = chunks[0]
                    continue
                pairs = [
                    (
                        a * device_count + 2 * z + core,
                        b * device_count + 2 * ((z + direction * step) % expert_count) + core,
                    )
                    for a, b in jobs
                    for z in range(expert_count)
                    for core in range(2)
                ]
                moved[step] = lax.ppermute(chunks[step], both, pairs)
            return moved
        (block,) = chunks
        shape = block.shape
        spread = block.reshape(-1, expert_count, capacity, shape[-1])
        groups = [[2 * z + core for z in range(expert_count)] for core in range(2)]
        spread = lax.all_to_all(
            spread, "expert", split_axis=1, concat_axis=1, tiled=True, axis_index_groups=groups
        )
        block = spread.reshape(shape)
        if any(a != b for a, b in jobs):
            block = lax.ppermute(block, "section", jobs)
        return [block]

    def cut(block):
        return [block[:, part * rows : (part + 1) * rows] for part in range(parts)]

    own = (w_gate[0, 0], w_up[0, 0], w_down[0, 0])
    swap = [(i, i ^ 1) for i in range(device_count)]
    other = tuple(lax.ppermute(matrix, "expert", swap) for matrix in own)
    weights = (*own, *other)

    sec = section.reshape(1).astype(jnp.int32)
    gain = norm_gain
    ids = expert_ids[0, :, :, 0]
    onto_next = [(s, s + 1) for s in sections[:-1]]
    onto_former = [(s + 1, s) for s in sections[:-1]]
    within = [(s, s) for s in sections]
    former_ids = lax.ppermute(
        ids, both, [(a * device_count + i, b * device_count + i) for a, b in onto_next for i in range(device_count)]
    )
    slot_own = slots_of(ids, expert_count, capacity, turn)
    slot_former = slots_of(former_ids, expert_count, capacity, turn)
    numbers = jnp.arange(slots, dtype=jnp.int32)
    is_own = numbers[None, :, None] == slot_own[:, None, :]
    place_own = is_own.astype(jnp.bfloat16)
    place_former = (numbers[None, :, None] == slot_former[:, None, :]).astype(jnp.bfloat16)
    take_own = place_own.transpose(0, 2, 1)
    move_forward = jnp.einsum("mjt,mit->mji", place_own, place_former)
    move_back = jnp.einsum("mjt,mit->mji", place_former, place_own)
    route_slots = jnp.sum(jnp.where(is_own, gate_weights[0, :, None, :, 0], 0.0), axis=-1)
    route = route_slots[:, :, None]

    tokens_all = [tokens_in[0]]
    cotangent_all = []
    for step in range(1, section_count):
        sent = jnp.where(section == step, tokens_in[0], cotangent[0])
        came = lax.ppermute(sent, "section", [(step, 0), (step - 1, section_count - 1)])
        tokens_all.append(came)
        cotangent_all.append(came)
    cotangent_all.append(cotangent[0])
    packed = jnp.einsum(
        "mjt,mtd->mjd", place_own, jnp.stack(cotangent_all), preferred_element_type=jnp.float32
    ).astype(jnp.bfloat16)
    first_grads = exchange(cut(packed), [(first_back, first_back)], 1)

    chunk = jax.ShapeDtypeStruct((rows, model_dim), jnp.bfloat16)
    wide = jax.ShapeDtypeStruct((rows, model_dim + lanes), jnp.bfloat16)
    weight_scratch = [
        pltpu.VMEM((2, model_dim, hidden_dim), jnp.bfloat16),
        pltpu.VMEM((2, model_dim, hidden_dim), jnp.bfloat16),
        pltpu.VMEM((2, hidden_dim, model_dim), jnp.bfloat16),
    ]
    weight_bytes = 6 * model_dim * hidden_dim * 2
    flops = 2 * slots * 6 * model_dim * hidden_dim
    heavy = pl.CostEstimate(flops=flops, bytes_accessed=weight_bytes, transcendentals=0)
    state_shapes = [
        jax.ShapeDtypeStruct((slots, model_dim + lanes), jnp.bfloat16),
        jax.ShapeDtypeStruct((slots, 2 * hidden_dim), jnp.float32),
        jax.ShapeDtypeStruct((slots, 2 * hidden_dim), jnp.float32),
        jax.ShapeDtypeStruct((slots, model_dim), jnp.float32),
    ]

    saved = {}
    ahead = None
    behind = None
    results = None
    for slot in range(slot_count):
        forward_on = [s for s in sections if 0 <= slot - s < micro_count]
        if forward_on:
            has_first = 0 in forward_on
            has_rest = ahead is not None
            packed = pl.pallas_call(
                partial(forward_router, slot, micro_count, parts, has_first, has_rest),
                out_shape=[wide] * parts,
                in_specs=[in_smem, in_vmem, in_vmem, in_vmem]
                + [in_vmem] * ((1 if has_first else 0) + (parts if has_rest else 0)),
                out_specs=[in_vmem] * parts,
                compiler_params=params(16),
                name=f"route_forward_{slot}",
            )(
                sec,
                route,
                place_own,
                move_forward,
                *([tokens_all[slot]] if has_first else []),
                *(ahead if has_rest else []),
            )
            moved = exchange(packed, within, 1)
            outs = pl.pallas_call(
                partial(forward_kernel, slot, micro_count, parts),
                out_shape=[chunk] * parts + state_shapes,
                in_specs=[in_smem, in_vmem] + [in_vmem] * parts + [in_hbm] * 6,
                out_specs=[in_vmem] * (parts + 4),
                scratch_shapes=weight_scratch
                + [
                    pltpu.VMEM((slots, model_dim), jnp.bfloat16),
                    pltpu.VMEM((2, slots, hidden_dim), jnp.bfloat16),
                    pltpu.SemaphoreType.DMA((3, 2)),
                ],
                compiler_params=params(40),
                cost_estimate=heavy,
                name=f"expert_forward_{slot}",
            )(sec, gain, *moved, *weights)
            x_rows, pre_gate, pre_up, made = outs[parts:]
            saved[slot] = (made, x_rows, pre_gate, pre_up)
            more = any(s + 1 < section_count for s in forward_on)
            ahead = exchange(outs[:parts], onto_next, -1) if more else None
        backward_on = [s for s in sections if 0 <= slot - 2 * first_back + s < micro_count]
        if backward_on:
            if behind is None:
                grads = [part[0] for part in first_grads]
            else:
                grads = exchange(behind, onto_former, 1)
            states = []
            for s in backward_on:
                states += list(saved[slot - 2 * first_back + 2 * s])
            outs = pl.pallas_call(
                partial(backward_kernel, slot, counts, backward_on, parts),
                out_shape=[wide] * parts,
                in_specs=[in_smem, in_vmem] + [pl.BlockSpec(memory_space=pl.ANY)] * (2 * parts)
                + [in_hbm] * (6 + len(states)),
                out_specs=[in_vmem] * parts,
                scratch_shapes=weight_scratch
                + [
                    pltpu.VMEM((slots, model_dim), jnp.bfloat16),
                    pltpu.VMEM((slots, model_dim + lanes), jnp.bfloat16),
                    pltpu.VMEM((slots, 2 * hidden_dim), jnp.float32),
                    pltpu.VMEM((slots, 2 * hidden_dim), jnp.float32),
                    pltpu.VMEM((slots, model_dim), jnp.float32),
                    pltpu.VMEM((slots, model_dim), jnp.bfloat16),
                    pltpu.VMEM((slots, model_dim), jnp.float32),
                    pltpu.SemaphoreType.DMA((3, 2)),
                    pltpu.SemaphoreType.DMA((4,)),
                    pltpu.SemaphoreType.DMA((parts,)),
                ],
                compiler_params=params(40),
                cost_estimate=heavy,
                name=f"expert_backward_{slot}",
            )(sec, gain, *grads, *first_grads, *weights, *states)
            home = exchange(outs, within, -1)
            onward = slot + 1 < slot_count
            has_former = results is not None
            outs = pl.pallas_call(
                partial(backward_router, slot, counts, parts, has_former, onward),
                out_shape=[
                    jax.ShapeDtypeStruct((micro_count, tok_rows, model_dim), jnp.bfloat16),
                    jax.ShapeDtypeStruct((micro_count, tok_rows, lanes), jnp.float32),
                ]
                + [chunk] * (parts if onward else 0),
                in_specs=[in_smem, in_vmem, in_vmem]
                + [in_vmem] * parts
                + [in_hbm] * (2 if has_former else 0),
                out_specs=[in_hbm] * 2 + [in_vmem] * (parts if onward else 0),
                scratch_shapes=[
                    pltpu.VMEM((tok_rows, model_dim), jnp.bfloat16),
                    pltpu.VMEM((tok_rows, lanes), jnp.float32),
                    pltpu.SemaphoreType.DMA((2,)),
                ],
                input_output_aliases={3 + parts: 0, 4 + parts: 1} if has_former else {},
                compiler_params=params(16),
                name=f"route_backward_{slot}",
            )(sec, take_own, move_back, *home, *(results if has_former else []))
            results = outs[:2]
            behind = outs[2:]

    return (results[0][None], results[1][None, :, :, :1])


def solution(mesh):
    return jax.shard_map(
        body,
        mesh=mesh,
        in_specs=(
            P("section", "expert", None),
            P("section", "expert", None),
            P("section", None),
            P("section", "expert", None, None),
            P("section", "expert", None, None),
            P("section", "expert", None, None),
            P("section", None, "expert", None),
            P("section", None, "expert", None),
        ),
        out_specs=(P("section", None, "expert", None), P("section", None, "expert", None)),
        check_vma=False,
    )
```

```python
from functools import partial

import jax
import jax.numpy as jnp
from jax import lax
from jax.experimental import pallas as pl
from jax.experimental.pallas import tpu as pltpu
from jax.sharding import PartitionSpec as P

epsilon = 1e-06
both = ("section", "expert")
last_with_last = (((1,), (1,)), ((), ()))

in_vmem = pl.BlockSpec(memory_space=pltpu.VMEM)
in_smem = pl.BlockSpec(memory_space=pltpu.SMEM)
in_hbm = pl.BlockSpec(memory_space=pltpu.HBM)
lanes = 128


def spans(total, size):
    size = size if total % size == 0 else total
    return [pl.ds(start, size) for start in range(0, total, size)]


def params(mib):
    return pltpu.CompilerParams(vmem_limit_bytes=mib * 2**20)


def product(left, right):
    return jnp.dot(left, right, preferred_element_type=jnp.float32)


def product_t(left, right):
    return lax.dot_general(left, right, last_with_last, preferred_element_type=jnp.float32)


def coded(column):
    high = column.astype(jnp.bfloat16).astype(jnp.float32)
    left = column - high
    middle = left.astype(jnp.bfloat16).astype(jnp.float32)
    lane = lax.broadcasted_iota(jnp.int32, (column.shape[0], lanes), 1)
    spread = jnp.where(lane == 1, middle, jnp.where(lane == 2, left - middle, 0.0))
    return jnp.where(lane == 0, high, spread).astype(jnp.bfloat16)


def decoded(columns):
    return jnp.sum(columns.astype(jnp.float32), axis=-1, keepdims=True)


def forward_kernel(slot, micro_count, parts, loading, *refs):
    sec_ref, gain_ref = refs[:2]
    x_refs = refs[2 : 2 + parts]
    given = refs[2 + parts : 8 + parts]
    rest = refs[8 + parts :]
    out_refs = rest[:parts]
    save_x, save_gate, save_up, save_rows, mark_ref = rest[parts : 5 + parts]
    rest = rest[5 + parts :]
    matrices = rest[:6] if loading else given
    normed, hidden = rest[6:8] if loading else rest
    copies = []
    if loading:
        sems = rest[8]
        copies = [
            pltpu.make_async_copy(given[number], matrices[number], sems.at[number])
            for number in range(6)
        ]
        for number in (0, 1, 3, 4, 2, 5):
            copies[number].start()
    half_refs = [matrices[0:3], matrices[3:6]]
    mark_ref[0] = sec_ref[0]
    micro = slot - sec_ref[0]
    active = (micro >= 0) & (micro < micro_count)
    width = gain_ref.shape[1]
    hidden_dim = half_refs[0][0].shape[1]
    rows = x_refs[0].shape[0]

    @pl.when(active)
    def _():
        for part in range(parts):
            values = x_refs[part][:, :width].astype(jnp.float32)
            inv_rms = lax.rsqrt(jnp.mean(values * values, axis=-1, keepdims=True) + epsilon)
            here = pl.ds(part * rows, rows)
            normed[here, :] = (values * inv_rms * gain_ref[...]).astype(jnp.bfloat16)
            save_x[here, :] = x_refs[part][...]

    for half in range(2):
        if loading:
            copies[3 * half].wait()
            copies[3 * half + 1].wait()

        @pl.when(active)
        def _():
            side = pl.ds(half * hidden_dim, hidden_dim)
            gate_pre = product(normed[...], half_refs[half][0][...])
            up_pre = product(normed[...], half_refs[half][1][...])
            save_gate[:, side] = gate_pre
            save_up[:, side] = up_pre
            hidden[half] = (gate_pre * jax.nn.sigmoid(gate_pre) * up_pre).astype(jnp.bfloat16)

    if loading:
        copies[2].wait()
        copies[5].wait()

    @pl.when(active)
    def _():
        route = [decoded(x_refs[part][:, width:]) for part in range(parts)]
        for span in spans(width, 256):
            made = product(hidden[0], half_refs[0][2][:, span])
            made = made + product(hidden[1], half_refs[1][2][:, span])
            save_rows[:, span] = made
            for part in range(parts):
                added = route[part] * made[part * rows : (part + 1) * rows]
                values = x_refs[part][:, span].astype(jnp.float32)
                out_refs[part][:, span] = (values + added).astype(jnp.bfloat16)


def backward_kernel(slot, counts, candidates, parts, *refs):
    section_count, micro_count = counts
    sec_ref, gain_ref = refs[:2]
    rest = refs[2:]
    arrived = rest[:parts]
    first = rest[parts : 2 * parts]
    rest = rest[2 * parts :]
    half_refs = [rest[0:3], rest[3:6]]
    rest = rest[6:]
    saved = {}
    for section in candidates:
        saved[section] = rest[:4]
        rest = rest[4:]
    out_refs = rest[:parts]
    (grad_buf, x_buf, pre_gate, pre_up, rows_buf, grad_rows, scaled_buf, state_sems, grad_sems) = rest[parts:]
    sec = sec_ref[0]
    micro = slot - 2 * (section_count - 1) + sec
    width = gain_ref.shape[1]
    hidden_dim = half_refs[0][0].shape[1]
    slots = grad_buf.shape[0]
    rows = slots // parts

    @pl.when((micro >= 0) & (micro < micro_count))
    def _():
        def for_section(section, act):
            @pl.when(sec == section)
            def _():
                for part in range(parts):
                    if section == section_count - 1:
                        source = first[part].at[slot - (section_count - 1)]
                    else:
                        source = arrived[part]
                    act(pltpu.make_async_copy(
                        source, grad_buf.at[pl.ds(part * rows, rows), :], grad_sems.at[part]
                    ))
                targets = (rows_buf, x_buf, pre_gate, pre_up)
                for number, target in enumerate(targets):
                    act(pltpu.make_async_copy(
                        saved[section][number], target, state_sems.at[number]
                    ))

        for section in candidates:
            for_section(section, lambda copy: copy.start())
        for section in candidates:
            for_section(section, lambda copy: copy.wait())
        route = decoded(x_buf[:, width:])
        gate_grad = jnp.zeros((slots, 1), jnp.float32)
        square = jnp.zeros((slots, 1), jnp.float32)
        for span in spans(width, 512):
            grad_f = grad_buf[:, span].astype(jnp.float32)
            gate_grad += jnp.sum(grad_f * rows_buf[:, span], axis=-1, keepdims=True)
            grad_rows[:, span] = (route * grad_f).astype(jnp.bfloat16)
            values = x_buf[:, span].astype(jnp.float32)
            square += jnp.sum(values * values, axis=-1, keepdims=True)
        gate_columns = coded(gate_grad)
        for part in range(parts):
            out_refs[part][:, width:] = gate_columns[part * rows : (part + 1) * rows]
        inv_rms = lax.rsqrt(square / width + epsilon)
        grads = []
        for half in range(2):
            side = pl.ds(half * hidden_dim, hidden_dim)
            grad_hidden = product_t(half_refs[half][2][...], grad_rows[...]).T
            gate_pre = pre_gate[:, side]
            sigma = jax.nn.sigmoid(gate_pre)
            grad_gate = grad_hidden * pre_up[:, side] * sigma * (1.0 + gate_pre * (1.0 - sigma))
            grad_up = grad_hidden * gate_pre * sigma
            grads.append((grad_gate.astype(jnp.bfloat16), grad_up.astype(jnp.bfloat16)))
        dotted = jnp.zeros((slots, 1), jnp.float32)
        for span in spans(width, 256):
            total = product_t(half_refs[0][0][span, :], grads[0][0])
            total = total + product_t(half_refs[0][1][span, :], grads[0][1])
            total = total + product_t(half_refs[1][0][span, :], grads[1][0])
            total = total + product_t(half_refs[1][1][span, :], grads[1][1])
            scaled = total.T * gain_ref[:, span]
            scaled_buf[:, span] = scaled
            dotted += jnp.sum(x_buf[:, span].astype(jnp.float32) * scaled, axis=-1, keepdims=True)
        back = inv_rms * inv_rms * inv_rms * (dotted / width)
        for span in spans(width, 512):
            grad_in = (
                grad_buf[:, span].astype(jnp.float32)
                + inv_rms * scaled_buf[:, span]
                - x_buf[:, span].astype(jnp.float32) * back
            ).astype(jnp.bfloat16)
            for part in range(parts):
                out_refs[part][:, span] = grad_in[part * rows : (part + 1) * rows]


def forward_router(slot, micro_count, parts, has_first, has_rest, *refs):
    sec_ref, route_ref, place_ref, move_ref = refs[:4]
    rest = refs[4:]
    tokens_ref = rest[0] if has_first else None
    rest = rest[1:] if has_first else rest
    arrived = rest[:parts] if has_rest else None
    rest = rest[parts:] if has_rest else rest
    out_refs = rest[:parts]
    sec = sec_ref[0]
    micro = slot - sec
    width = out_refs[0].shape[1] - lanes
    rows = out_refs[0].shape[0]

    def put(number, table, source):
        columns = coded(route_ref[number])
        for part in range(parts):
            out_refs[part][:, width:] = columns[part * rows : (part + 1) * rows]
        for span in spans(width, 512):
            made = product(table, source(span)).astype(jnp.bfloat16)
            for part in range(parts):
                out_refs[part][:, span] = made[part * rows : (part + 1) * rows]

    if has_first:

        @pl.when(sec == 0)
        def _():
            put(slot, place_ref[slot], lambda span: tokens_ref[:, span])

    if has_rest:

        @pl.when((sec > 0) & (micro >= 0) & (micro < micro_count))
        def _():
            put(
                micro,
                move_ref[micro],
                lambda span: jnp.concatenate([ref[:, span] for ref in arrived], axis=0),
            )


def backward_router(slot, counts, parts, has_former, onward, *refs):
    section_count, micro_count = counts
    sec_ref, take_ref, move_ref = refs[:3]
    arrived = refs[3 : 3 + parts]
    rest = refs[3 + parts + (2 if has_former else 0) :]
    result, gates = rest[:2]
    out_refs = rest[2 : 2 + parts] if onward else []
    ordered, gate_rows, sems = rest[2 + len(out_refs) :]
    sec = sec_ref[0]
    micro = slot - 2 * (section_count - 1) + sec
    width = arrived[0].shape[1] - lanes
    rows = arrived[0].shape[0]

    @pl.when((micro >= 0) & (micro < micro_count))
    def _():
        def source(span):
            return jnp.concatenate([ref[:, span] for ref in arrived], axis=0)

        if onward:

            @pl.when(sec > 0)
            def _():
                for span in spans(width, 512):
                    made = product(move_ref[micro], source(span)).astype(jnp.bfloat16)
                    for part in range(parts):
                        out_refs[part][:, span] = made[part * rows : (part + 1) * rows]

        for span in spans(width, 512):
            ordered[:, span] = product(take_ref[micro], source(span)).astype(jnp.bfloat16)
        copy = pltpu.make_async_copy(ordered, result.at[micro], sems.at[0])
        copy.start()
        columns = decoded(product(take_ref[micro], source(pl.ds(width, lanes))))
        gate_rows[...] = jnp.broadcast_to(columns, gate_rows.shape)
        gate_copy = pltpu.make_async_copy(gate_rows, gates.at[micro], sems.at[1])
        gate_copy.start()
        copy.wait()
        gate_copy.wait()


def slots_of(route_ids, expert_count, capacity, turn):
    one_hot = (route_ids[:, :, None] == jnp.arange(expert_count, dtype=jnp.int32)).astype(jnp.int32)
    position = jnp.sum((jnp.cumsum(one_hot, axis=1, dtype=jnp.int32) - 1) * one_hot, axis=-1)
    return lax.rem(route_ids - turn + expert_count, expert_count) * capacity + position


def body(tokens_in, cotangent, norm_gain, w_gate, w_up, w_down, expert_ids, gate_weights):
    section_count = lax.axis_size("section")
    device_count = lax.axis_size("expert")
    section = lax.axis_index("section")
    place = lax.axis_index("expert") // 2
    expert_count = device_count // 2
    micro_count = expert_ids.shape[1]
    tok_rows = expert_ids.shape[2]
    model_dim = tokens_in.shape[2]
    hidden_dim = w_gate.shape[3]
    capacity = 2 * ((tok_rows + expert_count - 1) // expert_count)
    slots = expert_count * capacity
    by_permute = capacity % 16 == 0
    parts = expert_count if by_permute else 1
    rows = slots // parts
    turn = place if by_permute else jnp.int32(0)
    counts = (section_count, micro_count)
    first_back = section_count - 1
    slot_count = micro_count + 2 * (section_count - 1)
    sections = range(section_count)

    def exchange(chunks, jobs, direction):
        if by_permute:
            moved = [None] * parts
            for step in sorted(range(parts), key=lambda k: -min(k, parts - k)):
                if step == 0 and all(a == b for a, b in jobs):
                    moved[0] = chunks[0]
                    continue
                pairs = [
                    (
                        a * device_count + 2 * z + core,
                        b * device_count + 2 * ((z + direction * step) % expert_count) + core,
                    )
                    for a, b in jobs
                    for z in range(expert_count)
                    for core in range(2)
                ]
                moved[step] = lax.ppermute(chunks[step], both, pairs)
            return moved
        (block,) = chunks
        shape = block.shape
        spread = block.reshape(-1, expert_count, capacity, shape[-1])
        groups = [[2 * z + core for z in range(expert_count)] for core in range(2)]
        spread = lax.all_to_all(
            spread, "expert", split_axis=1, concat_axis=1, tiled=True, axis_index_groups=groups
        )
        block = spread.reshape(shape)
        if any(a != b for a, b in jobs):
            block = lax.ppermute(block, "section", jobs)
        return [block]

    def cut(block):
        return [block[:, part * rows : (part + 1) * rows] for part in range(parts)]

    own = (w_gate[0, 0], w_up[0, 0], w_down[0, 0])
    swap = [(i, i ^ 1) for i in range(device_count)]
    other = tuple(lax.ppermute(matrix, "expert", swap) for matrix in own)
    weights = (*own, *other)

    sec = section.reshape(1).astype(jnp.int32)
    gain = norm_gain
    ids = expert_ids[0, :, :, 0]
    onto_next = [(s, s + 1) for s in sections[:-1]]
    onto_former = [(s + 1, s) for s in sections[:-1]]
    within = [(s, s) for s in sections]
    former_ids = lax.ppermute(
        ids, both, [(a * device_count + i, b * device_count + i) for a, b in onto_next for i in range(device_count)]
    )
    slot_own = slots_of(ids, expert_count, capacity, turn)
    slot_former = slots_of(former_ids, expert_count, capacity, turn)
    numbers = jnp.arange(slots, dtype=jnp.int32)
    is_own = numbers[None, :, None] == slot_own[:, None, :]
    place_own = is_own.astype(jnp.bfloat16)
    place_former = (numbers[None, :, None] == slot_former[:, None, :]).astype(jnp.bfloat16)
    take_own = place_own.transpose(0, 2, 1)
    move_forward = jnp.einsum("mjt,mit->mji", place_own, place_former)
    move_back = jnp.einsum("mjt,mit->mji", place_former, place_own)
    route_slots = jnp.sum(jnp.where(is_own, gate_weights[0, :, None, :, 0], 0.0), axis=-1)
    route = route_slots[:, :, None]

    def spread_inputs(own_section):
        own_tokens, own_cotangent = tokens_in[0], cotangent[0]
        cotangent_all = []
        for step in range(1, section_count):
            sent = jnp.where(own_section == step, own_tokens, own_cotangent)
            came = lax.ppermute(
                sent, "section", [(step, 0), (step - 1, section_count - 1)]
            )
            tokens_all.append(came)
            cotangent_all.append(came)
        cotangent_all.append(own_cotangent)
        packed = jnp.einsum(
            "mjt,mtd->mjd", place_own, jnp.stack(cotangent_all), preferred_element_type=jnp.float32
        ).astype(jnp.bfloat16)
        return exchange(cut(packed), [(first_back, first_back)], 1)

    tokens_all = [tokens_in[0]]
    first_grads = None

    chunk = jax.ShapeDtypeStruct((rows, model_dim), jnp.bfloat16)
    wide = jax.ShapeDtypeStruct((rows, model_dim + lanes), jnp.bfloat16)
    light = pl.CostEstimate(flops=0, bytes_accessed=0, transcendentals=0)
    state_shapes = [
        jax.ShapeDtypeStruct((slots, model_dim + lanes), jnp.bfloat16),
        jax.ShapeDtypeStruct((slots, 2 * hidden_dim), jnp.float32),
        jax.ShapeDtypeStruct((slots, 2 * hidden_dim), jnp.float32),
        jax.ShapeDtypeStruct((slots, model_dim), jnp.float32),
    ]

    saved = {}
    ahead = None
    behind = None
    results = None
    for slot in range(slot_count):
        forward_on = [s for s in sections if 0 <= slot - s < micro_count]
        if forward_on:
            has_first = 0 in forward_on
            has_rest = ahead is not None
            packed = pl.pallas_call(
                partial(forward_router, slot, micro_count, parts, has_first, has_rest),
                out_shape=[wide] * parts,
                in_specs=[in_smem, in_vmem, in_vmem, in_vmem]
                + [in_vmem] * ((1 if has_first else 0) + (parts if has_rest else 0)),
                out_specs=[in_vmem] * parts,
                compiler_params=params(4),
                cost_estimate=light,
                name=f"route_forward_{slot}",
            )(
                sec,
                route,
                place_own,
                move_forward,
                *([tokens_all[slot]] if has_first else []),
                *(ahead if has_rest else []),
            )
            moved = exchange(packed, within, 1)
            loading = slot == 0
            matrix_shapes = [jax.ShapeDtypeStruct(m.shape, m.dtype) for m in weights]
            outs = pl.pallas_call(
                partial(forward_kernel, slot, micro_count, parts, loading),
                out_shape=[chunk] * parts
                + state_shapes
                + [jax.ShapeDtypeStruct((1,), jnp.int32)]
                + (matrix_shapes if loading else []),
                in_specs=[in_smem, in_vmem]
                + [in_vmem] * parts
                + [in_hbm if loading else in_vmem] * 6,
                out_specs=[in_vmem] * (parts + 4) + [in_smem] + [in_vmem] * (6 if loading else 0),
                scratch_shapes=[
                    pltpu.VMEM((slots, model_dim), jnp.bfloat16),
                    pltpu.VMEM((2, slots, hidden_dim), jnp.bfloat16),
                ]
                + ([pltpu.SemaphoreType.DMA((6,))] if loading else []),
                compiler_params=params(28 if loading else 6),
                cost_estimate=light,
                name=f"expert_forward_{slot}",
            )(sec, gain, *moved, *weights)
            x_rows, pre_gate, pre_up, made = outs[parts : parts + 4]
            saved[slot] = (made, x_rows, pre_gate, pre_up)
            more = any(s + 1 < section_count for s in forward_on)
            jobs = [(a, b) for a, b in onto_next if a <= slot]
            ahead = exchange(outs[:parts], jobs, -1) if more else None
            if loading:
                weights = outs[parts + 5 :]
                first_grads = spread_inputs(outs[parts + 4][0])
        backward_on = [s for s in sections if 0 <= slot - 2 * first_back + s < micro_count]
        if backward_on:
            if behind is None:
                grads = [part[0] for part in first_grads]
            else:
                grads = exchange(behind, onto_former, 1)
            states = []
            for s in backward_on:
                states += list(saved[slot - 2 * first_back + 2 * s])
            outs = pl.pallas_call(
                partial(backward_kernel, slot, counts, backward_on, parts),
                out_shape=[wide] * parts,
                in_specs=[in_smem, in_vmem] + [pl.BlockSpec(memory_space=pl.ANY)] * (2 * parts)
                + [in_vmem] * 6
                + [pl.BlockSpec(memory_space=pl.ANY)] * len(states),
                out_specs=[in_vmem] * parts,
                scratch_shapes=[
                    pltpu.VMEM((slots, model_dim), jnp.bfloat16),
                    pltpu.VMEM((slots, model_dim + lanes), jnp.bfloat16),
                    pltpu.VMEM((slots, 2 * hidden_dim), jnp.float32),
                    pltpu.VMEM((slots, 2 * hidden_dim), jnp.float32),
                    pltpu.VMEM((slots, model_dim), jnp.float32),
                    pltpu.VMEM((slots, model_dim), jnp.bfloat16),
                    pltpu.VMEM((slots, model_dim), jnp.float32),
                    pltpu.SemaphoreType.DMA((4,)),
                    pltpu.SemaphoreType.DMA((parts,)),
                ],
                compiler_params=params(8),
                cost_estimate=light,
                name=f"expert_backward_{slot}",
            )(sec, gain, *grads, *first_grads, *weights, *states)
            home = exchange(outs, within, -1)
            onward = slot + 1 < slot_count
            has_former = results is not None
            outs = pl.pallas_call(
                partial(backward_router, slot, counts, parts, has_former, onward),
                out_shape=[
                    jax.ShapeDtypeStruct((micro_count, tok_rows, model_dim), jnp.bfloat16),
                    jax.ShapeDtypeStruct((micro_count, tok_rows, lanes), jnp.float32),
                ]
                + [chunk] * (parts if onward else 0),
                in_specs=[in_smem, in_vmem, in_vmem]
                + [in_vmem] * parts
                + [in_hbm] * (2 if has_former else 0),
                out_specs=[in_hbm] * 2 + [in_vmem] * (parts if onward else 0),
                scratch_shapes=[
                    pltpu.VMEM((tok_rows, model_dim), jnp.bfloat16),
                    pltpu.VMEM((tok_rows, lanes), jnp.float32),
                    pltpu.SemaphoreType.DMA((2,)),
                ],
                input_output_aliases={3 + parts: 0, 4 + parts: 1} if has_former else {},
                compiler_params=params(4),
                cost_estimate=light,
                name=f"route_backward_{slot}",
            )(sec, take_own, move_back, *home, *(results if has_former else []))
            results = outs[:2]
            behind = outs[2:]

    return (results[0][None], results[1][None, :, :, :1])


def solution(mesh):
    return jax.shard_map(
        body,
        mesh=mesh,
        in_specs=(
            P("section", "expert", None),
            P("section", "expert", None),
            P("section", None),
            P("section", "expert", None, None),
            P("section", "expert", None, None),
            P("section", "expert", None, None),
            P("section", None, "expert", None),
            P("section", None, "expert", None),
        ),
        out_specs=(P("section", None, "expert", None), P("section", None, "expert", None)),
        check_vma=False,
    )
```

```python
from functools import partial

import jax
import jax.numpy as jnp
from jax import lax
from jax.experimental import pallas as pl
from jax.experimental.pallas import tpu as pltpu
from jax.sharding import PartitionSpec as P

epsilon = 1e-06
both = ("section", "expert")
last_with_last = (((1,), (1,)), ((), ()))

in_vmem = pl.BlockSpec(memory_space=pltpu.VMEM)
in_smem = pl.BlockSpec(memory_space=pltpu.SMEM)
in_hbm = pl.BlockSpec(memory_space=pltpu.HBM)
anywhere = pl.BlockSpec(memory_space=pl.ANY)
lanes = 128


def spans(total, size):
    size = size if total % size == 0 else total
    return [pl.ds(start, size) for start in range(0, total, size)]


def params(mib):
    return pltpu.CompilerParams(vmem_limit_bytes=mib * 2**20)


def product(left, right):
    return jnp.dot(left, right, preferred_element_type=jnp.float32)


def product_t(left, right):
    return lax.dot_general(left, right, last_with_last, preferred_element_type=jnp.float32)


def coded(column):
    high = column.astype(jnp.bfloat16).astype(jnp.float32)
    left = column - high
    middle = left.astype(jnp.bfloat16).astype(jnp.float32)
    lane = lax.broadcasted_iota(jnp.int32, (column.shape[0], lanes), 1)
    spread = jnp.where(lane == 1, middle, jnp.where(lane == 2, left - middle, 0.0))
    return jnp.where(lane == 0, high, spread).astype(jnp.bfloat16)


def decoded(columns):
    return jnp.sum(columns.astype(jnp.float32), axis=-1, keepdims=True)


def load_kernel(mark_ref, *refs):
    copies = [
        pltpu.make_async_copy(refs[number], refs[3 + number], refs[6].at[number])
        for number in range(3)
    ]
    for copy in copies:
        copy.start()
    for copy in copies:
        copy.wait()


def forward_kernel(slot, micro_count, parts, loading, *refs):
    sec_ref, gain_ref = refs[:2]
    x_refs = refs[2 : 2 + parts]
    given = refs[2 + parts : 8 + parts]
    rest = refs[8 + parts :]
    out_refs = rest[:parts]
    save_x, save_gate, save_up, save_rows, mark_ref = rest[parts : 5 + parts]
    rest = rest[5 + parts :]
    half_refs = [given[0:3], rest[0:3] if loading else given[3:6]]
    copies = []
    if loading:
        normed, hidden, sems = rest[3:]
        copies = [
            pltpu.make_async_copy(given[3 + number], half_refs[1][number], sems.at[number])
            for number in range(3)
        ]
        for copy in copies:
            copy.start()
    else:
        normed, hidden = rest
    mark_ref[0] = sec_ref[0]
    micro = slot - sec_ref[0]
    active = (micro >= 0) & (micro < micro_count)
    width = gain_ref.shape[1]
    hidden_dim = half_refs[0][0].shape[1]
    rows = x_refs[0].shape[0]

    @pl.when(active)
    def _():
        for part in range(parts):
            values = x_refs[part][:, :width].astype(jnp.float32)
            inv_rms = lax.rsqrt(jnp.mean(values * values, axis=-1, keepdims=True) + epsilon)
            here = pl.ds(part * rows, rows)
            normed[here, :] = (values * inv_rms * gain_ref[...]).astype(jnp.bfloat16)
            save_x[here, :] = x_refs[part][...]

    for half in range(2):
        if loading and half == 1:
            copies[0].wait()
            copies[1].wait()

        @pl.when(active)
        def _():
            side = pl.ds(half * hidden_dim, hidden_dim)
            gate_pre = product(normed[...], half_refs[half][0][...])
            up_pre = product(normed[...], half_refs[half][1][...])
            save_gate[:, side] = gate_pre
            save_up[:, side] = up_pre
            hidden[half] = (gate_pre * jax.nn.sigmoid(gate_pre) * up_pre).astype(jnp.bfloat16)

    if loading:
        copies[2].wait()

    @pl.when(active)
    def _():
        route = [decoded(x_refs[part][:, width:]) for part in range(parts)]
        for span in spans(width, 256):
            made = product(hidden[0], half_refs[0][2][:, span])
            made = made + product(hidden[1], half_refs[1][2][:, span])
            save_rows[:, span] = made
            for part in range(parts):
                added = route[part] * made[part * rows : (part + 1) * rows]
                values = x_refs[part][:, span].astype(jnp.float32)
                out_refs[part][:, span] = (values + added).astype(jnp.bfloat16)


def backward_kernel(slot, counts, candidates, parts, *refs):
    section_count, micro_count = counts
    sec_ref, gain_ref = refs[:2]
    rest = refs[2:]
    arrived = rest[:parts]
    first = rest[parts : 2 * parts]
    rest = rest[2 * parts :]
    half_refs = [rest[0:3], rest[3:6]]
    rest = rest[6:]
    saved = {}
    for section in candidates:
        saved[section] = rest[:4]
        rest = rest[4:]
    out_refs = rest[:parts]
    (grad_buf, x_buf, pre_gate, pre_up, rows_buf, grad_rows, scaled_buf, state_sems, grad_sems) = rest[parts:]
    sec = sec_ref[0]
    micro = slot - 2 * (section_count - 1) + sec
    width = gain_ref.shape[1]
    hidden_dim = half_refs[0][0].shape[1]
    slots = grad_buf.shape[0]
    rows = slots // parts

    @pl.when((micro >= 0) & (micro < micro_count))
    def _():
        def for_section(section, act):
            @pl.when(sec == section)
            def _():
                for part in range(parts):
                    if section == section_count - 1:
                        source = first[part].at[slot - (section_count - 1)]
                    else:
                        source = arrived[part]
                    act(pltpu.make_async_copy(
                        source, grad_buf.at[pl.ds(part * rows, rows), :], grad_sems.at[part]
                    ))
                targets = (rows_buf, x_buf, pre_gate, pre_up)
                for number, target in enumerate(targets):
                    act(pltpu.make_async_copy(
                        saved[section][number], target, state_sems.at[number]
                    ))

        for section in candidates:
            for_section(section, lambda copy: copy.start())
        for section in candidates:
            for_section(section, lambda copy: copy.wait())
        route = decoded(x_buf[:, width:])
        gate_grad = jnp.zeros((slots, 1), jnp.float32)
        square = jnp.zeros((slots, 1), jnp.float32)
        for span in spans(width, 512):
            grad_f = grad_buf[:, span].astype(jnp.float32)
            gate_grad += jnp.sum(grad_f * rows_buf[:, span], axis=-1, keepdims=True)
            grad_rows[:, span] = (route * grad_f).astype(jnp.bfloat16)
            values = x_buf[:, span].astype(jnp.float32)
            square += jnp.sum(values * values, axis=-1, keepdims=True)
        gate_columns = coded(gate_grad)
        for part in range(parts):
            out_refs[part][:, width:] = gate_columns[part * rows : (part + 1) * rows]
        inv_rms = lax.rsqrt(square / width + epsilon)
        grads = []
        for half in range(2):
            side = pl.ds(half * hidden_dim, hidden_dim)
            grad_hidden = product_t(half_refs[half][2][...], grad_rows[...]).T
            gate_pre = pre_gate[:, side]
            sigma = jax.nn.sigmoid(gate_pre)
            grad_gate = grad_hidden * pre_up[:, side] * sigma * (1.0 + gate_pre * (1.0 - sigma))
            grad_up = grad_hidden * gate_pre * sigma
            grads.append((grad_gate.astype(jnp.bfloat16), grad_up.astype(jnp.bfloat16)))
        dotted = jnp.zeros((slots, 1), jnp.float32)
        for span in spans(width, 256):
            total = product_t(half_refs[0][0][span, :], grads[0][0])
            total = total + product_t(half_refs[0][1][span, :], grads[0][1])
            total = total + product_t(half_refs[1][0][span, :], grads[1][0])
            total = total + product_t(half_refs[1][1][span, :], grads[1][1])
            scaled = total.T * gain_ref[:, span]
            scaled_buf[:, span] = scaled
            dotted += jnp.sum(x_buf[:, span].astype(jnp.float32) * scaled, axis=-1, keepdims=True)
        back = inv_rms * inv_rms * inv_rms * (dotted / width)
        for span in spans(width, 512):
            grad_in = (
                grad_buf[:, span].astype(jnp.float32)
                + inv_rms * scaled_buf[:, span]
                - x_buf[:, span].astype(jnp.float32) * back
            ).astype(jnp.bfloat16)
            for part in range(parts):
                out_refs[part][:, span] = grad_in[part * rows : (part + 1) * rows]


def pack_kernel(micro_of, micro_count, parts, kinds, *refs):
    has_first, has_rest, has_route = kinds
    sec_ref, place_ref = refs[:2]
    rest = refs[2:]
    route_ref = rest[0] if has_route else None
    rest = rest[1:] if has_route else rest
    first_ref = rest[0] if has_first else None
    rest_ref = rest[1 if has_first else 0] if has_rest else None
    rest = rest[(1 if has_first else 0) + (1 if has_rest else 0) :]
    out_refs = rest[:parts]
    sec = sec_ref[0]
    micro = micro_of(sec)
    active = (micro >= 0) & (micro < micro_count)
    rows = out_refs[0].shape[0]
    width = out_refs[0].shape[1] - (lanes if has_route else 0)
    if has_route:
        rest[parts][0] = sec

    def put(source):
        table = place_ref[micro]
        if has_route:
            columns = coded(route_ref[micro])
            for part in range(parts):
                out_refs[part][:, width:] = columns[part * rows : (part + 1) * rows]
        for span in spans(width, 512):
            made = product(table, source[:, span]).astype(jnp.bfloat16)
            for part in range(parts):
                out_refs[part][:, span] = made[part * rows : (part + 1) * rows]

    if has_first:

        @pl.when((sec == 0) & active)
        def _():
            put(first_ref)

    if has_rest:

        @pl.when((sec > 0) & active if has_first else active)
        def _():
            put(rest_ref)


def forward_unpack(slot, micro_count, parts, *refs):
    sec_ref, take_ref = refs[:2]
    arrived = refs[2 : 2 + parts]
    out_ref = refs[2 + parts]
    micro = slot - sec_ref[0]

    @pl.when((micro >= 0) & (micro < micro_count))
    def _():
        for span in spans(out_ref.shape[1], 512):
            rows = jnp.concatenate([ref[:, span] for ref in arrived], axis=0)
            out_ref[:, span] = product(take_ref[micro], rows).astype(jnp.bfloat16)


def backward_unpack(slot, counts, parts, has_former, *refs):
    section_count, micro_count = counts
    sec_ref, take_ref = refs[:2]
    arrived = refs[2 : 2 + parts]
    result, gates, ordered, gate_rows, sems = refs[2 + parts + (2 if has_former else 0) :]
    micro = slot - 2 * (section_count - 1) + sec_ref[0]
    width = ordered.shape[1]

    @pl.when((micro >= 0) & (micro < micro_count))
    def _():
        def source(span):
            return jnp.concatenate([ref[:, span] for ref in arrived], axis=0)

        for span in spans(width, 512):
            ordered[:, span] = product(take_ref[micro], source(span)).astype(jnp.bfloat16)
        copy = pltpu.make_async_copy(ordered, result.at[micro], sems.at[0])
        copy.start()
        columns = decoded(product(take_ref[micro], source(pl.ds(width, lanes))))
        gate_rows[...] = jnp.broadcast_to(columns, gate_rows.shape)
        gate_copy = pltpu.make_async_copy(gate_rows, gates.at[micro], sems.at[1])
        gate_copy.start()
        copy.wait()
        gate_copy.wait()


def slots_of(route_ids, expert_count, capacity, turn):
    one_hot = (route_ids[:, :, None] == jnp.arange(expert_count, dtype=jnp.int32)).astype(jnp.int32)
    position = jnp.sum((jnp.cumsum(one_hot, axis=1, dtype=jnp.int32) - 1) * one_hot, axis=-1)
    return lax.rem(route_ids - turn + expert_count, expert_count) * capacity + position


def body(tokens_in, cotangent, norm_gain, w_gate, w_up, w_down, expert_ids, gate_weights):
    section_count = lax.axis_size("section")
    device_count = lax.axis_size("expert")
    section = lax.axis_index("section")
    place = lax.axis_index("expert") // 2
    expert_count = device_count // 2
    micro_count = expert_ids.shape[1]
    tok_rows = expert_ids.shape[2]
    model_dim = tokens_in.shape[2]
    hidden_dim = w_gate.shape[3]
    capacity = 2 * ((tok_rows + expert_count - 1) // expert_count)
    slots = expert_count * capacity
    by_permute = capacity % 16 == 0
    parts = expert_count if by_permute else 1
    rows = slots // parts
    turn = place if by_permute else jnp.int32(0)
    counts = (section_count, micro_count)
    first_back = section_count - 1
    slot_count = micro_count + 2 * (section_count - 1)
    sections = list(range(section_count))

    def exchange(chunks, members, direction):
        if by_permute:
            moved = [chunks[0]]
            for step in range(1, parts):
                pairs = [
                    (
                        s * device_count + 2 * z + core,
                        s * device_count + 2 * ((z + direction * step) % expert_count) + core,
                    )
                    for s in members
                    for z in range(expert_count)
                    for core in range(2)
                ]
                moved.append(lax.ppermute(chunks[step], both, sorted(pairs)))
            return moved
        (block,) = chunks
        shape = block.shape
        spread = block.reshape(-1, expert_count, capacity, shape[-1])
        groups = [[2 * z + core for z in range(expert_count)] for core in range(2)]
        spread = lax.all_to_all(
            spread, "expert", split_axis=1, concat_axis=1, tiled=True, axis_index_groups=groups
        )
        return [spread.reshape(shape)]

    def cut(block):
        return [block[:, part * rows : (part + 1) * rows] for part in range(parts)]

    own = (w_gate[0, 0], w_up[0, 0], w_down[0, 0])
    swap = [(i, i ^ 1) for i in range(device_count)]
    other = tuple(lax.ppermute(matrix, "expert", swap) for matrix in own)

    sec = section.reshape(1).astype(jnp.int32)
    gain = norm_gain
    ids = expert_ids[0, :, :, 0]
    slot_own = slots_of(ids, expert_count, capacity, turn)
    numbers = jnp.arange(slots, dtype=jnp.int32)
    is_own = numbers[None, :, None] == slot_own[:, None, :]
    place_own = is_own.astype(jnp.bfloat16)
    take_own = place_own.transpose(0, 2, 1)
    route_slots = jnp.sum(jnp.where(is_own, gate_weights[0, :, None, :, 0], 0.0), axis=-1)
    route = route_slots[:, :, None]

    def spread_inputs(own_section):
        own_tokens, own_cotangent = tokens_in[0], cotangent[0]
        cotangent_all = []
        for step in range(1, section_count):
            sent = jnp.where(own_section == step, own_tokens, own_cotangent)
            came = lax.ppermute(
                sent, "section", [(step, 0), (step - 1, section_count - 1)]
            )
            tokens_all.append(came)
            cotangent_all.append(came)
        cotangent_all.append(own_cotangent)
        packed = jnp.einsum(
            "mjt,mtd->mjd", place_own, jnp.stack(cotangent_all), preferred_element_type=jnp.float32
        ).astype(jnp.bfloat16)
        return exchange(cut(packed), [first_back], 1)

    tokens_all = [tokens_in[0]]
    first_grads = None

    chunk = jax.ShapeDtypeStruct((rows, model_dim), jnp.bfloat16)
    wide = jax.ShapeDtypeStruct((rows, model_dim + lanes), jnp.bfloat16)
    light = pl.CostEstimate(flops=0, bytes_accessed=0, transcendentals=0)
    state_shapes = [
        jax.ShapeDtypeStruct((slots, model_dim + lanes), jnp.bfloat16),
        jax.ShapeDtypeStruct((slots, 2 * hidden_dim), jnp.float32),
        jax.ShapeDtypeStruct((slots, 2 * hidden_dim), jnp.float32),
        jax.ShapeDtypeStruct((slots, model_dim), jnp.float32),
    ]

    saved = {}
    ahead = None
    behind = None
    results = None
    rows_shape = jax.ShapeDtypeStruct((tok_rows, model_dim), jnp.bfloat16)
    mark_shape = jax.ShapeDtypeStruct((1,), jnp.int32)
    matrix_shapes = [jax.ShapeDtypeStruct(m.shape, m.dtype) for m in own]
    for slot in range(slot_count):
        forward_on = [s for s in sections if 0 <= slot - s < micro_count]
        if forward_on:
            loading = slot == 0
            has_first = 0 in forward_on
            has_rest = ahead is not None
            outs = pl.pallas_call(
                partial(
                    pack_kernel,
                    lambda sec, slot=slot: slot - sec,
                    micro_count,
                    parts,
                    (has_first, has_rest, True),
                ),
                out_shape=[wide] * parts + [mark_shape],
                in_specs=[in_smem] + [in_vmem] * (2 + has_first + has_rest),
                out_specs=[in_vmem] * parts + [in_smem],
                compiler_params=params(4),
                cost_estimate=light,
                name=f"pack_forward_{slot}",
            )(
                sec,
                place_own,
                route,
                *([tokens_all[slot]] if has_first else []),
                *([ahead] if has_rest else []),
            )
            moved = exchange(outs[:parts], sections, 1)
            if loading:
                own = pl.pallas_call(
                    load_kernel,
                    out_shape=matrix_shapes,
                    in_specs=[in_smem] + [in_hbm] * 3,
                    out_specs=[in_vmem] * 3,
                    scratch_shapes=[pltpu.SemaphoreType.DMA((3,))],
                    compiler_params=params(42),
                    name="load_weights",
                )(outs[parts], *own)
                weights = (*own, *other)
            outs = pl.pallas_call(
                partial(forward_kernel, slot, micro_count, parts, loading),
                out_shape=[chunk] * parts
                + state_shapes
                + [mark_shape]
                + (matrix_shapes if loading else []),
                in_specs=[in_smem, in_vmem]
                + [in_vmem] * (parts + 3)
                + [in_hbm if loading else in_vmem] * 3,
                out_specs=[in_vmem] * (parts + 4) + [in_smem] + [in_vmem] * (3 if loading else 0),
                scratch_shapes=[
                    pltpu.VMEM((slots, model_dim), jnp.bfloat16),
                    pltpu.VMEM((2, slots, hidden_dim), jnp.bfloat16),
                ]
                + ([pltpu.SemaphoreType.DMA((3,))] if loading else []),
                compiler_params=params(28 if loading else 6),
                cost_estimate=light,
                name=f"expert_forward_{slot}",
            )(sec, gain, *moved, *weights)
            x_rows, pre_gate, pre_up, made = outs[parts : parts + 4]
            saved[slot] = (made, x_rows, pre_gate, pre_up)
            if loading:
                weights = (*own, *outs[parts + 5 :])
                first_grads = spread_inputs(outs[parts + 4][0])
            jobs = [(s, s + 1) for s in forward_on if s + 1 < section_count]
            ahead = None
            if jobs:
                home = exchange(outs[:parts], sections[:-1], -1)
                ordered = pl.pallas_call(
                    partial(forward_unpack, slot, micro_count, parts),
                    out_shape=rows_shape,
                    in_specs=[in_smem] + [in_vmem] * (1 + parts),
                    out_specs=in_vmem,
                    compiler_params=params(4),
                    cost_estimate=light,
                    name=f"unpack_forward_{slot}",
                )(sec, take_own, *home)
                ahead = lax.ppermute(ordered, "section", jobs)
        backward_on = [s for s in sections if 0 <= slot - 2 * first_back + s < micro_count]
        if backward_on:
            if behind is None:
                grads = [part[0] for part in first_grads]
            else:
                packed = pl.pallas_call(
                    partial(
                        pack_kernel,
                        lambda sec, slot=slot: slot - 2 * first_back + sec,
                        micro_count,
                        parts,
                        (False, True, False),
                    ),
                    out_shape=[chunk] * parts,
                    in_specs=[in_smem] + [in_vmem] * 2,
                    out_specs=[in_vmem] * parts,
                    compiler_params=params(4),
                    cost_estimate=light,
                    name=f"pack_backward_{slot}",
                )(sec, place_own, behind)
                grads = exchange(packed, sections[:-1], 1)
            states = []
            for s in backward_on:
                states += list(saved[slot - 2 * first_back + 2 * s])
            outs = pl.pallas_call(
                partial(backward_kernel, slot, counts, backward_on, parts),
                out_shape=[wide] * parts,
                in_specs=[in_smem, in_vmem]
                + [anywhere] * (2 * parts)
                + [in_vmem] * 6
                + [anywhere] * len(states),
                out_specs=[in_vmem] * parts,
                scratch_shapes=[
                    pltpu.VMEM((slots, model_dim), jnp.bfloat16),
                    pltpu.VMEM((slots, model_dim + lanes), jnp.bfloat16),
                    pltpu.VMEM((slots, 2 * hidden_dim), jnp.float32),
                    pltpu.VMEM((slots, 2 * hidden_dim), jnp.float32),
                    pltpu.VMEM((slots, model_dim), jnp.float32),
                    pltpu.VMEM((slots, model_dim), jnp.bfloat16),
                    pltpu.VMEM((slots, model_dim), jnp.float32),
                    pltpu.SemaphoreType.DMA((4,)),
                    pltpu.SemaphoreType.DMA((parts,)),
                ],
                compiler_params=params(8),
                cost_estimate=light,
                name=f"expert_backward_{slot}",
            )(sec, gain, *grads, *first_grads, *weights, *states)
            home = exchange(outs, sections, -1)
            has_former = results is not None
            outs = pl.pallas_call(
                partial(backward_unpack, slot, counts, parts, has_former),
                out_shape=[
                    jax.ShapeDtypeStruct((micro_count, tok_rows, model_dim), jnp.bfloat16),
                    jax.ShapeDtypeStruct((micro_count, tok_rows, lanes), jnp.float32),
                    rows_shape,
                ],
                in_specs=[in_smem] + [in_vmem] * (1 + parts) + [in_hbm] * (2 if has_former else 0),
                out_specs=[in_hbm] * 2 + [in_vmem],
                scratch_shapes=[
                    pltpu.VMEM((tok_rows, lanes), jnp.float32),
                    pltpu.SemaphoreType.DMA((2,)),
                ],
                input_output_aliases={2 + parts: 0, 3 + parts: 1} if has_former else {},
                compiler_params=params(4),
                cost_estimate=light,
                name=f"unpack_backward_{slot}",
            )(sec, take_own, *home, *(results if has_former else []))
            results = outs[:2]
            jobs = [(s, s - 1) for s in backward_on if s > 0]
            if slot + 1 < slot_count:
                behind = lax.ppermute(outs[2], "section", jobs)

    return (results[0][None], results[1][None, :, :, :1])


def solution(mesh):
    return jax.shard_map(
        body,
        mesh=mesh,
        in_specs=(
            P("section", "expert", None),
            P("section", "expert", None),
            P("section", None),
            P("section", "expert", None, None),
            P("section", "expert", None, None),
            P("section", "expert", None, None),
            P("section", None, "expert", None),
            P("section", None, "expert", None),
        ),
        out_specs=(P("section", None, "expert", None), P("section", None, "expert", None)),
        check_vma=False,
    )
```

```python
from functools import partial

import jax
import jax.numpy as jnp
from jax import lax
from jax.experimental import pallas as pl
from jax.experimental.pallas import tpu as pltpu
from jax.sharding import PartitionSpec as P

epsilon = 1e-06
both = ("section", "expert")
last_with_last = (((1,), (1,)), ((), ()))

in_vmem = pl.BlockSpec(memory_space=pltpu.VMEM)
in_smem = pl.BlockSpec(memory_space=pltpu.SMEM)
in_hbm = pl.BlockSpec(memory_space=pltpu.HBM)
lanes = 128


def spans(total, size):
    size = size if total % size == 0 else total
    return [pl.ds(start, size) for start in range(0, total, size)]


def params(mib):
    return pltpu.CompilerParams(vmem_limit_bytes=mib * 2**20)


def product(left, right):
    return jnp.dot(left, right, preferred_element_type=jnp.float32)


def product_t(left, right):
    return lax.dot_general(left, right, last_with_last, preferred_element_type=jnp.float32)


def coded(column):
    high = column.astype(jnp.bfloat16).astype(jnp.float32)
    left = column - high
    middle = left.astype(jnp.bfloat16).astype(jnp.float32)
    lane = lax.broadcasted_iota(jnp.int32, (column.shape[0], lanes), 1)
    spread = jnp.where(lane == 1, middle, jnp.where(lane == 2, left - middle, 0.0))
    return jnp.where(lane == 0, high, spread).astype(jnp.bfloat16)


def decoded(columns):
    return jnp.sum(columns.astype(jnp.float32), axis=-1, keepdims=True)


def load_kernel(mark_ref, *refs):
    copies = [
        pltpu.make_async_copy(refs[number], refs[3 + number], refs[6].at[number])
        for number in range(3)
    ]
    for copy in copies:
        copy.start()
    for copy in copies:
        copy.wait()


def choose_kernel(steps, mark_ref, sec_ref, tokens_ref, cotangent_ref, *out_refs):
    for step, out_ref in zip(steps, out_refs):

        @pl.when(sec_ref[0] == step)
        def _():
            out_ref[...] = tokens_ref[...]

        @pl.when(sec_ref[0] != step)
        def _():
            out_ref[...] = cotangent_ref[...]


def forward_kernel(slot, micro_count, parts, loading, *refs):
    sec_ref, gain_ref = refs[:2]
    x_refs = refs[2 : 2 + parts]
    given = refs[2 + parts : 8 + parts]
    rest = refs[8 + parts :]
    out_refs = rest[:parts]
    save_x, save_gate, save_up, save_rows, mark_ref = rest[parts : 5 + parts]
    rest = rest[5 + parts :]
    half_refs = [given[0:3], rest[0:3] if loading else given[3:6]]
    copies = []
    if loading:
        normed, hidden, sems = rest[3:]
        copies = [
            pltpu.make_async_copy(given[3 + number], half_refs[1][number], sems.at[number])
            for number in range(3)
        ]
        for copy in copies:
            copy.start()
    else:
        normed, hidden = rest
    mark_ref[0] = sec_ref[0]
    micro = slot - sec_ref[0]
    active = (micro >= 0) & (micro < micro_count)
    width = gain_ref.shape[1]
    hidden_dim = half_refs[0][0].shape[1]
    rows = x_refs[0].shape[0]

    @pl.when(active)
    def _():
        for part in range(parts):
            values = x_refs[part][:, :width].astype(jnp.float32)
            inv_rms = lax.rsqrt(jnp.mean(values * values, axis=-1, keepdims=True) + epsilon)
            here = pl.ds(part * rows, rows)
            normed[here, :] = (values * inv_rms * gain_ref[...]).astype(jnp.bfloat16)
            save_x[here, :] = x_refs[part][...]

    for half in range(2):
        if loading and half == 1:
            copies[0].wait()
            copies[1].wait()

        @pl.when(active)
        def _():
            side = pl.ds(half * hidden_dim, hidden_dim)
            gate_pre = product(normed[...], half_refs[half][0][...])
            up_pre = product(normed[...], half_refs[half][1][...])
            save_gate[:, side] = gate_pre
            save_up[:, side] = up_pre
            hidden[half] = (gate_pre * jax.nn.sigmoid(gate_pre) * up_pre).astype(jnp.bfloat16)

    if loading:
        copies[2].wait()

    @pl.when(active)
    def _():
        route = [decoded(x_refs[part][:, width:]) for part in range(parts)]
        for span in spans(width, 256):
            made = product(hidden[0], half_refs[0][2][:, span])
            made = made + product(hidden[1], half_refs[1][2][:, span])
            save_rows[:, span] = made
            for part in range(parts):
                added = route[part] * made[part * rows : (part + 1) * rows]
                values = x_refs[part][:, span].astype(jnp.float32)
                out_refs[part][:, span] = (values + added).astype(jnp.bfloat16)


def backward_kernel(slot, counts, candidates, parts, *refs):
    section_count, micro_count = counts
    sec_ref, gain_ref = refs[:2]
    rest = refs[2:]
    arrived = rest[:parts]
    first = rest[parts : 2 * parts]
    rest = rest[2 * parts :]
    half_refs = [rest[0:3], rest[3:6]]
    rest = rest[6:]
    saved = {}
    for section in candidates:
        saved[section] = rest[:4]
        rest = rest[4:]
    out_refs = rest[:parts]
    (grad_buf, x_buf, pre_gate, pre_up, rows_buf, grad_rows, scaled_buf, state_sems, grad_sems) = rest[parts:]
    sec = sec_ref[0]
    micro = slot - 2 * (section_count - 1) + sec
    width = gain_ref.shape[1]
    hidden_dim = half_refs[0][0].shape[1]
    slots = grad_buf.shape[0]
    rows = slots // parts

    @pl.when((micro >= 0) & (micro < micro_count))
    def _():
        def for_section(section, act):
            @pl.when(sec == section)
            def _():
                for part in range(parts):
                    if section == section_count - 1:
                        source = first[part].at[slot - (section_count - 1)]
                    else:
                        source = arrived[part]
                    act(pltpu.make_async_copy(
                        source, grad_buf.at[pl.ds(part * rows, rows), :], grad_sems.at[part]
                    ))
                targets = (rows_buf, x_buf, pre_gate, pre_up)
                for number, target in enumerate(targets):
                    act(pltpu.make_async_copy(
                        saved[section][number], target, state_sems.at[number]
                    ))

        for section in candidates:
            for_section(section, lambda copy: copy.start())
        for section in candidates:
            for_section(section, lambda copy: copy.wait())
        route = decoded(x_buf[:, width:])
        gate_grad = jnp.zeros((slots, 1), jnp.float32)
        square = jnp.zeros((slots, 1), jnp.float32)
        for span in spans(width, 512):
            grad_f = grad_buf[:, span].astype(jnp.float32)
            gate_grad += jnp.sum(grad_f * rows_buf[:, span], axis=-1, keepdims=True)
            grad_rows[:, span] = (route * grad_f).astype(jnp.bfloat16)
            values = x_buf[:, span].astype(jnp.float32)
            square += jnp.sum(values * values, axis=-1, keepdims=True)
        gate_columns = coded(gate_grad)
        for part in range(parts):
            out_refs[part][:, width:] = gate_columns[part * rows : (part + 1) * rows]
        inv_rms = lax.rsqrt(square / width + epsilon)
        grads = []
        for half in range(2):
            side = pl.ds(half * hidden_dim, hidden_dim)
            grad_hidden = product_t(half_refs[half][2][...], grad_rows[...]).T
            gate_pre = pre_gate[:, side]
            sigma = jax.nn.sigmoid(gate_pre)
            grad_gate = grad_hidden * pre_up[:, side] * sigma * (1.0 + gate_pre * (1.0 - sigma))
            grad_up = grad_hidden * gate_pre * sigma
            grads.append((grad_gate.astype(jnp.bfloat16), grad_up.astype(jnp.bfloat16)))
        dotted = jnp.zeros((slots, 1), jnp.float32)
        for span in spans(width, 256):
            total = product_t(half_refs[0][0][span, :], grads[0][0])
            total = total + product_t(half_refs[0][1][span, :], grads[0][1])
            total = total + product_t(half_refs[1][0][span, :], grads[1][0])
            total = total + product_t(half_refs[1][1][span, :], grads[1][1])
            scaled = total.T * gain_ref[:, span]
            scaled_buf[:, span] = scaled
            dotted += jnp.sum(x_buf[:, span].astype(jnp.float32) * scaled, axis=-1, keepdims=True)
        back = inv_rms * inv_rms * inv_rms * (dotted / width)
        for span in spans(width, 512):
            grad_in = (
                grad_buf[:, span].astype(jnp.float32)
                + inv_rms * scaled_buf[:, span]
                - x_buf[:, span].astype(jnp.float32) * back
            ).astype(jnp.bfloat16)
            for part in range(parts):
                out_refs[part][:, span] = grad_in[part * rows : (part + 1) * rows]


def forward_router(slot, micro_count, parts, has_first, has_rest, *refs):
    sec_ref, route_ref, place_ref, move_ref = refs[:4]
    rest = refs[4:]
    tokens_ref = rest[0] if has_first else None
    rest = rest[1:] if has_first else rest
    arrived = rest[:parts] if has_rest else None
    rest = rest[parts:] if has_rest else rest
    out_refs = rest[:parts]
    sec = sec_ref[0]
    rest[parts][0] = sec
    micro = slot - sec
    width = out_refs[0].shape[1] - lanes
    rows = out_refs[0].shape[0]

    def put(number, table, source):
        columns = coded(route_ref[number])
        for part in range(parts):
            out_refs[part][:, width:] = columns[part * rows : (part + 1) * rows]
        for span in spans(width, 512):
            made = product(table, source(span)).astype(jnp.bfloat16)
            for part in range(parts):
                out_refs[part][:, span] = made[part * rows : (part + 1) * rows]

    if has_first:

        @pl.when(sec == 0)
        def _():
            put(slot, place_ref[slot], lambda span: tokens_ref[:, span])

    if has_rest:

        @pl.when((sec > 0) & (micro >= 0) & (micro < micro_count))
        def _():
            put(
                micro,
                move_ref[micro],
                lambda span: jnp.concatenate([ref[:, span] for ref in arrived], axis=0),
            )


def backward_router(slot, counts, parts, has_former, onward, *refs):
    section_count, micro_count = counts
    sec_ref, take_ref, move_ref = refs[:3]
    arrived = refs[3 : 3 + parts]
    rest = refs[3 + parts + (2 if has_former else 0) :]
    result, gates = rest[:2]
    out_refs = rest[2 : 2 + parts] if onward else []
    ordered, gate_rows, sems = rest[2 + len(out_refs) :]
    sec = sec_ref[0]
    micro = slot - 2 * (section_count - 1) + sec
    width = arrived[0].shape[1] - lanes
    rows = arrived[0].shape[0]

    @pl.when((micro >= 0) & (micro < micro_count))
    def _():
        def source(span):
            return jnp.concatenate([ref[:, span] for ref in arrived], axis=0)

        if onward:

            @pl.when(sec > 0)
            def _():
                for span in spans(width, 512):
                    made = product(move_ref[micro], source(span)).astype(jnp.bfloat16)
                    for part in range(parts):
                        out_refs[part][:, span] = made[part * rows : (part + 1) * rows]

        for span in spans(width, 512):
            ordered[:, span] = product(take_ref[micro], source(span)).astype(jnp.bfloat16)
        copy = pltpu.make_async_copy(ordered, result.at[micro], sems.at[0])
        copy.start()
        columns = decoded(product(take_ref[micro], source(pl.ds(width, lanes))))
        gate_rows[...] = jnp.broadcast_to(columns, gate_rows.shape)
        gate_copy = pltpu.make_async_copy(gate_rows, gates.at[micro], sems.at[1])
        gate_copy.start()
        copy.wait()
        gate_copy.wait()


def slots_of(route_ids, expert_count, capacity, turn):
    count = route_ids.shape[1]
    before = jnp.arange(count)[None, :] < jnp.arange(count)[:, None]
    alike = (route_ids[:, None, :] == route_ids[:, :, None]) & before
    position = jnp.sum(alike.astype(jnp.int32), axis=-1)
    return (route_ids ^ turn) * capacity + position


def body(tokens_in, cotangent, norm_gain, w_gate, w_up, w_down, expert_ids, gate_weights):
    section_count = lax.axis_size("section")
    device_count = lax.axis_size("expert")
    section = lax.axis_index("section")
    place = lax.axis_index("expert") // 2
    expert_count = device_count // 2
    micro_count = expert_ids.shape[1]
    tok_rows = expert_ids.shape[2]
    model_dim = tokens_in.shape[2]
    hidden_dim = w_gate.shape[3]
    capacity = 2 * ((tok_rows + expert_count - 1) // expert_count)
    slots = expert_count * capacity
    by_permute = capacity % 16 == 0 and expert_count & (expert_count - 1) == 0
    parts = expert_count if by_permute else 1
    rows = slots // parts
    turn = place if by_permute else jnp.int32(0)
    counts = (section_count, micro_count)
    first_back = section_count - 1
    slot_count = micro_count + 2 * (section_count - 1)
    sections = list(range(section_count))

    def exchange(chunks, jobs):
        if by_permute:
            moved = [None] * parts
            for step in sorted(range(parts), key=lambda k: -min(k, parts - k)):
                if step == 0 and all(a == b for a, b in jobs):
                    moved[0] = chunks[0]
                    continue
                pairs = [
                    (a * device_count + 2 * z + core, b * device_count + 2 * (z ^ step) + core)
                    for a, b in jobs
                    for z in range(expert_count)
                    for core in range(2)
                ]
                moved[step] = lax.ppermute(chunks[step], both, pairs)
            return moved
        (block,) = chunks
        shape = block.shape
        spread = block.reshape(-1, expert_count, capacity, shape[-1])
        groups = [[2 * z + core for z in range(expert_count)] for core in range(2)]
        spread = lax.all_to_all(
            spread, "expert", split_axis=1, concat_axis=1, tiled=True, axis_index_groups=groups
        )
        block = spread.reshape(shape)
        if any(a != b for a, b in jobs):
            block = lax.ppermute(block, "section", jobs)
        return [block]

    def cut(block):
        return [block[:, part * rows : (part + 1) * rows] for part in range(parts)]

    own = (w_gate[0, 0], w_up[0, 0], w_down[0, 0])
    swap = [(i, i ^ 1) for i in range(device_count)]
    other = tuple(lax.ppermute(matrix, "expert", swap) for matrix in own)

    sec = section.reshape(1).astype(jnp.int32)
    gain = norm_gain
    ids = expert_ids[0, :, :, 0]
    onto_next = [(s, s + 1) for s in sections[:-1]]
    onto_former = [(s + 1, s) for s in sections[:-1]]
    numbers = jnp.arange(slots, dtype=jnp.int32)

    def placed(route_ids):
        turned = slots_of(route_ids, expert_count, capacity, turn)
        return numbers[None, :, None] == turned[:, None, :]

    is_own = placed(ids)
    place_own = is_own.astype(jnp.bfloat16)
    take_own = place_own.transpose(0, 2, 1)

    former_ids = lax.ppermute(
        ids, both, [(a * device_count + i, b * device_count + i) for a, b in onto_next for i in range(device_count)]
    )
    place_former = placed(former_ids).astype(jnp.bfloat16)
    move_forward = jnp.einsum("mjt,mit->mji", place_own, place_former)
    move_back = jnp.einsum("mjt,mit->mji", place_former, place_own)

    def staying(members):
        return [(s, s) for s in members]

    route_slots = jnp.sum(jnp.where(is_own, gate_weights[0, :, None, :, 0], 0.0), axis=-1)
    route = route_slots[:, :, None]

    def send_inputs(steps, mark):
        sent = pl.pallas_call(
            partial(choose_kernel, steps),
            out_shape=[rows_shape] * len(steps),
            in_specs=[in_smem] * 2 + [in_vmem] * 2,
            out_specs=[in_vmem] * len(steps),
            compiler_params=params(4),
            cost_estimate=light,
            name=f"choose_{steps[0]}",
        )(mark, sec, tokens_in[0], cotangent[0])
        for step, rows_sent in zip(steps, sent):
            came = lax.ppermute(rows_sent, "section", [(step, 0), (step - 1, section_count - 1)])
            tokens_all.append(came)
            cotangent_all.append(came)

    def send_cotangents():
        packed = jnp.einsum(
            "mjt,mtd->mjd",
            place_own,
            jnp.stack([*cotangent_all, cotangent[0]]),
            preferred_element_type=jnp.float32,
        ).astype(jnp.bfloat16)
        return exchange(cut(packed), staying([first_back]))

    cotangent_all = []
    tokens_all = [tokens_in[0]]
    first_grads = None

    chunk = jax.ShapeDtypeStruct((rows, model_dim), jnp.bfloat16)
    rows_shape = jax.ShapeDtypeStruct((tok_rows, model_dim), jnp.bfloat16)
    mark_shape = jax.ShapeDtypeStruct((1,), jnp.int32)
    matrix_shapes = [jax.ShapeDtypeStruct(m.shape, m.dtype) for m in own]
    wide = jax.ShapeDtypeStruct((rows, model_dim + lanes), jnp.bfloat16)
    light = pl.CostEstimate(flops=0, bytes_accessed=0, transcendentals=0)
    state_shapes = [
        jax.ShapeDtypeStruct((slots, model_dim + lanes), jnp.bfloat16),
        jax.ShapeDtypeStruct((slots, 2 * hidden_dim), jnp.float32),
        jax.ShapeDtypeStruct((slots, 2 * hidden_dim), jnp.float32),
        jax.ShapeDtypeStruct((slots, model_dim), jnp.float32),
    ]

    saved = {}
    ahead = None
    behind = None
    results = None
    for slot in range(slot_count):
        forward_on = [s for s in sections if 0 <= slot - s < micro_count]
        if forward_on:
            has_first = 0 in forward_on
            has_rest = ahead is not None
            loading = slot == 0
            outs = pl.pallas_call(
                partial(forward_router, slot, micro_count, parts, has_first, has_rest),
                out_shape=[wide] * parts + [mark_shape],
                in_specs=[in_smem, in_vmem, in_vmem, in_vmem]
                + [in_vmem] * ((1 if has_first else 0) + (parts if has_rest else 0)),
                out_specs=[in_vmem] * parts + [in_smem],
                compiler_params=params(4),
                cost_estimate=light,
                name=f"route_forward_{slot}",
            )(
                sec,
                route,
                place_own,
                move_forward,
                *([tokens_all[slot]] if has_first else []),
                *(ahead if has_rest else []),
            )
            busy = slot > section_count
            moved = exchange(outs[:parts], staying(forward_on if busy else sections))
            mark = outs[parts]
            if loading:
                own = pl.pallas_call(
                    load_kernel,
                    out_shape=matrix_shapes,
                    in_specs=[in_smem] + [in_hbm] * 3,
                    out_specs=[in_vmem] * 3,
                    scratch_shapes=[pltpu.SemaphoreType.DMA((3,))],
                    compiler_params=params(42),
                    name="load_weights",
                )(mark, *own)
                weights = (*own, *other)
                send_inputs([1], mark)
            if slot == 1:
                send_inputs(list(range(2, section_count)), mark)
                first_grads = send_cotangents()
            outs = pl.pallas_call(
                partial(forward_kernel, slot, micro_count, parts, loading),
                out_shape=[chunk] * parts
                + state_shapes
                + [jax.ShapeDtypeStruct((1,), jnp.int32)]
                + (matrix_shapes if loading else []),
                in_specs=[in_smem, in_vmem]
                + [in_vmem] * parts
                + [in_vmem] * 3
                + [in_hbm if loading else in_vmem] * 3,
                out_specs=[in_vmem] * (parts + 4) + [in_smem] + [in_vmem] * (3 if loading else 0),
                scratch_shapes=[
                    pltpu.VMEM((slots, model_dim), jnp.bfloat16),
                    pltpu.VMEM((2, slots, hidden_dim), jnp.bfloat16),
                ]
                + ([pltpu.SemaphoreType.DMA((3,))] if loading else []),
                compiler_params=params(28 if loading else 6),
                cost_estimate=light,
                name=f"expert_forward_{slot}",
            )(sec, gain, *moved, *weights)
            x_rows, pre_gate, pre_up, made = outs[parts : parts + 4]
            saved[slot] = (made, x_rows, pre_gate, pre_up)
            more = any(s + 1 < section_count for s in forward_on)
            jobs = [(a, b) for a, b in onto_next if a in forward_on] if busy else onto_next
            ahead = exchange(outs[:parts], jobs) if more else None
            if loading:
                weights = (*own, *outs[parts + 5 :])
        backward_on = [s for s in sections if 0 <= slot - 2 * first_back + s < micro_count]
        if backward_on:
            if behind is None:
                grads = [part[0] for part in first_grads]
            else:
                first_time = len(backward_on) == 2 and first_back in backward_on
                grads = exchange(behind, onto_former[-1:] if first_time else onto_former)
            states = []
            for s in backward_on:
                states += list(saved[slot - 2 * first_back + 2 * s])
            outs = pl.pallas_call(
                partial(backward_kernel, slot, counts, backward_on, parts),
                out_shape=[wide] * parts,
                in_specs=[in_smem, in_vmem] + [pl.BlockSpec(memory_space=pl.ANY)] * (2 * parts)
                + [in_vmem] * 6
                + [pl.BlockSpec(memory_space=pl.ANY)] * len(states),
                out_specs=[in_vmem] * parts,
                scratch_shapes=[
                    pltpu.VMEM((slots, model_dim), jnp.bfloat16),
                    pltpu.VMEM((slots, model_dim + lanes), jnp.bfloat16),
                    pltpu.VMEM((slots, 2 * hidden_dim), jnp.float32),
                    pltpu.VMEM((slots, 2 * hidden_dim), jnp.float32),
                    pltpu.VMEM((slots, model_dim), jnp.float32),
                    pltpu.VMEM((slots, model_dim), jnp.bfloat16),
                    pltpu.VMEM((slots, model_dim), jnp.float32),
                    pltpu.SemaphoreType.DMA((4,)),
                    pltpu.SemaphoreType.DMA((parts,)),
                ],
                compiler_params=params(8),
                cost_estimate=light,
                name=f"expert_backward_{slot}",
            )(sec, gain, *grads, *first_grads, *weights, *states)
            alone = slot < section_count + 1
            home = exchange(outs, staying(backward_on if alone else sections))
            onward = slot + 1 < slot_count
            has_former = results is not None
            outs = pl.pallas_call(
                partial(backward_router, slot, counts, parts, has_former, onward),
                out_shape=[
                    jax.ShapeDtypeStruct((micro_count, tok_rows, model_dim), jnp.bfloat16),
                    jax.ShapeDtypeStruct((micro_count, tok_rows, lanes), jnp.float32),
                ]
                + [chunk] * (parts if onward else 0),
                in_specs=[in_smem, in_vmem, in_vmem]
                + [in_vmem] * parts
                + [in_hbm] * (2 if has_former else 0),
                out_specs=[in_hbm] * 2 + [in_vmem] * (parts if onward else 0),
                scratch_shapes=[
                    pltpu.VMEM((tok_rows, model_dim), jnp.bfloat16),
                    pltpu.VMEM((tok_rows, lanes), jnp.float32),
                    pltpu.SemaphoreType.DMA((2,)),
                ],
                input_output_aliases={3 + parts: 0, 4 + parts: 1} if has_former else {},
                compiler_params=params(4),
                cost_estimate=light,
                name=f"route_backward_{slot}",
            )(sec, take_own, move_back, *home, *(results if has_former else []))
            results = outs[:2]
            behind = outs[2:]

    return (results[0][None], results[1][None, :, :, :1])


def solution(mesh):
    return jax.shard_map(
        body,
        mesh=mesh,
        in_specs=(
            P("section", "expert", None),
            P("section", "expert", None),
            P("section", None),
            P("section", "expert", None, None),
            P("section", "expert", None, None),
            P("section", "expert", None, None),
            P("section", None, "expert", None),
            P("section", None, "expert", None),
        ),
        out_specs=(P("section", None, "expert", None), P("section", None, "expert", None)),
        check_vma=False,
    )
```

```python
from functools import partial

import jax
import jax.numpy as jnp
from jax import lax
from jax.experimental import pallas as pl
from jax.experimental.pallas import tpu as pltpu
from jax.sharding import PartitionSpec as P

epsilon = 1e-06
both = ("section", "expert")
last_with_last = (((1,), (1,)), ((), ()))

in_vmem = pl.BlockSpec(memory_space=pltpu.VMEM)
in_smem = pl.BlockSpec(memory_space=pltpu.SMEM)
in_hbm = pl.BlockSpec(memory_space=pltpu.HBM)
lanes = 128


def spans(total, size):
    size = size if total % size == 0 else total
    return [pl.ds(start, size) for start in range(0, total, size)]


def params(mib):
    return pltpu.CompilerParams(vmem_limit_bytes=mib * 2**20)


def product(left, right):
    return jnp.dot(left, right, preferred_element_type=jnp.float32)


def product_t(left, right):
    return lax.dot_general(left, right, last_with_last, preferred_element_type=jnp.float32)


def coded(column):
    high = column.astype(jnp.bfloat16).astype(jnp.float32)
    left = column - high
    middle = left.astype(jnp.bfloat16).astype(jnp.float32)
    lane = lax.broadcasted_iota(jnp.int32, (column.shape[0], lanes), 1)
    spread = jnp.where(lane == 1, middle, jnp.where(lane == 2, left - middle, 0.0))
    return jnp.where(lane == 0, high, spread).astype(jnp.bfloat16)


def decoded(columns):
    return jnp.sum(columns.astype(jnp.float32), axis=-1, keepdims=True)


def load_kernel(mark_ref, *refs):
    copies = [
        pltpu.make_async_copy(refs[number], refs[3 + number], refs[7].at[number])
        for number in range(3)
    ]
    for copy in copies:
        copy.start()
    refs[6][0] = mark_ref[0]
    for copy in copies:
        copy.wait()


def choose_kernel(steps, mark_ref, sec_ref, tokens_ref, cotangent_ref, *out_refs):
    for step, out_ref in zip(steps, out_refs):

        @pl.when(sec_ref[0] == step)
        def _():
            out_ref[...] = tokens_ref[...]

        @pl.when(sec_ref[0] != step)
        def _():
            out_ref[...] = cotangent_ref[...]


def forward_kernel(slot, micro_count, parts, loading, *refs):
    sec_ref, gain_ref = refs[:2]
    x_refs = refs[2 : 2 + parts]
    given = refs[2 + parts : 8 + parts]
    rest = refs[8 + parts :]
    out_refs = rest[:parts]
    save_x, save_gate, save_up, save_rows, mark_ref = rest[parts : 5 + parts]
    rest = rest[5 + parts :]
    half_refs = [given[0:3], rest[0:3] if loading else given[3:6]]
    copies = []
    if loading:
        normed, hidden, sems = rest[3:]
        copies = [
            pltpu.make_async_copy(given[3 + number], half_refs[1][number], sems.at[number])
            for number in range(3)
        ]
        for copy in copies:
            copy.start()
    else:
        normed, hidden = rest
    mark_ref[0] = sec_ref[0]
    micro = slot - sec_ref[0]
    active = (micro >= 0) & (micro < micro_count)
    width = gain_ref.shape[1]
    hidden_dim = half_refs[0][0].shape[1]
    rows = x_refs[0].shape[0]

    @pl.when(active)
    def _():
        for part in range(parts):
            values = x_refs[part][:, :width].astype(jnp.float32)
            inv_rms = lax.rsqrt(jnp.mean(values * values, axis=-1, keepdims=True) + epsilon)
            here = pl.ds(part * rows, rows)
            normed[here, :] = (values * inv_rms * gain_ref[...]).astype(jnp.bfloat16)
            save_x[here, :] = x_refs[part][...]

    for half in range(2):
        if loading and half == 1:
            copies[0].wait()
            copies[1].wait()

        @pl.when(active)
        def _():
            side = pl.ds(half * hidden_dim, hidden_dim)
            gate_pre = product(normed[...], half_refs[half][0][...])
            up_pre = product(normed[...], half_refs[half][1][...])
            save_gate[:, side] = gate_pre
            save_up[:, side] = up_pre
            hidden[half] = (gate_pre * jax.nn.sigmoid(gate_pre) * up_pre).astype(jnp.bfloat16)

    if loading:
        copies[2].wait()

    @pl.when(active)
    def _():
        route = [decoded(x_refs[part][:, width:]) for part in range(parts)]
        for span in spans(width, 256):
            made = product(hidden[0], half_refs[0][2][:, span])
            made = made + product(hidden[1], half_refs[1][2][:, span])
            save_rows[:, span] = made
            for part in range(parts):
                added = route[part] * made[part * rows : (part + 1) * rows]
                values = x_refs[part][:, span].astype(jnp.float32)
                out_refs[part][:, span] = (values + added).astype(jnp.bfloat16)


def backward_kernel(slot, counts, candidates, parts, *refs):
    section_count, micro_count = counts
    sec_ref, gain_ref = refs[:2]
    rest = refs[2:]
    arrived = rest[:parts]
    first = rest[parts : 2 * parts]
    rest = rest[2 * parts :]
    half_refs = [rest[0:3], rest[3:6]]
    rest = rest[6:]
    saved = {}
    for section in candidates:
        saved[section] = rest[:4]
        rest = rest[4:]
    out_refs = rest[:parts]
    (grad_buf, x_buf, pre_gate, pre_up, rows_buf, grad_rows, scaled_buf, state_sems, grad_sems) = rest[parts:]
    sec = sec_ref[0]
    micro = slot - 2 * (section_count - 1) + sec
    width = gain_ref.shape[1]
    hidden_dim = half_refs[0][0].shape[1]
    slots = grad_buf.shape[0]
    rows = slots // parts

    @pl.when((micro >= 0) & (micro < micro_count))
    def _():
        def for_section(section, act):
            @pl.when(sec == section)
            def _():
                for part in range(parts):
                    if section == section_count - 1:
                        source = first[part].at[slot - (section_count - 1)]
                    else:
                        source = arrived[part]
                    act(pltpu.make_async_copy(
                        source, grad_buf.at[pl.ds(part * rows, rows), :], grad_sems.at[part]
                    ))
                targets = (rows_buf, x_buf, pre_gate, pre_up)
                for number, target in enumerate(targets):
                    act(pltpu.make_async_copy(
                        saved[section][number], target, state_sems.at[number]
                    ))

        for section in candidates:
            for_section(section, lambda copy: copy.start())
        for section in candidates:
            for_section(section, lambda copy: copy.wait())
        route = decoded(x_buf[:, width:])
        gate_grad = jnp.zeros((slots, 1), jnp.float32)
        square = jnp.zeros((slots, 1), jnp.float32)
        for span in spans(width, 512):
            grad_f = grad_buf[:, span].astype(jnp.float32)
            gate_grad += jnp.sum(grad_f * rows_buf[:, span], axis=-1, keepdims=True)
            grad_rows[:, span] = (route * grad_f).astype(jnp.bfloat16)
            values = x_buf[:, span].astype(jnp.float32)
            square += jnp.sum(values * values, axis=-1, keepdims=True)
        gate_columns = coded(gate_grad)
        for part in range(parts):
            out_refs[part][:, width:] = gate_columns[part * rows : (part + 1) * rows]
        inv_rms = lax.rsqrt(square / width + epsilon)
        grads = []
        for half in range(2):
            side = pl.ds(half * hidden_dim, hidden_dim)
            grad_hidden = product_t(half_refs[half][2][...], grad_rows[...]).T
            gate_pre = pre_gate[:, side]
            sigma = jax.nn.sigmoid(gate_pre)
            grad_gate = grad_hidden * pre_up[:, side] * sigma * (1.0 + gate_pre * (1.0 - sigma))
            grad_up = grad_hidden * gate_pre * sigma
            grads.append((grad_gate.astype(jnp.bfloat16), grad_up.astype(jnp.bfloat16)))
        dotted = jnp.zeros((slots, 1), jnp.float32)
        for span in spans(width, 256):
            total = product_t(half_refs[0][0][span, :], grads[0][0])
            total = total + product_t(half_refs[0][1][span, :], grads[0][1])
            total = total + product_t(half_refs[1][0][span, :], grads[1][0])
            total = total + product_t(half_refs[1][1][span, :], grads[1][1])
            scaled = total.T * gain_ref[:, span]
            scaled_buf[:, span] = scaled
            dotted += jnp.sum(x_buf[:, span].astype(jnp.float32) * scaled, axis=-1, keepdims=True)
        back = inv_rms * inv_rms * inv_rms * (dotted / width)
        for span in spans(width, 512):
            grad_in = (
                grad_buf[:, span].astype(jnp.float32)
                + inv_rms * scaled_buf[:, span]
                - x_buf[:, span].astype(jnp.float32) * back
            ).astype(jnp.bfloat16)
            for part in range(parts):
                out_refs[part][:, span] = grad_in[part * rows : (part + 1) * rows]


def forward_router(slot, micro_count, parts, has_first, has_rest, *refs):
    sec_ref, route_ref, place_ref, move_ref = refs[:4]
    rest = refs[4:]
    tokens_ref = rest[0] if has_first else None
    rest = rest[1:] if has_first else rest
    arrived = rest[:parts] if has_rest else None
    rest = rest[parts:] if has_rest else rest
    out_refs = rest[:parts]
    sec = sec_ref[0]
    rest[parts][0] = sec
    micro = slot - sec
    width = out_refs[0].shape[1] - lanes
    rows = out_refs[0].shape[0]

    def put(number, table, source):
        columns = coded(route_ref[number])
        for part in range(parts):
            out_refs[part][:, width:] = columns[part * rows : (part + 1) * rows]
        for span in spans(width, 512):
            made = product(table, source(span)).astype(jnp.bfloat16)
            for part in range(parts):
                out_refs[part][:, span] = made[part * rows : (part + 1) * rows]

    if has_first:

        @pl.when(sec == 0)
        def _():
            put(slot, place_ref[slot], lambda span: tokens_ref[:, span])

    if has_rest:

        @pl.when((sec > 0) & (micro >= 0) & (micro < micro_count))
        def _():
            put(
                micro,
                move_ref[micro],
                lambda span: jnp.concatenate([ref[:, span] for ref in arrived], axis=0),
            )


def backward_router(slot, counts, parts, has_former, onward, *refs):
    section_count, micro_count = counts
    sec_ref, take_ref, move_ref = refs[:3]
    arrived = refs[3 : 3 + parts]
    rest = refs[3 + parts + (2 if has_former else 0) :]
    result, gates = rest[:2]
    out_refs = rest[2 : 2 + parts] if onward else []
    ordered, gate_rows, sems = rest[2 + len(out_refs) :]
    sec = sec_ref[0]
    micro = slot - 2 * (section_count - 1) + sec
    width = arrived[0].shape[1] - lanes
    rows = arrived[0].shape[0]

    @pl.when((micro >= 0) & (micro < micro_count))
    def _():
        def source(span):
            return jnp.concatenate([ref[:, span] for ref in arrived], axis=0)

        if onward:

            @pl.when(sec > 0)
            def _():
                for span in spans(width, 512):
                    made = product(move_ref[micro], source(span)).astype(jnp.bfloat16)
                    for part in range(parts):
                        out_refs[part][:, span] = made[part * rows : (part + 1) * rows]

        for span in spans(width, 512):
            ordered[:, span] = product(take_ref[micro], source(span)).astype(jnp.bfloat16)
        copy = pltpu.make_async_copy(ordered, result.at[micro], sems.at[0])
        copy.start()
        columns = decoded(product(take_ref[micro], source(pl.ds(width, lanes))))
        gate_rows[...] = jnp.broadcast_to(columns, gate_rows.shape)
        gate_copy = pltpu.make_async_copy(gate_rows, gates.at[micro], sems.at[1])
        gate_copy.start()
        copy.wait()
        gate_copy.wait()


def slots_of(route_ids, expert_count, capacity, turn):
    count = route_ids.shape[1]
    before = jnp.arange(count)[None, :] < jnp.arange(count)[:, None]
    alike = (route_ids[:, None, :] == route_ids[:, :, None]) & before
    position = jnp.sum(alike.astype(jnp.int32), axis=-1)
    return lax.rem(route_ids - turn + expert_count, expert_count) * capacity + position


def body(tokens_in, cotangent, norm_gain, w_gate, w_up, w_down, expert_ids, gate_weights):
    section_count = lax.axis_size("section")
    device_count = lax.axis_size("expert")
    section = lax.axis_index("section")
    place = lax.axis_index("expert") // 2
    expert_count = device_count // 2
    micro_count = expert_ids.shape[1]
    tok_rows = expert_ids.shape[2]
    model_dim = tokens_in.shape[2]
    hidden_dim = w_gate.shape[3]
    capacity = 2 * ((tok_rows + expert_count - 1) // expert_count)
    slots = expert_count * capacity
    by_permute = capacity % 16 == 0
    parts = expert_count if by_permute else 1
    rows = slots // parts
    turn = place if by_permute else jnp.int32(0)
    counts = (section_count, micro_count)
    first_back = section_count - 1
    slot_count = micro_count + 2 * (section_count - 1)
    sections = list(range(section_count))

    def exchange(chunks, jobs, direction):
        if by_permute:
            moved = [None] * parts
            for step in sorted(range(parts), key=lambda k: -min(k, parts - k)):
                if step == 0 and all(a == b for a, b in jobs):
                    moved[0] = chunks[0]
                    continue
                pairs = [
                    (
                        a * device_count + 2 * z + core,
                        b * device_count + 2 * ((z + direction * step) % expert_count) + core,
                    )
                    for a, b in jobs
                    for z in range(expert_count)
                    for core in range(2)
                ]
                moved[step] = lax.ppermute(chunks[step], both, sorted(pairs))
            return moved
        (block,) = chunks
        shape = block.shape
        spread = block.reshape(-1, expert_count, capacity, shape[-1])
        groups = [[2 * z + core for z in range(expert_count)] for core in range(2)]
        spread = lax.all_to_all(
            spread, "expert", split_axis=1, concat_axis=1, tiled=True, axis_index_groups=groups
        )
        block = spread.reshape(shape)
        if any(a != b for a, b in jobs):
            block = lax.ppermute(block, "section", jobs)
        return [block]

    def cut(block):
        return [block[:, part * rows : (part + 1) * rows] for part in range(parts)]

    own = (w_gate[0, 0], w_up[0, 0], w_down[0, 0])
    swap = [(i, i ^ 1) for i in range(device_count)]
    other = tuple(lax.ppermute(matrix, "expert", swap) for matrix in own)

    sec = section.reshape(1).astype(jnp.int32)
    gain = norm_gain
    ids = expert_ids[0, :, :, 0]
    onto_next = [(s, s + 1) for s in sections[:-1]]
    onto_former = [(s + 1, s) for s in sections[:-1]]
    numbers = jnp.arange(slots, dtype=jnp.int32)

    def placed(route_ids):
        turned = slots_of(route_ids, expert_count, capacity, turn)
        return numbers[None, :, None] == turned[:, None, :]

    is_own = placed(ids)
    place_own = is_own.astype(jnp.bfloat16)
    take_own = place_own.transpose(0, 2, 1)

    former_ids = lax.ppermute(
        ids, both, [(a * device_count + i, b * device_count + i) for a, b in onto_next for i in range(device_count)]
    )
    place_former = placed(former_ids).astype(jnp.bfloat16)
    move_forward = jnp.einsum("mjt,mit->mji", place_own, place_former)
    move_back = jnp.einsum("mjt,mit->mji", place_former, place_own)

    def staying(members):
        return [(s, s) for s in members]

    route_slots = jnp.sum(jnp.where(is_own, gate_weights[0, :, None, :, 0], 0.0), axis=-1)
    route = route_slots[:, :, None]

    def send_inputs(steps, mark):
        sent = pl.pallas_call(
            partial(choose_kernel, steps),
            out_shape=[rows_shape] * len(steps),
            in_specs=[in_smem] * 2 + [in_vmem] * 2,
            out_specs=[in_vmem] * len(steps),
            compiler_params=params(4),
            cost_estimate=light,
            name=f"choose_{steps[0]}",
        )(mark, sec, tokens_in[0], cotangent[0])
        for step, rows_sent in zip(steps, sent):
            came = lax.ppermute(rows_sent, "section", [(step, 0), (step - 1, section_count - 1)])
            tokens_all.append(came)
            cotangent_all.append(came)

    def send_cotangents():
        packed = jnp.einsum(
            "mjt,mtd->mjd",
            place_own,
            jnp.stack([*cotangent_all, cotangent[0]]),
            preferred_element_type=jnp.float32,
        ).astype(jnp.bfloat16)
        return exchange(cut(packed), staying([first_back]), 1)

    cotangent_all = []
    tokens_all = [tokens_in[0]]
    first_grads = None

    chunk = jax.ShapeDtypeStruct((rows, model_dim), jnp.bfloat16)
    rows_shape = jax.ShapeDtypeStruct((tok_rows, model_dim), jnp.bfloat16)
    mark_shape = jax.ShapeDtypeStruct((1,), jnp.int32)
    matrix_shapes = [jax.ShapeDtypeStruct(m.shape, m.dtype) for m in own]
    wide = jax.ShapeDtypeStruct((rows, model_dim + lanes), jnp.bfloat16)
    light = pl.CostEstimate(flops=0, bytes_accessed=0, transcendentals=0)
    state_shapes = [
        jax.ShapeDtypeStruct((slots, model_dim + lanes), jnp.bfloat16),
        jax.ShapeDtypeStruct((slots, 2 * hidden_dim), jnp.float32),
        jax.ShapeDtypeStruct((slots, 2 * hidden_dim), jnp.float32),
        jax.ShapeDtypeStruct((slots, model_dim), jnp.float32),
    ]

    saved = {}
    ahead = None
    behind = None
    results = None
    for slot in range(slot_count):
        forward_on = [s for s in sections if 0 <= slot - s < micro_count]
        if forward_on:
            has_first = 0 in forward_on
            has_rest = ahead is not None
            loading = slot == 0
            outs = pl.pallas_call(
                partial(forward_router, slot, micro_count, parts, has_first, has_rest),
                out_shape=[wide] * parts + [mark_shape],
                in_specs=[in_smem, in_vmem, in_vmem, in_vmem]
                + [in_vmem] * ((1 if has_first else 0) + (parts if has_rest else 0)),
                out_specs=[in_vmem] * parts + [in_smem],
                compiler_params=params(4),
                cost_estimate=light,
                name=f"route_forward_{slot}",
            )(
                sec,
                route,
                place_own,
                move_forward,
                *([tokens_all[slot]] if has_first else []),
                *(ahead if has_rest else []),
            )
            busy = slot > section_count
            moved = exchange(outs[:parts], staying(forward_on if busy else sections), 1)
            mark = outs[parts]
            if loading:
                *own, mark = pl.pallas_call(
                    load_kernel,
                    out_shape=matrix_shapes + [mark_shape],
                    in_specs=[in_smem] + [in_hbm] * 3,
                    out_specs=[in_vmem] * 3 + [in_smem],
                    scratch_shapes=[pltpu.SemaphoreType.DMA((3,))],
                    compiler_params=params(42),
                    name="load_weights",
                )(mark, *own)
                weights = (*own, *other)
                send_inputs([1], mark)
            if slot == 1:
                send_inputs(list(range(2, section_count)), mark)
                first_grads = send_cotangents()
            outs = pl.pallas_call(
                partial(forward_kernel, slot, micro_count, parts, loading),
                out_shape=[chunk] * parts
                + state_shapes
                + [jax.ShapeDtypeStruct((1,), jnp.int32)]
                + (matrix_shapes if loading else []),
                in_specs=[in_smem, in_vmem]
                + [in_vmem] * parts
                + [in_vmem] * 3
                + [in_hbm if loading else in_vmem] * 3,
                out_specs=[in_vmem] * (parts + 4) + [in_smem] + [in_vmem] * (3 if loading else 0),
                scratch_shapes=[
                    pltpu.VMEM((slots, model_dim), jnp.bfloat16),
                    pltpu.VMEM((2, slots, hidden_dim), jnp.bfloat16),
                ]
                + ([pltpu.SemaphoreType.DMA((3,))] if loading else []),
                compiler_params=params(28 if loading else 6),
                cost_estimate=light,
                name=f"expert_forward_{slot}",
            )(sec, gain, *moved, *weights)
            x_rows, pre_gate, pre_up, made = outs[parts : parts + 4]
            saved[slot] = (made, x_rows, pre_gate, pre_up)
            more = any(s + 1 < section_count for s in forward_on)
            jobs = [(a, b) for a, b in onto_next if a in forward_on] if busy else onto_next
            ahead = exchange(outs[:parts], jobs, -1) if more else None
            if loading:
                weights = (*own, *outs[parts + 5 :])
        backward_on = [s for s in sections if 0 <= slot - 2 * first_back + s < micro_count]
        if backward_on:
            if behind is None:
                grads = [part[0] for part in first_grads]
            else:
                first_time = len(backward_on) == 2 and first_back in backward_on
                grads = exchange(behind, onto_former[-1:] if first_time else onto_former, 1)
            states = []
            for s in backward_on:
                states += list(saved[slot - 2 * first_back + 2 * s])
            outs = pl.pallas_call(
                partial(backward_kernel, slot, counts, backward_on, parts),
                out_shape=[wide] * parts,
                in_specs=[in_smem, in_vmem] + [pl.BlockSpec(memory_space=pl.ANY)] * (2 * parts)
                + [in_vmem] * 6
                + [pl.BlockSpec(memory_space=pl.ANY)] * len(states),
                out_specs=[in_vmem] * parts,
                scratch_shapes=[
                    pltpu.VMEM((slots, model_dim), jnp.bfloat16),
                    pltpu.VMEM((slots, model_dim + lanes), jnp.bfloat16),
                    pltpu.VMEM((slots, 2 * hidden_dim), jnp.float32),
                    pltpu.VMEM((slots, 2 * hidden_dim), jnp.float32),
                    pltpu.VMEM((slots, model_dim), jnp.float32),
                    pltpu.VMEM((slots, model_dim), jnp.bfloat16),
                    pltpu.VMEM((slots, model_dim), jnp.float32),
                    pltpu.SemaphoreType.DMA((4,)),
                    pltpu.SemaphoreType.DMA((parts,)),
                ],
                compiler_params=params(8),
                cost_estimate=light,
                name=f"expert_backward_{slot}",
            )(sec, gain, *grads, *first_grads, *weights, *states)
            alone = slot < section_count + 1
            home = exchange(outs, staying(backward_on if alone else sections), -1)
            onward = slot + 1 < slot_count
            has_former = results is not None
            outs = pl.pallas_call(
                partial(backward_router, slot, counts, parts, has_former, onward),
                out_shape=[
                    jax.ShapeDtypeStruct((micro_count, tok_rows, model_dim), jnp.bfloat16),
                    jax.ShapeDtypeStruct((micro_count, tok_rows, lanes), jnp.float32),
                ]
                + [chunk] * (parts if onward else 0),
                in_specs=[in_smem, in_vmem, in_vmem]
                + [in_vmem] * parts
                + [in_hbm] * (2 if has_former else 0),
                out_specs=[in_hbm] * 2 + [in_vmem] * (parts if onward else 0),
                scratch_shapes=[
                    pltpu.VMEM((tok_rows, model_dim), jnp.bfloat16),
                    pltpu.VMEM((tok_rows, lanes), jnp.float32),
                    pltpu.SemaphoreType.DMA((2,)),
                ],
                input_output_aliases={3 + parts: 0, 4 + parts: 1} if has_former else {},
                compiler_params=params(4),
                cost_estimate=light,
                name=f"route_backward_{slot}",
            )(sec, take_own, move_back, *home, *(results if has_former else []))
            results = outs[:2]
            behind = outs[2:]

    return (results[0][None], results[1][None, :, :, :1])


def solution(mesh):
    return jax.shard_map(
        body,
        mesh=mesh,
        in_specs=(
            P("section", "expert", None),
            P("section", "expert", None),
            P("section", None),
            P("section", "expert", None, None),
            P("section", "expert", None, None),
            P("section", "expert", None, None),
            P("section", None, "expert", None),
            P("section", None, "expert", None),
        ),
        out_specs=(P("section", None, "expert", None), P("section", None, "expert", None)),
        check_vma=False,
    )
```

```python
from functools import partial

import jax
import jax.numpy as jnp
from jax import lax
from jax.experimental import pallas as pl
from jax.experimental.pallas import tpu as pltpu
from jax.sharding import PartitionSpec as P

epsilon = 1e-06
both = ("section", "expert")
last_with_last = (((1,), (1,)), ((), ()))

in_vmem = pl.BlockSpec(memory_space=pltpu.VMEM)
in_smem = pl.BlockSpec(memory_space=pltpu.SMEM)
in_hbm = pl.BlockSpec(memory_space=pltpu.HBM)
anywhere = pl.BlockSpec(memory_space=pl.ANY)
lanes = 128


def spans(total, size):
    size = size if total % size == 0 else total
    return [pl.ds(start, size) for start in range(0, total, size)]


def params(mib):
    return pltpu.CompilerParams(vmem_limit_bytes=mib * 2**20)


def product(left, right):
    return jnp.dot(left, right, preferred_element_type=jnp.float32)


def product_t(left, right):
    return lax.dot_general(left, right, last_with_last, preferred_element_type=jnp.float32)


def coded(column, number=None):
    high = column.astype(jnp.bfloat16).astype(jnp.float32)
    left = column - high
    middle = left.astype(jnp.bfloat16).astype(jnp.float32)
    lane = lax.broadcasted_iota(jnp.int32, (column.shape[0], lanes), 1)
    spread = jnp.where(lane == 1, middle, jnp.where(lane == 2, left - middle, 0.0))
    spread = jnp.where(lane == 0, high, spread)
    if number is not None:
        spread = jnp.where(lane == 3, number, spread)
    return spread.astype(jnp.bfloat16)


def decoded(columns):
    lane = lax.broadcasted_iota(jnp.int32, columns.shape, 1)
    values = jnp.where(lane < 3, columns.astype(jnp.float32), 0.0)
    return jnp.sum(values, axis=-1, keepdims=True)


def numbered(columns):
    lane = lax.broadcasted_iota(jnp.int32, columns.shape, 1)
    values = columns.astype(jnp.float32)
    number = jnp.sum(jnp.where(lane == 3, values, 0.0), axis=-1, keepdims=True)
    return (number == (lane + 1).astype(jnp.float32)).astype(jnp.bfloat16)


def load_kernel(mark_ref, *refs):
    copies = [
        pltpu.make_async_copy(refs[number], refs[3 + number], refs[6].at[number])
        for number in range(3)
    ]
    for copy in copies:
        copy.start()
    for copy in copies:
        copy.wait()


def choose_kernel(steps, after_ref, sec_ref, tokens_ref, cotangent_ref, *out_refs):
    for step, out_ref in zip(steps, out_refs):

        @pl.when(sec_ref[0] == step)
        def _():
            out_ref[...] = tokens_ref[...]

        @pl.when(sec_ref[0] != step)
        def _():
            out_ref[...] = cotangent_ref[...]


def forward_kernel(slot, micro_count, parts, loading, later, *refs):
    sec_ref, gain_ref = refs[:2]
    x_refs = refs[2 : 2 + parts]
    given = refs[2 + parts : 8 + parts]
    rest = refs[8 + parts + later :]
    if loading:
        inputs, rest = rest[:2], rest[2:]
    out_refs = rest[:parts]
    save_x, save_gate, save_up, save_rows = rest[parts : 4 + parts]
    rest = rest[4 + parts :]
    if loading:
        choose_kernel([1], None, sec_ref, *inputs, rest[0])
        rest = rest[1:]
    half_refs = [given[0:3], rest[0:3] if loading else given[3:6]]
    copies = []
    if loading:
        normed, hidden, sems = rest[3:]
        copies = [
            pltpu.make_async_copy(given[3 + number], half_refs[1][number], sems.at[number])
            for number in range(3)
        ]
        for copy in copies:
            copy.start()
    else:
        normed, hidden = rest
    micro = slot - sec_ref[0]
    active = (micro >= 0) & (micro < micro_count)
    width = gain_ref.shape[1]
    hidden_dim = half_refs[0][0].shape[1]
    rows = x_refs[0].shape[0]

    @pl.when(active)
    def _():
        for part in range(parts):
            values = x_refs[part][:, :width].astype(jnp.float32)
            inv_rms = lax.rsqrt(jnp.mean(values * values, axis=-1, keepdims=True) + epsilon)
            here = pl.ds(part * rows, rows)
            normed[here, :] = (values * inv_rms * gain_ref[...]).astype(jnp.bfloat16)
            save_x[here, :] = x_refs[part][...]
            out_refs[part][:, width:] = x_refs[part][:, width:]

    for half in range(2):
        if loading and half == 1:
            copies[0].wait()
            copies[1].wait()

        @pl.when(active)
        def _():
            side = pl.ds(half * hidden_dim, hidden_dim)
            gate_pre = product(normed[...], half_refs[half][0][...])
            up_pre = product(normed[...], half_refs[half][1][...])
            save_gate[:, side] = gate_pre
            save_up[:, side] = up_pre
            hidden[half] = (gate_pre * jax.nn.sigmoid(gate_pre) * up_pre).astype(jnp.bfloat16)

    if loading:
        copies[2].wait()

    @pl.when(active)
    def _():
        route = [decoded(x_refs[part][:, width:]) for part in range(parts)]
        for span in spans(width, 256):
            made = product(hidden[0], half_refs[0][2][:, span])
            made = made + product(hidden[1], half_refs[1][2][:, span])
            save_rows[:, span] = made
            for part in range(parts):
                added = route[part] * made[part * rows : (part + 1) * rows]
                values = x_refs[part][:, span].astype(jnp.float32)
                out_refs[part][:, span] = (values + added).astype(jnp.bfloat16)


def backward_kernel(slot, counts, candidates, parts, *refs):
    section_count, micro_count = counts
    sec_ref, gain_ref = refs[:2]
    rest = refs[2:]
    arrived = rest[:parts]
    first = rest[parts : 2 * parts]
    rest = rest[2 * parts :]
    half_refs = [rest[0:3], rest[3:6]]
    rest = rest[6:]
    saved = {}
    for section in candidates:
        saved[section] = rest[:4]
        rest = rest[4:]
    out_refs = rest[:parts]
    (grad_buf, x_buf, pre_gate, pre_up, rows_buf, grad_rows, scaled_buf, state_sems, grad_sems) = rest[parts:]
    sec = sec_ref[0]
    micro = slot - 2 * (section_count - 1) + sec
    width = gain_ref.shape[1]
    hidden_dim = half_refs[0][0].shape[1]
    slots = grad_buf.shape[0]
    rows = slots // parts

    @pl.when((micro >= 0) & (micro < micro_count))
    def _():
        def for_section(section, act):
            @pl.when(sec == section)
            def _():
                for part in range(parts):
                    if section == section_count - 1:
                        source = first[part].at[slot - (section_count - 1)]
                    else:
                        source = arrived[part]
                    act(pltpu.make_async_copy(
                        source, grad_buf.at[pl.ds(part * rows, rows), :], grad_sems.at[part]
                    ))
                targets = (rows_buf, x_buf, pre_gate, pre_up)
                for number, target in enumerate(targets):
                    act(pltpu.make_async_copy(
                        saved[section][number], target, state_sems.at[number]
                    ))

        for section in candidates:
            for_section(section, lambda copy: copy.start())
        for section in candidates:
            for_section(section, lambda copy: copy.wait())
        route = decoded(x_buf[:, width:])
        gate_grad = jnp.zeros((slots, 1), jnp.float32)
        square = jnp.zeros((slots, 1), jnp.float32)
        for span in spans(width, 512):
            grad_f = grad_buf[:, span].astype(jnp.float32)
            gate_grad += jnp.sum(grad_f * rows_buf[:, span], axis=-1, keepdims=True)
            grad_rows[:, span] = (route * grad_f).astype(jnp.bfloat16)
            values = x_buf[:, span].astype(jnp.float32)
            square += jnp.sum(values * values, axis=-1, keepdims=True)
        gate_columns = coded(gate_grad)
        for part in range(parts):
            out_refs[part][:, width:] = gate_columns[part * rows : (part + 1) * rows]
        inv_rms = lax.rsqrt(square / width + epsilon)
        grads = []
        for half in range(2):
            side = pl.ds(half * hidden_dim, hidden_dim)
            grad_hidden = product_t(half_refs[half][2][...], grad_rows[...]).T
            gate_pre = pre_gate[:, side]
            sigma = jax.nn.sigmoid(gate_pre)
            grad_gate = grad_hidden * pre_up[:, side] * sigma * (1.0 + gate_pre * (1.0 - sigma))
            grad_up = grad_hidden * gate_pre * sigma
            grads.append((grad_gate.astype(jnp.bfloat16), grad_up.astype(jnp.bfloat16)))
        dotted = jnp.zeros((slots, 1), jnp.float32)
        for span in spans(width, 256):
            total = product_t(half_refs[0][0][span, :], grads[0][0])
            total = total + product_t(half_refs[0][1][span, :], grads[0][1])
            total = total + product_t(half_refs[1][0][span, :], grads[1][0])
            total = total + product_t(half_refs[1][1][span, :], grads[1][1])
            scaled = total.T * gain_ref[:, span]
            scaled_buf[:, span] = scaled
            dotted += jnp.sum(x_buf[:, span].astype(jnp.float32) * scaled, axis=-1, keepdims=True)
        back = inv_rms * inv_rms * inv_rms * (dotted / width)
        for span in spans(width, 512):
            grad_in = (
                grad_buf[:, span].astype(jnp.float32)
                + inv_rms * scaled_buf[:, span]
                - x_buf[:, span].astype(jnp.float32) * back
            ).astype(jnp.bfloat16)
            for part in range(parts):
                out_refs[part][:, span] = grad_in[part * rows : (part + 1) * rows]


def forward_router(slot, micro_count, parts, has_first, has_rest, *refs):
    sec_ref, route_ref, place_ref = refs[:3]
    rest = refs[3:]
    tokens_ref = rest[0] if has_first else None
    rest = rest[1:] if has_first else rest
    arrived = rest[:parts] if has_rest else None
    rest = rest[parts:] if has_rest else rest
    rest = rest[1:] if slot == 2 else rest
    out_refs = rest[:parts]
    sec = sec_ref[0]
    rest[parts][0] = sec
    micro = slot - sec
    width = out_refs[0].shape[1] - lanes
    rows = out_refs[0].shape[0]

    def put(number, table, source):
        place = place_ref[number].astype(jnp.float32)
        lane = lax.broadcasted_iota(jnp.int32, place.shape, 1)
        token = jnp.sum(place * (lane + 1).astype(jnp.float32), axis=-1, keepdims=True)
        columns = coded(route_ref[number], token)
        for part in range(parts):
            out_refs[part][:, width:] = columns[part * rows : (part + 1) * rows]
        for span in spans(width, 512):
            made = product(table, source(span)).astype(jnp.bfloat16)
            for part in range(parts):
                out_refs[part][:, span] = made[part * rows : (part + 1) * rows]

    if has_first:

        @pl.when(sec == 0)
        def _():
            table = place_ref[slot][:, : tokens_ref.shape[0]]
            put(slot, table, lambda span: tokens_ref[:, span])

    if has_rest:

        @pl.when((sec > 0) & (micro >= 0) & (micro < micro_count))
        def _():
            def source(span):
                return jnp.concatenate([ref[:, span] for ref in arrived], axis=0)

            former = numbered(source(pl.ds(width, lanes)))
            rest[parts + 1][...] = former
            put(micro, product_t(place_ref[micro], former).astype(jnp.bfloat16), source)


def backward_router(slot, counts, parts, has_former, onward, *refs):
    section_count, micro_count = counts
    sec_ref, take_ref, place_ref = refs[:3]
    arrived = refs[3 : 3 + parts]
    rest = refs[3 + parts + (2 if has_former else 0) :]
    formers, rest = rest[: len(onward)], rest[len(onward) :]
    result, gates = rest[:2]
    out_refs = rest[2 : 2 + parts] if onward else []
    ordered, gate_rows, sems = rest[2 + len(out_refs) :]
    sec = sec_ref[0]
    micro = slot - 2 * (section_count - 1) + sec
    width = arrived[0].shape[1] - lanes
    rows = arrived[0].shape[0]

    @pl.when((micro >= 0) & (micro < micro_count))
    def _():
        def source(span):
            return jnp.concatenate([ref[:, span] for ref in arrived], axis=0)

        for section, former in zip(onward, formers):

            @pl.when(sec == section)
            def _():
                table = product_t(former[...], place_ref[micro]).astype(jnp.bfloat16)
                for span in spans(width, 512):
                    made = product(table, source(span)).astype(jnp.bfloat16)
                    for part in range(parts):
                        out_refs[part][:, span] = made[part * rows : (part + 1) * rows]

        for span in spans(width, 512):
            ordered[:, span] = product(take_ref[micro], source(span)).astype(jnp.bfloat16)
        copy = pltpu.make_async_copy(ordered, result.at[micro], sems.at[0])
        copy.start()
        columns = decoded(product(take_ref[micro], source(pl.ds(width, lanes))))
        gate_rows[...] = jnp.broadcast_to(columns, gate_rows.shape)
        gate_copy = pltpu.make_async_copy(gate_rows, gates.at[micro], sems.at[1])
        gate_copy.start()
        copy.wait()
        gate_copy.wait()


def slots_of(route_ids, expert_count, capacity, turn):
    count = route_ids.shape[1]
    before = jnp.arange(count)[None, :] < jnp.arange(count)[:, None]
    alike = (route_ids[:, None, :] == route_ids[:, :, None]) & before
    position = jnp.sum(alike.astype(jnp.int32), axis=-1)
    return lax.rem(route_ids - turn + expert_count, expert_count) * capacity + position


def body(tokens_in, cotangent, norm_gain, w_gate, w_up, w_down, expert_ids, gate_weights):
    section_count = lax.axis_size("section")
    device_count = lax.axis_size("expert")
    section = lax.axis_index("section")
    place = lax.axis_index("expert") // 2
    expert_count = device_count // 2
    micro_count = expert_ids.shape[1]
    tok_rows = expert_ids.shape[2]
    model_dim = tokens_in.shape[2]
    hidden_dim = w_gate.shape[3]
    capacity = 2 * ((tok_rows + expert_count - 1) // expert_count)
    slots = expert_count * capacity
    by_permute = capacity % 16 == 0
    parts = expert_count if by_permute else 1
    rows = slots // parts
    turn = place if by_permute else jnp.int32(0)
    counts = (section_count, micro_count)
    first_back = section_count - 1
    slot_count = micro_count + 2 * (section_count - 1)
    sections = list(range(section_count))

    def exchange(chunks, jobs, direction):
        if by_permute:
            moved = [None] * parts
            for step in sorted(range(parts), key=lambda k: -min(k, parts - k)):
                if step == 0 and all(a == b for a, b in jobs):
                    moved[0] = chunks[0]
                    continue
                pairs = [
                    (
                        a * device_count + 2 * z + core,
                        b * device_count + 2 * ((z + direction * step) % expert_count) + core,
                    )
                    for a, b in jobs
                    for z in range(expert_count)
                    for core in range(2)
                ]
                moved[step] = lax.ppermute(chunks[step], both, sorted(pairs))
            return moved
        (block,) = chunks
        shape = block.shape
        spread = block.reshape(-1, expert_count, capacity, shape[-1])
        groups = [[2 * z + core for z in range(expert_count)] for core in range(2)]
        spread = lax.all_to_all(
            spread, "expert", split_axis=1, concat_axis=1, tiled=True, axis_index_groups=groups
        )
        block = spread.reshape(shape)
        if any(a != b for a, b in jobs):
            block = lax.ppermute(block, "section", jobs)
        return [block]

    def cut(block):
        return [block[:, part * rows : (part + 1) * rows] for part in range(parts)]

    own = (w_gate[0, 0], w_up[0, 0], w_down[0, 0])
    swap = [(i, i ^ 1) for i in range(device_count)]
    other = [lax.ppermute(matrix, "expert", swap) for matrix in own]

    sec = section.reshape(1).astype(jnp.int32)
    gain = norm_gain
    ids = expert_ids[0, :, :, 0]
    onto_next = [(s, s + 1) for s in sections[:-1]]
    onto_former = [(s + 1, s) for s in sections[:-1]]
    numbers = jnp.arange(slots, dtype=jnp.int32)

    slot_own = slots_of(ids, expert_count, capacity, turn)
    padded = jnp.pad(slot_own, ((0, 0), (0, lanes - tok_rows)), constant_values=-1)
    place_wide = (numbers[None, :, None] == padded[:, None, :]).astype(jnp.bfloat16)
    is_own = numbers[None, :, None] == slot_own[:, None, :]
    place_own = is_own.astype(jnp.bfloat16)
    take_own = place_own.transpose(0, 2, 1)

    def staying(members):
        return [(s, s) for s in members]

    route_slots = jnp.sum(jnp.where(is_own, gate_weights[0, :, None, :, 0], 0.0), axis=-1)
    route = route_slots[:, :, None]

    def send_inputs(after):
        steps = list(range(2, section_count))
        sent = pl.pallas_call(
            partial(choose_kernel, steps),
            out_shape=[rows_shape] * len(steps),
            in_specs=[anywhere, in_smem] + [in_vmem] * 2,
            out_specs=[in_vmem] * len(steps),
            compiler_params=params(4),
            cost_estimate=light,
            name="choose_inputs",
        )(after, sec, tokens_in[0], cotangent[0])
        for step, rows_sent in zip(steps, sent):
            travel(step, rows_sent)

    def travel(step, rows_sent):
        came = lax.ppermute(rows_sent, "section", [(step, 0), (step - 1, section_count - 1)])
        tokens_all.append(came)
        cotangent_all.append(came)
        return came

    def send_cotangents():
        packed = jnp.einsum(
            "mjt,mtd->mjd",
            place_own,
            jnp.stack([*cotangent_all, cotangent[0]]),
            preferred_element_type=jnp.float32,
        ).astype(jnp.bfloat16)
        return exchange(cut(packed), staying([first_back]), 1)

    cotangent_all = []
    tokens_all = [tokens_in[0]]
    first_grads = None

    chunk = jax.ShapeDtypeStruct((rows, model_dim), jnp.bfloat16)
    rows_shape = jax.ShapeDtypeStruct((tok_rows, model_dim), jnp.bfloat16)
    mark_shape = jax.ShapeDtypeStruct((1,), jnp.int32)
    matrix_shapes = [jax.ShapeDtypeStruct(m.shape, m.dtype) for m in own]
    wide = jax.ShapeDtypeStruct((rows, model_dim + lanes), jnp.bfloat16)
    light = pl.CostEstimate(flops=0, bytes_accessed=0, transcendentals=0)
    state_shapes = [
        jax.ShapeDtypeStruct((slots, model_dim + lanes), jnp.bfloat16),
        jax.ShapeDtypeStruct((slots, 2 * hidden_dim), jnp.float32),
        jax.ShapeDtypeStruct((slots, 2 * hidden_dim), jnp.float32),
        jax.ShapeDtypeStruct((slots, model_dim), jnp.float32),
    ]

    saved = {}
    formers = {}
    former_shape = jax.ShapeDtypeStruct((slots, lanes), jnp.bfloat16)
    ahead = None
    behind = None
    results = None
    for slot in range(slot_count):
        forward_on = [s for s in sections if 0 <= slot - s < micro_count]
        if forward_on:
            has_first = 0 in forward_on
            has_rest = ahead is not None
            loading = slot == 0
            early = first_grads[parts // 2 :][:1] if slot == 2 else []
            outs = pl.pallas_call(
                partial(forward_router, slot, micro_count, parts, has_first, has_rest),
                out_shape=[wide] * parts + [mark_shape] + ([former_shape] if has_rest else []),
                in_specs=[in_smem, in_vmem, in_vmem]
                + [in_vmem] * ((1 if has_first else 0) + (parts if has_rest else 0))
                + [anywhere] * len(early),
                out_specs=[in_vmem] * parts + [in_smem] + ([in_vmem] if has_rest else []),
                compiler_params=params(4),
                cost_estimate=light,
                name=f"route_forward_{slot}",
            )(
                sec,
                route,
                place_wide,
                *([tokens_all[slot]] if has_first else []),
                *(ahead if has_rest else []),
                *early,
            )
            busy = slot > section_count
            moved = exchange(outs[:parts], staying(forward_on if busy else sections), 1)
            mark = outs[parts]
            formers[slot] = outs[parts + 1] if has_rest else None
            if loading:
                own = pl.pallas_call(
                    load_kernel,
                    out_shape=matrix_shapes,
                    in_specs=[in_smem] + [in_hbm] * 3,
                    out_specs=[in_vmem] * 3,
                    scratch_shapes=[pltpu.SemaphoreType.DMA((3,))],
                    compiler_params=params(42),
                    name="load_weights",
                )(mark, *own)
                weights = (*own, *other)
            later = first_grads[1:] if slot == 2 else []
            outs = pl.pallas_call(
                partial(forward_kernel, slot, micro_count, parts, loading, len(later)),
                out_shape=[wide] * parts
                + state_shapes
                + ([rows_shape] + matrix_shapes if loading else []),
                in_specs=[in_smem, in_vmem]
                + [in_vmem] * parts
                + [in_vmem] * 3
                + [in_hbm if loading else in_vmem] * 3
                + [anywhere] * len(later)
                + [in_vmem] * (2 if loading else 0),
                out_specs=[in_vmem] * (parts + 4 + (4 if loading else 0)),
                scratch_shapes=[
                    pltpu.VMEM((slots, model_dim), jnp.bfloat16),
                    pltpu.VMEM((2, slots, hidden_dim), jnp.bfloat16),
                ]
                + ([pltpu.SemaphoreType.DMA((3,))] if loading else []),
                compiler_params=params(28 if loading else 6),
                cost_estimate=light,
                name=f"expert_forward_{slot}",
            )(sec, gain, *moved, *weights, *later, *([tokens_in[0], cotangent[0]] if loading else []))
            x_rows, pre_gate, pre_up, made = outs[parts : parts + 4]
            saved[slot] = (made, x_rows, pre_gate, pre_up)
            more = any(s + 1 < section_count for s in forward_on)
            jobs = onto_next[:-1] if slot < section_count - 2 else onto_next
            ahead = exchange(outs[:parts], jobs, -1) if more else None
            if loading:
                weights = (*own, *outs[parts + 5 :])
                send_inputs(travel(1, outs[parts + 4]))
                first_grads = send_cotangents()
        backward_on = [s for s in sections if 0 <= slot - 2 * first_back + s < micro_count]
        if backward_on:
            if behind is None:
                grads = [part[0] for part in first_grads]
            else:
                first_time = len(backward_on) == 2 and first_back in backward_on
                grads = exchange(behind, onto_former[-1:] if first_time else onto_former, 1)
            states = []
            for s in backward_on:
                states += list(saved[slot - 2 * first_back + 2 * s])
            outs = pl.pallas_call(
                partial(backward_kernel, slot, counts, backward_on, parts),
                out_shape=[wide] * parts,
                in_specs=[in_smem, in_vmem] + [pl.BlockSpec(memory_space=pl.ANY)] * (2 * parts)
                + [in_vmem] * 6
                + [pl.BlockSpec(memory_space=pl.ANY)] * len(states),
                out_specs=[in_vmem] * parts,
                scratch_shapes=[
                    pltpu.VMEM((slots, model_dim), jnp.bfloat16),
                    pltpu.VMEM((slots, model_dim + lanes), jnp.bfloat16),
                    pltpu.VMEM((slots, 2 * hidden_dim), jnp.float32),
                    pltpu.VMEM((slots, 2 * hidden_dim), jnp.float32),
                    pltpu.VMEM((slots, model_dim), jnp.float32),
                    pltpu.VMEM((slots, model_dim), jnp.bfloat16),
                    pltpu.VMEM((slots, model_dim), jnp.float32),
                    pltpu.SemaphoreType.DMA((4,)),
                    pltpu.SemaphoreType.DMA((parts,)),
                ],
                compiler_params=params(8),
                cost_estimate=light,
                name=f"expert_backward_{slot}",
            )(sec, gain, *grads, *first_grads, *weights, *states)
            alone = slot < section_count + 1
            home = exchange(outs, staying(backward_on if alone else sections), -1)
            onward = [s for s in backward_on if s > 0]
            has_former = results is not None
            outs = pl.pallas_call(
                partial(backward_router, slot, counts, parts, has_former, onward),
                out_shape=[
                    jax.ShapeDtypeStruct((micro_count, tok_rows, model_dim), jnp.bfloat16),
                    jax.ShapeDtypeStruct((micro_count, tok_rows, lanes), jnp.float32),
                ]
                + [chunk] * (parts if onward else 0),
                in_specs=[in_smem, in_vmem, in_vmem]
                + [in_vmem] * parts
                + [in_hbm] * (2 if has_former else 0)
                + [in_vmem] * len(onward),
                out_specs=[in_hbm] * 2 + [in_vmem] * (parts if onward else 0),
                scratch_shapes=[
                    pltpu.VMEM((tok_rows, model_dim), jnp.bfloat16),
                    pltpu.VMEM((tok_rows, lanes), jnp.float32),
                    pltpu.SemaphoreType.DMA((2,)),
                ],
                input_output_aliases={3 + parts: 0, 4 + parts: 1} if has_former else {},
                compiler_params=params(4),
                cost_estimate=light,
                name=f"route_backward_{slot}",
            )(
                sec,
                take_own,
                place_wide,
                *home,
                *(results if has_former else []),
                *[formers[slot - 2 * first_back + 2 * s] for s in onward],
            )
            results = outs[:2]
            behind = outs[2:]

    return (results[0][None], results[1][None, :, :, :1])


def solution(mesh):
    return jax.shard_map(
        body,
        mesh=mesh,
        in_specs=(
            P("section", "expert", None),
            P("section", "expert", None),
            P("section", None),
            P("section", "expert", None, None),
            P("section", "expert", None, None),
            P("section", "expert", None, None),
            P("section", None, "expert", None),
            P("section", None, "expert", None),
        ),
        out_specs=(P("section", None, "expert", None), P("section", None, "expert", None)),
        check_vma=False,
    )
```

```python
from functools import partial

import jax
import jax.numpy as jnp
from jax import lax
from jax.experimental import pallas as pl
from jax.experimental.pallas import tpu as pltpu
from jax.sharding import PartitionSpec as P

epsilon = 1e-06
both = ("section", "expert")
last_with_last = (((1,), (1,)), ((), ()))

in_vmem = pl.BlockSpec(memory_space=pltpu.VMEM)
in_smem = pl.BlockSpec(memory_space=pltpu.SMEM)
in_hbm = pl.BlockSpec(memory_space=pltpu.HBM)
anywhere = pl.BlockSpec(memory_space=pl.ANY)
lanes = 128


def spans(total, size):
    size = size if total % size == 0 else total
    return [pl.ds(start, size) for start in range(0, total, size)]


def params(mib):
    return pltpu.CompilerParams(vmem_limit_bytes=mib * 2**20)


def product(left, right):
    return jnp.dot(left, right, preferred_element_type=jnp.float32)


def product_t(left, right):
    return lax.dot_general(left, right, last_with_last, preferred_element_type=jnp.float32)


def coded(column, number=None):
    high = column.astype(jnp.bfloat16).astype(jnp.float32)
    left = column - high
    middle = left.astype(jnp.bfloat16).astype(jnp.float32)
    lane = lax.broadcasted_iota(jnp.int32, (column.shape[0], lanes), 1)
    spread = jnp.where(lane == 1, middle, jnp.where(lane == 2, left - middle, 0.0))
    spread = jnp.where(lane == 0, high, spread)
    if number is not None:
        spread = jnp.where(lane == 3, number, spread)
    return spread.astype(jnp.bfloat16)


def decoded(columns):
    lane = lax.broadcasted_iota(jnp.int32, columns.shape, 1)
    values = jnp.where(lane < 3, columns.astype(jnp.float32), 0.0)
    return jnp.sum(values, axis=-1, keepdims=True)


def numbered(columns):
    lane = lax.broadcasted_iota(jnp.int32, columns.shape, 1)
    values = columns.astype(jnp.float32)
    number = jnp.sum(jnp.where(lane == 3, values, 0.0), axis=-1, keepdims=True)
    return (number == (lane + 1).astype(jnp.float32)).astype(jnp.bfloat16)


def load_kernel(mark_ref, *refs):
    copies = [
        pltpu.make_async_copy(refs[number], refs[3 + number], refs[6].at[number])
        for number in range(3)
    ]
    for copy in copies:
        copy.start()
    for copy in copies:
        copy.wait()


def choose_kernel(steps, after_ref, sec_ref, tokens_ref, cotangent_ref, *out_refs):
    for step, out_ref in zip(steps, out_refs):

        @pl.when(sec_ref[0] == step)
        def _():
            out_ref[...] = tokens_ref[...]

        @pl.when(sec_ref[0] != step)
        def _():
            out_ref[...] = cotangent_ref[...]


def forward_kernel(slot, micro_count, parts, loading, later, *refs):
    sec_ref, gain_ref = refs[:2]
    x_refs = refs[2 : 2 + parts]
    given = refs[2 + parts : 8 + parts]
    rest = refs[8 + parts + later :]
    if loading:
        inputs, rest = rest[:2], rest[2:]
    out_refs = rest[:parts]
    save_x, save_gate, save_up, save_rows = rest[parts : 4 + parts]
    rest = rest[4 + parts :]
    if loading:
        choose_kernel([1], None, sec_ref, *inputs, rest[0])
        rest = rest[1:]
    half_refs = [given[0:3], rest[0:3] if loading else given[3:6]]
    copies = []
    if loading:
        normed, hidden, sems = rest[3:]
        copies = [
            pltpu.make_async_copy(given[3 + number], half_refs[1][number], sems.at[number])
            for number in range(3)
        ]
        for copy in copies:
            copy.start()
    else:
        normed, hidden = rest
    micro = slot - sec_ref[0]
    active = (micro >= 0) & (micro < micro_count)
    width = gain_ref.shape[1]
    hidden_dim = half_refs[0][0].shape[1]
    rows = x_refs[0].shape[0]

    @pl.when(active)
    def _():
        for part in range(parts):
            values = x_refs[part][:, :width].astype(jnp.float32)
            inv_rms = lax.rsqrt(jnp.mean(values * values, axis=-1, keepdims=True) + epsilon)
            here = pl.ds(part * rows, rows)
            normed[here, :] = (values * inv_rms * gain_ref[...]).astype(jnp.bfloat16)
            save_x[here, :] = x_refs[part][...]
            out_refs[part][:, width:] = x_refs[part][:, width:]

    for half in range(2):
        if loading and half == 1:
            copies[0].wait()
            copies[1].wait()

        @pl.when(active)
        def _():
            side = pl.ds(half * hidden_dim, hidden_dim)
            gate_pre = product(normed[...], half_refs[half][0][...])
            up_pre = product(normed[...], half_refs[half][1][...])
            save_gate[:, side] = gate_pre
            save_up[:, side] = up_pre
            hidden[half] = (gate_pre * jax.nn.sigmoid(gate_pre) * up_pre).astype(jnp.bfloat16)

    if loading:
        copies[2].wait()

    @pl.when(active)
    def _():
        route = [decoded(x_refs[part][:, width:]) for part in range(parts)]
        for span in spans(width, 256):
            made = product(hidden[0], half_refs[0][2][:, span])
            made = made + product(hidden[1], half_refs[1][2][:, span])
            save_rows[:, span] = made
            for part in range(parts):
                added = route[part] * made[part * rows : (part + 1) * rows]
                values = x_refs[part][:, span].astype(jnp.float32)
                out_refs[part][:, span] = (values + added).astype(jnp.bfloat16)


def backward_kernel(slot, counts, candidates, parts, index, *refs):
    section_count, micro_count = counts
    sec_ref, gain_ref = refs[:2]
    rest = refs[2:]
    arrived = rest[:parts]
    first = rest[parts : 2 * parts]
    rest = rest[2 * parts :]
    half_refs = [rest[0:3], rest[3:6]]
    rest = rest[6:]
    saved = {}
    for section in candidates:
        saved[section] = rest[:4]
        rest = rest[4:]
    out_refs = rest[:parts]
    (grad_buf, x_buf, pre_gate, pre_up, rows_buf, grad_rows, scaled_buf, state_sems, grad_sems) = rest[parts:]
    sec = sec_ref[0]
    micro = slot - 2 * (section_count - 1) + sec
    width = gain_ref.shape[1]
    hidden_dim = half_refs[0][0].shape[1]
    slots = grad_buf.shape[0]
    rows = slots // parts

    @pl.when((micro >= 0) & (micro < micro_count))
    def _():
        def for_section(section, act):
            @pl.when(sec == section)
            def _():
                for part in range(parts):
                    if section == section_count - 1:
                        source = first[part].at[index]
                    else:
                        source = arrived[part]
                    act(pltpu.make_async_copy(
                        source, grad_buf.at[pl.ds(part * rows, rows), :], grad_sems.at[part]
                    ))
                targets = (rows_buf, x_buf, pre_gate, pre_up)
                for number, target in enumerate(targets):
                    act(pltpu.make_async_copy(
                        saved[section][number], target, state_sems.at[number]
                    ))

        for section in candidates:
            for_section(section, lambda copy: copy.start())
        for section in candidates:
            for_section(section, lambda copy: copy.wait())
        route = decoded(x_buf[:, width:])
        gate_grad = jnp.zeros((slots, 1), jnp.float32)
        square = jnp.zeros((slots, 1), jnp.float32)
        for span in spans(width, 512):
            grad_f = grad_buf[:, span].astype(jnp.float32)
            gate_grad += jnp.sum(grad_f * rows_buf[:, span], axis=-1, keepdims=True)
            grad_rows[:, span] = (route * grad_f).astype(jnp.bfloat16)
            values = x_buf[:, span].astype(jnp.float32)
            square += jnp.sum(values * values, axis=-1, keepdims=True)
        gate_columns = coded(gate_grad)
        for part in range(parts):
            out_refs[part][:, width:] = gate_columns[part * rows : (part + 1) * rows]
        inv_rms = lax.rsqrt(square / width + epsilon)
        grads = []
        for half in range(2):
            side = pl.ds(half * hidden_dim, hidden_dim)
            grad_hidden = product_t(half_refs[half][2][...], grad_rows[...]).T
            gate_pre = pre_gate[:, side]
            sigma = jax.nn.sigmoid(gate_pre)
            grad_gate = grad_hidden * pre_up[:, side] * sigma * (1.0 + gate_pre * (1.0 - sigma))
            grad_up = grad_hidden * gate_pre * sigma
            grads.append((grad_gate.astype(jnp.bfloat16), grad_up.astype(jnp.bfloat16)))
        dotted = jnp.zeros((slots, 1), jnp.float32)
        for span in spans(width, 256):
            total = product_t(half_refs[0][0][span, :], grads[0][0])
            total = total + product_t(half_refs[0][1][span, :], grads[0][1])
            total = total + product_t(half_refs[1][0][span, :], grads[1][0])
            total = total + product_t(half_refs[1][1][span, :], grads[1][1])
            scaled = total.T * gain_ref[:, span]
            scaled_buf[:, span] = scaled
            dotted += jnp.sum(x_buf[:, span].astype(jnp.float32) * scaled, axis=-1, keepdims=True)
        back = inv_rms * inv_rms * inv_rms * (dotted / width)
        for span in spans(width, 512):
            grad_in = (
                grad_buf[:, span].astype(jnp.float32)
                + inv_rms * scaled_buf[:, span]
                - x_buf[:, span].astype(jnp.float32) * back
            ).astype(jnp.bfloat16)
            for part in range(parts):
                out_refs[part][:, span] = grad_in[part * rows : (part + 1) * rows]


def forward_router(slot, micro_count, parts, has_first, has_rest, *refs):
    sec_ref, route_ref, place_ref = refs[:3]
    rest = refs[3:]
    tokens_ref = rest[0] if has_first else None
    rest = rest[1:] if has_first else rest
    arrived = rest[:parts] if has_rest else None
    rest = rest[parts:] if has_rest else rest
    out_refs = rest[:parts]
    sec = sec_ref[0]
    rest[parts][0] = sec
    micro = slot - sec
    width = out_refs[0].shape[1] - lanes
    rows = out_refs[0].shape[0]

    def put(number, table, source):
        place = place_ref[number].astype(jnp.float32)
        lane = lax.broadcasted_iota(jnp.int32, place.shape, 1)
        token = jnp.sum(place * (lane + 1).astype(jnp.float32), axis=-1, keepdims=True)
        columns = coded(route_ref[number], token)
        for part in range(parts):
            out_refs[part][:, width:] = columns[part * rows : (part + 1) * rows]
        for span in spans(width, 512):
            made = product(table, source(span)).astype(jnp.bfloat16)
            for part in range(parts):
                out_refs[part][:, span] = made[part * rows : (part + 1) * rows]

    if has_first:

        @pl.when(sec == 0)
        def _():
            table = place_ref[slot][:, : tokens_ref.shape[0]]
            put(slot, table, lambda span: tokens_ref[:, span])

    if has_rest:

        @pl.when((sec > 0) & (micro >= 0) & (micro < micro_count))
        def _():
            def source(span):
                return jnp.concatenate([ref[:, span] for ref in arrived], axis=0)

            former = numbered(source(pl.ds(width, lanes)))
            rest[parts + 1][...] = former
            put(micro, product_t(place_ref[micro], former).astype(jnp.bfloat16), source)


def backward_router(slot, counts, parts, has_former, onward, *refs):
    section_count, micro_count = counts
    sec_ref, take_ref, place_ref = refs[:3]
    arrived = refs[3 : 3 + parts]
    rest = refs[3 + parts + (2 if has_former else 0) :]
    formers, rest = rest[: len(onward)], rest[len(onward) :]
    result, gates = rest[:2]
    out_refs = rest[2 : 2 + parts] if onward else []
    ordered, gate_rows, sems = rest[2 + len(out_refs) :]
    sec = sec_ref[0]
    micro = slot - 2 * (section_count - 1) + sec
    width = arrived[0].shape[1] - lanes
    rows = arrived[0].shape[0]

    @pl.when((micro >= 0) & (micro < micro_count))
    def _():
        def source(span):
            return jnp.concatenate([ref[:, span] for ref in arrived], axis=0)

        for section, former in zip(onward, formers):

            @pl.when(sec == section)
            def _():
                table = product_t(former[...], place_ref[micro]).astype(jnp.bfloat16)
                for span in spans(width, 512):
                    made = product(table, source(span)).astype(jnp.bfloat16)
                    for part in range(parts):
                        out_refs[part][:, span] = made[part * rows : (part + 1) * rows]

        for span in spans(width, 512):
            ordered[:, span] = product(take_ref[micro], source(span)).astype(jnp.bfloat16)
        copy = pltpu.make_async_copy(ordered, result.at[micro], sems.at[0])
        copy.start()
        columns = decoded(product(take_ref[micro], source(pl.ds(width, lanes))))
        gate_rows[...] = jnp.broadcast_to(columns, gate_rows.shape)
        gate_copy = pltpu.make_async_copy(gate_rows, gates.at[micro], sems.at[1])
        gate_copy.start()
        copy.wait()
        gate_copy.wait()


def slots_of(route_ids, expert_count, capacity, turn):
    count = route_ids.shape[1]
    before = jnp.arange(count)[None, :] < jnp.arange(count)[:, None]
    alike = (route_ids[:, None, :] == route_ids[:, :, None]) & before
    position = jnp.sum(alike.astype(jnp.int32), axis=-1)
    return lax.rem(route_ids - turn + expert_count, expert_count) * capacity + position


def body(tokens_in, cotangent, norm_gain, w_gate, w_up, w_down, expert_ids, gate_weights):
    section_count = lax.axis_size("section")
    device_count = lax.axis_size("expert")
    section = lax.axis_index("section")
    place = lax.axis_index("expert") // 2
    expert_count = device_count // 2
    micro_count = expert_ids.shape[1]
    tok_rows = expert_ids.shape[2]
    model_dim = tokens_in.shape[2]
    hidden_dim = w_gate.shape[3]
    capacity = 2 * ((tok_rows + expert_count - 1) // expert_count)
    slots = expert_count * capacity
    by_permute = capacity % 16 == 0
    parts = expert_count if by_permute else 1
    rows = slots // parts
    turn = place if by_permute else jnp.int32(0)
    counts = (section_count, micro_count)
    first_back = section_count - 1
    slot_count = micro_count + 2 * (section_count - 1)
    sections = list(range(section_count))

    def exchange(chunks, jobs, direction):
        if by_permute:
            moved = [None] * parts
            for step in sorted(range(parts), key=lambda k: -min(k, parts - k)):
                if step == 0 and all(a == b for a, b in jobs):
                    moved[0] = chunks[0]
                    continue
                pairs = [
                    (
                        a * device_count + 2 * z + core,
                        b * device_count + 2 * ((z + direction * step) % expert_count) + core,
                    )
                    for a, b in jobs
                    for z in range(expert_count)
                    for core in range(2)
                ]
                moved[step] = lax.ppermute(chunks[step], both, sorted(pairs))
            return moved
        (block,) = chunks
        shape = block.shape
        spread = block.reshape(-1, expert_count, capacity, shape[-1])
        groups = [[2 * z + core for z in range(expert_count)] for core in range(2)]
        spread = lax.all_to_all(
            spread, "expert", split_axis=1, concat_axis=1, tiled=True, axis_index_groups=groups
        )
        block = spread.reshape(shape)
        if any(a != b for a, b in jobs):
            block = lax.ppermute(block, "section", jobs)
        return [block]

    def cut(block):
        return [block[:, part * rows : (part + 1) * rows] for part in range(parts)]

    own = (w_gate[0, 0], w_up[0, 0], w_down[0, 0])
    swap = [(i, i ^ 1) for i in range(device_count)]
    other = [lax.ppermute(matrix, "expert", swap) for matrix in own]

    sec = section.reshape(1).astype(jnp.int32)
    gain = norm_gain
    ids = expert_ids[0, :, :, 0]
    onto_next = [(s, s + 1) for s in sections[:-1]]
    onto_former = [(s + 1, s) for s in sections[:-1]]
    numbers = jnp.arange(slots, dtype=jnp.int32)

    slot_own = slots_of(ids, expert_count, capacity, turn)
    padded = jnp.pad(slot_own, ((0, 0), (0, lanes - tok_rows)), constant_values=-1)
    place_wide = (numbers[None, :, None] == padded[:, None, :]).astype(jnp.bfloat16)
    is_own = numbers[None, :, None] == slot_own[:, None, :]
    place_own = is_own.astype(jnp.bfloat16)
    take_own = place_own.transpose(0, 2, 1)

    def staying(members):
        return [(s, s) for s in members]

    route_slots = jnp.sum(jnp.where(is_own, gate_weights[0, :, None, :, 0], 0.0), axis=-1)
    route = route_slots[:, :, None]

    def send_inputs(after):
        steps = list(range(2, section_count))
        sent = pl.pallas_call(
            partial(choose_kernel, steps),
            out_shape=[rows_shape] * len(steps),
            in_specs=[anywhere, in_smem] + [in_vmem] * 2,
            out_specs=[in_vmem] * len(steps),
            compiler_params=params(4),
            cost_estimate=light,
            name="choose_inputs",
        )(after, sec, tokens_in[0], cotangent[0])
        for step, rows_sent in zip(steps, sent):
            travel(step, rows_sent)

    def travel(step, rows_sent):
        came = lax.ppermute(rows_sent, "section", [(step, 0), (step - 1, section_count - 1)])
        tokens_all.append(came)
        cotangent_all[step - 1] = came
        return came

    def send_cotangents(micros):
        packed = jnp.einsum(
            "mjt,mtd->mjd",
            jnp.stack([place_own[m] for m in micros]),
            jnp.stack([cotangent_all[m] for m in micros]),
            preferred_element_type=jnp.float32,
        ).astype(jnp.bfloat16)
        spread = exchange(cut(packed), staying([first_back]), 1)
        for index, m in enumerate(micros):
            first_grads[m] = (spread, index)
        return spread

    cotangent_all = {section_count - 1: cotangent[0]}
    tokens_all = [tokens_in[0]]
    first_grads = {}
    ends = middle = []

    chunk = jax.ShapeDtypeStruct((rows, model_dim), jnp.bfloat16)
    rows_shape = jax.ShapeDtypeStruct((tok_rows, model_dim), jnp.bfloat16)
    mark_shape = jax.ShapeDtypeStruct((1,), jnp.int32)
    matrix_shapes = [jax.ShapeDtypeStruct(m.shape, m.dtype) for m in own]
    wide = jax.ShapeDtypeStruct((rows, model_dim + lanes), jnp.bfloat16)
    light = pl.CostEstimate(flops=0, bytes_accessed=0, transcendentals=0)
    state_shapes = [
        jax.ShapeDtypeStruct((slots, model_dim + lanes), jnp.bfloat16),
        jax.ShapeDtypeStruct((slots, 2 * hidden_dim), jnp.float32),
        jax.ShapeDtypeStruct((slots, 2 * hidden_dim), jnp.float32),
        jax.ShapeDtypeStruct((slots, model_dim), jnp.float32),
    ]

    saved = {}
    formers = {}
    former_shape = jax.ShapeDtypeStruct((slots, lanes), jnp.bfloat16)
    ahead = None
    behind = None
    results = None
    for slot in range(slot_count):
        forward_on = [s for s in sections if 0 <= slot - s < micro_count]
        if forward_on:
            has_first = 0 in forward_on
            has_rest = ahead is not None
            loading = slot == 0
            outs = pl.pallas_call(
                partial(forward_router, slot, micro_count, parts, has_first, has_rest),
                out_shape=[wide] * parts + [mark_shape] + ([former_shape] if has_rest else []),
                in_specs=[in_smem, in_vmem, in_vmem]
                + [in_vmem] * ((1 if has_first else 0) + (parts if has_rest else 0)),
                out_specs=[in_vmem] * parts + [in_smem] + ([in_vmem] if has_rest else []),
                compiler_params=params(4),
                cost_estimate=light,
                name=f"route_forward_{slot}",
            )(
                sec,
                route,
                place_wide,
                *([tokens_all[slot]] if has_first else []),
                *(ahead if has_rest else []),
            )
            busy = slot > section_count
            moved = exchange(outs[:parts], staying(forward_on if busy else sections), 1)
            mark = outs[parts]
            formers[slot] = outs[parts + 1] if has_rest else None
            if loading:
                own = pl.pallas_call(
                    load_kernel,
                    out_shape=matrix_shapes,
                    in_specs=[in_smem] + [in_hbm] * 3,
                    out_specs=[in_vmem] * 3,
                    scratch_shapes=[pltpu.SemaphoreType.DMA((3,))],
                    compiler_params=params(42),
                    name="load_weights",
                )(mark, *own)
                weights = (*own, *other)
            later = {1: ends, 2: middle}.get(slot, [])
            outs = pl.pallas_call(
                partial(forward_kernel, slot, micro_count, parts, loading, len(later)),
                out_shape=[wide] * parts
                + state_shapes
                + ([rows_shape] + matrix_shapes if loading else []),
                in_specs=[in_smem, in_vmem]
                + [in_vmem] * parts
                + [in_vmem] * 3
                + [in_hbm if loading else in_vmem] * 3
                + [anywhere] * len(later)
                + [in_vmem] * (2 if loading else 0),
                out_specs=[in_vmem] * (parts + 4 + (4 if loading else 0)),
                scratch_shapes=[
                    pltpu.VMEM((slots, model_dim), jnp.bfloat16),
                    pltpu.VMEM((2, slots, hidden_dim), jnp.bfloat16),
                ]
                + ([pltpu.SemaphoreType.DMA((3,))] if loading else []),
                compiler_params=params(28 if loading else 6),
                cost_estimate=light,
                name=f"expert_forward_{slot}",
            )(sec, gain, *moved, *weights, *later, *([tokens_in[0], cotangent[0]] if loading else []))
            x_rows, pre_gate, pre_up, made = outs[parts : parts + 4]
            saved[slot] = (made, x_rows, pre_gate, pre_up)
            more = any(s + 1 < section_count for s in forward_on)
            jobs = onto_next[:-1] if slot < section_count - 2 else onto_next
            ahead = exchange(outs[:parts], jobs, -1) if more else None
            if loading:
                weights = (*own, *outs[parts + 5 :])
                came = travel(1, outs[parts + 4])
                ends = send_cotangents([0, section_count - 1])
                send_inputs(came)
                middle = send_cotangents(list(range(1, section_count - 1)))
        backward_on = [s for s in sections if 0 <= slot - 2 * first_back + s < micro_count]
        if backward_on:
            first, index = first_grads.get(slot - first_back, (behind, 0))
            if behind is None:
                grads = first
            else:
                first_time = len(backward_on) == 2 and first_back in backward_on
                grads = exchange(behind, onto_former[-1:] if first_time else onto_former, 1)
            states = []
            for s in backward_on:
                states += list(saved[slot - 2 * first_back + 2 * s])
            outs = pl.pallas_call(
                partial(backward_kernel, slot, counts, backward_on, parts, index),
                out_shape=[wide] * parts,
                in_specs=[in_smem, in_vmem] + [pl.BlockSpec(memory_space=pl.ANY)] * (2 * parts)
                + [in_vmem] * 6
                + [pl.BlockSpec(memory_space=pl.ANY)] * len(states),
                out_specs=[in_vmem] * parts,
                scratch_shapes=[
                    pltpu.VMEM((slots, model_dim), jnp.bfloat16),
                    pltpu.VMEM((slots, model_dim + lanes), jnp.bfloat16),
                    pltpu.VMEM((slots, 2 * hidden_dim), jnp.float32),
                    pltpu.VMEM((slots, 2 * hidden_dim), jnp.float32),
                    pltpu.VMEM((slots, model_dim), jnp.float32),
                    pltpu.VMEM((slots, model_dim), jnp.bfloat16),
                    pltpu.VMEM((slots, model_dim), jnp.float32),
                    pltpu.SemaphoreType.DMA((4,)),
                    pltpu.SemaphoreType.DMA((parts,)),
                ],
                compiler_params=params(8),
                cost_estimate=light,
                name=f"expert_backward_{slot}",
            )(sec, gain, *grads, *first, *weights, *states)
            alone = slot < section_count + 1
            home = exchange(outs, staying(backward_on if alone else sections), -1)
            onward = [s for s in backward_on if s > 0]
            has_former = results is not None
            outs = pl.pallas_call(
                partial(backward_router, slot, counts, parts, has_former, onward),
                out_shape=[
                    jax.ShapeDtypeStruct((micro_count, tok_rows, model_dim), jnp.bfloat16),
                    jax.ShapeDtypeStruct((micro_count, tok_rows, lanes), jnp.float32),
                ]
                + [chunk] * (parts if onward else 0),
                in_specs=[in_smem, in_vmem, in_vmem]
                + [in_vmem] * parts
                + [in_hbm] * (2 if has_former else 0)
                + [in_vmem] * len(onward),
                out_specs=[in_hbm] * 2 + [in_vmem] * (parts if onward else 0),
                scratch_shapes=[
                    pltpu.VMEM((tok_rows, model_dim), jnp.bfloat16),
                    pltpu.VMEM((tok_rows, lanes), jnp.float32),
                    pltpu.SemaphoreType.DMA((2,)),
                ],
                input_output_aliases={3 + parts: 0, 4 + parts: 1} if has_former else {},
                compiler_params=params(4),
                cost_estimate=light,
                name=f"route_backward_{slot}",
            )(
                sec,
                take_own,
                place_wide,
                *home,
                *(results if has_former else []),
                *[formers[slot - 2 * first_back + 2 * s] for s in onward],
            )
            results = outs[:2]
            behind = outs[2:]

    return (results[0][None], results[1][None, :, :, :1])


def solution(mesh):
    return jax.shard_map(
        body,
        mesh=mesh,
        in_specs=(
            P("section", "expert", None),
            P("section", "expert", None),
            P("section", None),
            P("section", "expert", None, None),
            P("section", "expert", None, None),
            P("section", "expert", None, None),
            P("section", None, "expert", None),
            P("section", None, "expert", None),
        ),
        out_specs=(P("section", None, "expert", None), P("section", None, "expert", None)),
        check_vma=False,
    )
```

```python
from functools import partial

import jax
import jax.numpy as jnp
from jax import lax
from jax.experimental import pallas as pl
from jax.experimental.pallas import tpu as pltpu
from jax.sharding import PartitionSpec as P

epsilon = 1e-06
both = ("section", "expert")
last_with_last = (((1,), (1,)), ((), ()))

in_vmem = pl.BlockSpec(memory_space=pltpu.VMEM)
in_smem = pl.BlockSpec(memory_space=pltpu.SMEM)
in_hbm = pl.BlockSpec(memory_space=pltpu.HBM)
anywhere = pl.BlockSpec(memory_space=pl.ANY)
lanes = 128


def spans(total, size):
    size = size if total % size == 0 else total
    return [pl.ds(start, size) for start in range(0, total, size)]


def params(mib):
    return pltpu.CompilerParams(vmem_limit_bytes=mib * 2**20)


def product(left, right):
    return jnp.dot(left, right, preferred_element_type=jnp.float32)


def product_t(left, right):
    return lax.dot_general(left, right, last_with_last, preferred_element_type=jnp.float32)


def coded(column, number=None):
    high = column.astype(jnp.bfloat16).astype(jnp.float32)
    left = column - high
    middle = left.astype(jnp.bfloat16).astype(jnp.float32)
    lane = lax.broadcasted_iota(jnp.int32, (column.shape[0], lanes), 1)
    spread = jnp.where(lane == 1, middle, jnp.where(lane == 2, left - middle, 0.0))
    spread = jnp.where(lane == 0, high, spread)
    if number is not None:
        spread = jnp.where(lane == 3, number, spread)
    return spread.astype(jnp.bfloat16)


def decoded(columns):
    lane = lax.broadcasted_iota(jnp.int32, columns.shape, 1)
    values = jnp.where(lane < 3, columns.astype(jnp.float32), 0.0)
    return jnp.sum(values, axis=-1, keepdims=True)


def numbered(columns):
    lane = lax.broadcasted_iota(jnp.int32, columns.shape, 1)
    values = columns.astype(jnp.float32)
    number = jnp.sum(jnp.where(lane == 3, values, 0.0), axis=-1, keepdims=True)
    return (number == (lane + 1).astype(jnp.float32)).astype(jnp.bfloat16)


def load_kernel(mark_ref, *refs):
    copies = [
        pltpu.make_async_copy(refs[number], refs[3 + number], refs[6].at[number])
        for number in range(3)
    ]
    for copy in copies:
        copy.start()
    for copy in copies:
        copy.wait()


def choose_kernel(steps, after_ref, sec_ref, tokens_ref, cotangent_ref, *out_refs):
    for step, out_ref in zip(steps, out_refs):

        @pl.when(sec_ref[0] == step)
        def _():
            out_ref[...] = tokens_ref[...]

        @pl.when(sec_ref[0] != step)
        def _():
            out_ref[...] = cotangent_ref[...]


def forward_kernel(slot, micro_count, parts, loading, later, last, closing, *refs):
    sec_ref, gain_ref = refs[:2]
    x_refs = refs[2 : 2 + parts]
    given = refs[2 + parts : 8 + parts]
    rest = refs[8 + parts + later :]
    if loading:
        inputs, rest = rest[:2], rest[2:]
    out_refs = [] if closing else rest[:parts]
    save_x, save_gate, save_up, save_rows = rest[len(out_refs) : 4 + len(out_refs)]
    rest = rest[4 + len(out_refs) :]
    if loading:
        choose_kernel([1], None, sec_ref, *inputs, rest[0])
        rest = rest[1:]
    half_refs = [given[0:3], rest[0:3] if loading else given[3:6]]
    copies = []
    if loading:
        normed, hidden, sems = rest[3:]
        copies = [
            pltpu.make_async_copy(given[3 + number], half_refs[1][number], sems.at[number])
            for number in range(3)
        ]
        for copy in copies:
            copy.start()
    else:
        normed, hidden = rest
    micro = slot - sec_ref[0]
    mine = sec_ref[0] == last if closing else sec_ref[0] < last
    active = (micro >= 0) & (micro < micro_count) & mine
    width = gain_ref.shape[1]
    hidden_dim = half_refs[0][0].shape[1]
    rows = x_refs[0].shape[0]

    @pl.when(active)
    def _():
        for part in range(parts):
            values = x_refs[part][:, :width].astype(jnp.float32)
            inv_rms = lax.rsqrt(jnp.mean(values * values, axis=-1, keepdims=True) + epsilon)
            here = pl.ds(part * rows, rows)
            normed[here, :] = (values * inv_rms * gain_ref[...]).astype(jnp.bfloat16)
            save_x[here, :] = x_refs[part][...]
            if out_refs:
                out_refs[part][:, width:] = x_refs[part][:, width:]

    for half in range(2):
        if loading and half == 1:
            copies[0].wait()
            copies[1].wait()

        @pl.when(active)
        def _():
            side = pl.ds(half * hidden_dim, hidden_dim)
            gate_pre = product(normed[...], half_refs[half][0][...])
            up_pre = product(normed[...], half_refs[half][1][...])
            save_gate[:, side] = gate_pre
            save_up[:, side] = up_pre
            hidden[half] = (gate_pre * jax.nn.sigmoid(gate_pre) * up_pre).astype(jnp.bfloat16)

    if loading:
        copies[2].wait()

    @pl.when(active)
    def _():
        route = [decoded(x_refs[part][:, width:]) for part in range(parts)]
        for span in spans(width, 256):
            made = product(hidden[0], half_refs[0][2][:, span])
            made = made + product(hidden[1], half_refs[1][2][:, span])
            save_rows[:, span] = made
            for part in range(len(out_refs)):
                added = route[part] * made[part * rows : (part + 1) * rows]
                values = x_refs[part][:, span].astype(jnp.float32)
                out_refs[part][:, span] = (values + added).astype(jnp.bfloat16)


def backward_kernel(slot, counts, candidates, parts, index, *refs):
    section_count, micro_count = counts
    sec_ref, gain_ref = refs[:2]
    rest = refs[2:]
    arrived = rest[:parts]
    first = rest[parts : 2 * parts]
    rest = rest[2 * parts :]
    half_refs = [rest[0:3], rest[3:6]]
    rest = rest[6:]
    saved = {}
    for section in candidates:
        saved[section] = rest[:4]
        rest = rest[4:]
    out_refs = rest[:parts]
    (grad_buf, x_buf, pre_gate, pre_up, rows_buf, grad_rows, scaled_buf, state_sems, grad_sems) = rest[parts:]
    sec = sec_ref[0]
    micro = slot - 2 * (section_count - 1) + sec
    width = gain_ref.shape[1]
    hidden_dim = half_refs[0][0].shape[1]
    slots = grad_buf.shape[0]
    rows = slots // parts

    @pl.when((micro >= 0) & (micro < micro_count))
    def _():
        def for_section(section, act):
            @pl.when(sec == section)
            def _():
                for part in range(parts):
                    if section == section_count - 1:
                        source = first[part].at[index]
                    else:
                        source = arrived[part]
                    act(pltpu.make_async_copy(
                        source, grad_buf.at[pl.ds(part * rows, rows), :], grad_sems.at[part]
                    ))
                targets = (rows_buf, x_buf, pre_gate, pre_up)
                for number, target in enumerate(targets):
                    act(pltpu.make_async_copy(
                        saved[section][number], target, state_sems.at[number]
                    ))

        for section in candidates:
            for_section(section, lambda copy: copy.start())
        for section in candidates:
            for_section(section, lambda copy: copy.wait())
        route = decoded(x_buf[:, width:])
        gate_grad = jnp.zeros((slots, 1), jnp.float32)
        square = jnp.zeros((slots, 1), jnp.float32)
        for span in spans(width, 512):
            grad_f = grad_buf[:, span].astype(jnp.float32)
            gate_grad += jnp.sum(grad_f * rows_buf[:, span], axis=-1, keepdims=True)
            grad_rows[:, span] = (route * grad_f).astype(jnp.bfloat16)
            values = x_buf[:, span].astype(jnp.float32)
            square += jnp.sum(values * values, axis=-1, keepdims=True)
        gate_columns = coded(gate_grad)
        for part in range(parts):
            out_refs[part][:, width:] = gate_columns[part * rows : (part + 1) * rows]
        inv_rms = lax.rsqrt(square / width + epsilon)
        grads = []
        for half in range(2):
            side = pl.ds(half * hidden_dim, hidden_dim)
            grad_hidden = product_t(half_refs[half][2][...], grad_rows[...]).T
            gate_pre = pre_gate[:, side]
            sigma = jax.nn.sigmoid(gate_pre)
            grad_gate = grad_hidden * pre_up[:, side] * sigma * (1.0 + gate_pre * (1.0 - sigma))
            grad_up = grad_hidden * gate_pre * sigma
            grads.append((grad_gate.astype(jnp.bfloat16), grad_up.astype(jnp.bfloat16)))
        dotted = jnp.zeros((slots, 1), jnp.float32)
        for span in spans(width, 256):
            total = product_t(half_refs[0][0][span, :], grads[0][0])
            total = total + product_t(half_refs[0][1][span, :], grads[0][1])
            total = total + product_t(half_refs[1][0][span, :], grads[1][0])
            total = total + product_t(half_refs[1][1][span, :], grads[1][1])
            scaled = total.T * gain_ref[:, span]
            scaled_buf[:, span] = scaled
            dotted += jnp.sum(x_buf[:, span].astype(jnp.float32) * scaled, axis=-1, keepdims=True)
        back = inv_rms * inv_rms * inv_rms * (dotted / width)
        for span in spans(width, 512):
            grad_in = (
                grad_buf[:, span].astype(jnp.float32)
                + inv_rms * scaled_buf[:, span]
                - x_buf[:, span].astype(jnp.float32) * back
            ).astype(jnp.bfloat16)
            for part in range(parts):
                out_refs[part][:, span] = grad_in[part * rows : (part + 1) * rows]


def forward_router(slot, micro_count, parts, has_first, has_rest, *refs):
    sec_ref, route_ref, place_ref = refs[:3]
    rest = refs[3:]
    tokens_ref = rest[0] if has_first else None
    rest = rest[1:] if has_first else rest
    arrived = rest[:parts] if has_rest else None
    rest = rest[parts:] if has_rest else rest
    out_refs = rest[:parts]
    sec = sec_ref[0]
    rest[parts][0] = sec
    micro = slot - sec
    width = out_refs[0].shape[1] - lanes
    rows = out_refs[0].shape[0]

    def put(number, table, source):
        place = place_ref[number].astype(jnp.float32)
        lane = lax.broadcasted_iota(jnp.int32, place.shape, 1)
        token = jnp.sum(place * (lane + 1).astype(jnp.float32), axis=-1, keepdims=True)
        columns = coded(route_ref[number], token)
        for part in range(parts):
            out_refs[part][:, width:] = columns[part * rows : (part + 1) * rows]
        for span in spans(width, 512):
            made = product(table, source(span)).astype(jnp.bfloat16)
            for part in range(parts):
                out_refs[part][:, span] = made[part * rows : (part + 1) * rows]

    if has_first:

        @pl.when(sec == 0)
        def _():
            table = place_ref[slot][:, : tokens_ref.shape[0]]
            put(slot, table, lambda span: tokens_ref[:, span])

    if has_rest:

        @pl.when((sec > 0) & (micro >= 0) & (micro < micro_count))
        def _():
            def source(span):
                return jnp.concatenate([ref[:, span] for ref in arrived], axis=0)

            former = numbered(source(pl.ds(width, lanes)))
            rest[parts + 1][...] = former
            put(micro, product_t(place_ref[micro], former).astype(jnp.bfloat16), source)


def backward_router(slot, counts, parts, has_former, onward, *refs):
    section_count, micro_count = counts
    sec_ref, take_ref, place_ref = refs[:3]
    arrived = refs[3 : 3 + parts]
    rest = refs[3 + parts + (2 if has_former else 0) :]
    formers, rest = rest[: len(onward)], rest[len(onward) :]
    result, gates = rest[:2]
    out_refs = rest[2 : 2 + parts] if onward else []
    ordered, gate_rows, sems = rest[2 + len(out_refs) :]
    sec = sec_ref[0]
    micro = slot - 2 * (section_count - 1) + sec
    width = arrived[0].shape[1] - lanes
    rows = arrived[0].shape[0]

    @pl.when((micro >= 0) & (micro < micro_count))
    def _():
        def source(span):
            return jnp.concatenate([ref[:, span] for ref in arrived], axis=0)

        for section, former in zip(onward, formers):

            @pl.when(sec == section)
            def _():
                table = product_t(former[...], place_ref[micro]).astype(jnp.bfloat16)
                for span in spans(width, 512):
                    made = product(table, source(span)).astype(jnp.bfloat16)
                    for part in range(parts):
                        out_refs[part][:, span] = made[part * rows : (part + 1) * rows]

        for span in spans(width, 512):
            ordered[:, span] = product(take_ref[micro], source(span)).astype(jnp.bfloat16)
        copy = pltpu.make_async_copy(ordered, result.at[micro], sems.at[0])
        copy.start()
        columns = decoded(product(take_ref[micro], source(pl.ds(width, lanes))))
        gate_rows[...] = jnp.broadcast_to(columns, gate_rows.shape)
        gate_copy = pltpu.make_async_copy(gate_rows, gates.at[micro], sems.at[1])
        gate_copy.start()
        copy.wait()
        gate_copy.wait()


def slots_of(route_ids, expert_count, capacity, turn):
    count = route_ids.shape[1]
    before = jnp.arange(count)[None, :] < jnp.arange(count)[:, None]
    alike = (route_ids[:, None, :] == route_ids[:, :, None]) & before
    position = jnp.sum(alike.astype(jnp.int32), axis=-1)
    return lax.rem(route_ids - turn + expert_count, expert_count) * capacity + position


def body(tokens_in, cotangent, norm_gain, w_gate, w_up, w_down, expert_ids, gate_weights):
    section_count = lax.axis_size("section")
    device_count = lax.axis_size("expert")
    section = lax.axis_index("section")
    place = lax.axis_index("expert") // 2
    expert_count = device_count // 2
    micro_count = expert_ids.shape[1]
    tok_rows = expert_ids.shape[2]
    model_dim = tokens_in.shape[2]
    hidden_dim = w_gate.shape[3]
    capacity = 2 * ((tok_rows + expert_count - 1) // expert_count)
    slots = expert_count * capacity
    by_permute = capacity % 16 == 0
    parts = expert_count if by_permute else 1
    rows = slots // parts
    turn = place if by_permute else jnp.int32(0)
    counts = (section_count, micro_count)
    first_back = section_count - 1
    slot_count = micro_count + 2 * (section_count - 1)
    sections = list(range(section_count))

    def exchange(chunks, jobs, direction):
        if by_permute:
            moved = [None] * parts
            for step in sorted(range(parts), key=lambda k: -min(k, parts - k)):
                if step == 0 and all(a == b for a, b in jobs):
                    moved[0] = chunks[0]
                    continue
                pairs = [
                    (
                        a * device_count + 2 * z + core,
                        b * device_count + 2 * ((z + direction * step) % expert_count) + core,
                    )
                    for a, b in jobs
                    for z in range(expert_count)
                    for core in range(2)
                ]
                moved[step] = lax.ppermute(chunks[step], both, sorted(pairs))
            return moved
        (block,) = chunks
        shape = block.shape
        spread = block.reshape(-1, expert_count, capacity, shape[-1])
        groups = [[2 * z + core for z in range(expert_count)] for core in range(2)]
        spread = lax.all_to_all(
            spread, "expert", split_axis=1, concat_axis=1, tiled=True, axis_index_groups=groups
        )
        block = spread.reshape(shape)
        if any(a != b for a, b in jobs):
            block = lax.ppermute(block, "section", jobs)
        return [block]

    def cut(block):
        return [block[:, part * rows : (part + 1) * rows] for part in range(parts)]

    own = (w_gate[0, 0], w_up[0, 0], w_down[0, 0])
    swap = [(i, i ^ 1) for i in range(device_count)]
    other = [lax.ppermute(matrix, "expert", swap) for matrix in own]

    sec = section.reshape(1).astype(jnp.int32)
    gain = norm_gain
    ids = expert_ids[0, :, :, 0]
    onto_next = [(s, s + 1) for s in sections[:-1]]
    onto_former = [(s + 1, s) for s in sections[:-1]]
    numbers = jnp.arange(slots, dtype=jnp.int32)

    slot_own = slots_of(ids, expert_count, capacity, turn)
    padded = jnp.pad(slot_own, ((0, 0), (0, lanes - tok_rows)), constant_values=-1)
    place_wide = (numbers[None, :, None] == padded[:, None, :]).astype(jnp.bfloat16)
    is_own = numbers[None, :, None] == slot_own[:, None, :]
    place_own = is_own.astype(jnp.bfloat16)
    take_own = place_own.transpose(0, 2, 1)

    def staying(members):
        return [(s, s) for s in members]

    route_slots = jnp.sum(jnp.where(is_own, gate_weights[0, :, None, :, 0], 0.0), axis=-1)
    route = route_slots[:, :, None]

    def send_inputs(after):
        steps = list(range(2, section_count))
        sent = pl.pallas_call(
            partial(choose_kernel, steps),
            out_shape=[rows_shape] * len(steps),
            in_specs=[anywhere, in_smem] + [in_vmem] * 2,
            out_specs=[in_vmem] * len(steps),
            compiler_params=params(4),
            cost_estimate=light,
            name="choose_inputs",
        )(after, sec, tokens_in[0], cotangent[0])
        for step, rows_sent in zip(steps, sent):
            travel(step, rows_sent)

    def travel(step, rows_sent):
        came = lax.ppermute(rows_sent, "section", [(step, 0), (step - 1, section_count - 1)])
        tokens_all.append(came)
        cotangent_all[step - 1] = came
        return came

    def send_cotangents(micros):
        packed = jnp.einsum(
            "mjt,mtd->mjd",
            jnp.stack([place_own[m] for m in micros]),
            jnp.stack([cotangent_all[m] for m in micros]),
            preferred_element_type=jnp.float32,
        ).astype(jnp.bfloat16)
        spread = exchange(cut(packed), staying([first_back]), 1)
        for index, m in enumerate(micros):
            first_grads[m] = (spread, index)
        return spread

    cotangent_all = {section_count - 1: cotangent[0]}
    tokens_all = [tokens_in[0]]
    first_grads = {}
    ends = middle = []

    chunk = jax.ShapeDtypeStruct((rows, model_dim), jnp.bfloat16)
    rows_shape = jax.ShapeDtypeStruct((tok_rows, model_dim), jnp.bfloat16)
    mark_shape = jax.ShapeDtypeStruct((1,), jnp.int32)
    matrix_shapes = [jax.ShapeDtypeStruct(m.shape, m.dtype) for m in own]
    wide = jax.ShapeDtypeStruct((rows, model_dim + lanes), jnp.bfloat16)
    light = pl.CostEstimate(flops=0, bytes_accessed=0, transcendentals=0)
    state_shapes = [
        jax.ShapeDtypeStruct((slots, model_dim + lanes), jnp.bfloat16),
        jax.ShapeDtypeStruct((slots, 2 * hidden_dim), jnp.float32),
        jax.ShapeDtypeStruct((slots, 2 * hidden_dim), jnp.float32),
        jax.ShapeDtypeStruct((slots, model_dim), jnp.float32),
    ]

    saved = {}
    formers = {}
    former_shape = jax.ShapeDtypeStruct((slots, lanes), jnp.bfloat16)
    ahead = None
    behind = None
    results = None
    for slot in range(slot_count):
        forward_on = [s for s in sections if 0 <= slot - s < micro_count]
        if forward_on:
            has_first = 0 in forward_on
            has_rest = ahead is not None
            loading = slot == 0
            outs = pl.pallas_call(
                partial(forward_router, slot, micro_count, parts, has_first, has_rest),
                out_shape=[wide] * parts + [mark_shape] + ([former_shape] if has_rest else []),
                in_specs=[in_smem, in_vmem, in_vmem]
                + [in_vmem] * ((1 if has_first else 0) + (parts if has_rest else 0)),
                out_specs=[in_vmem] * parts + [in_smem] + ([in_vmem] if has_rest else []),
                compiler_params=params(4),
                cost_estimate=light,
                name=f"route_forward_{slot}",
            )(
                sec,
                route,
                place_wide,
                *([tokens_all[slot]] if has_first else []),
                *(ahead if has_rest else []),
            )
            busy = slot > section_count
            moved = exchange(outs[:parts], staying(forward_on if busy else sections), 1)
            mark = outs[parts]
            formers[slot] = outs[parts + 1] if has_rest else None
            if loading:
                own = pl.pallas_call(
                    load_kernel,
                    out_shape=matrix_shapes,
                    in_specs=[in_smem] + [in_hbm] * 3,
                    out_specs=[in_vmem] * 3,
                    scratch_shapes=[pltpu.SemaphoreType.DMA((3,))],
                    compiler_params=params(42),
                    name="load_weights",
                )(mark, *own)
                weights = (*own, *other)
            later = {1: ends, 2: middle}.get(slot, [])
            def expert(closing):
                return pl.pallas_call(
                    partial(
                        forward_kernel,
                        slot,
                        micro_count,
                        parts,
                        loading,
                        len(later),
                        first_back,
                        closing,
                    ),
                    out_shape=([] if closing else [wide] * parts)
                    + state_shapes
                    + ([rows_shape] + matrix_shapes if loading else []),
                    in_specs=[in_smem, in_vmem]
                    + [in_vmem] * parts
                    + [in_vmem] * 3
                    + [in_hbm if loading else in_vmem] * 3
                    + [anywhere] * len(later)
                    + [in_vmem] * (2 if loading else 0),
                    out_specs=[in_vmem]
                    * ((0 if closing else parts) + 4 + (4 if loading else 0)),
                    scratch_shapes=[
                        pltpu.VMEM((slots, model_dim), jnp.bfloat16),
                        pltpu.VMEM((2, slots, hidden_dim), jnp.bfloat16),
                    ]
                    + ([pltpu.SemaphoreType.DMA((3,))] if loading else []),
                    compiler_params=params(28 if loading else 6),
                    cost_estimate=light,
                    name=f"expert_{'closing' if closing else 'forward'}_{slot}",
                )(
                    sec,
                    gain,
                    *moved,
                    *weights,
                    *later,
                    *([tokens_in[0], cotangent[0]] if loading else []),
                )

            def kept(states):
                x_rows, pre_gate, pre_up, made = states
                return (made, x_rows, pre_gate, pre_up)

            ahead = None
            if forward_on[0] < first_back:
                outs = expert(False)
                saved[slot] = kept(outs[parts : parts + 4])
                jobs = onto_next[:-1] if slot < section_count - 2 else onto_next
                ahead = exchange(outs[:parts], jobs, -1)
            if first_back in forward_on:
                saved_last = kept(expert(True))
            if loading:
                weights = (*own, *outs[parts + 5 :])
                came = travel(1, outs[parts + 4])
                ends = send_cotangents([0, section_count - 1])
                send_inputs(came)
                middle = send_cotangents(list(range(1, section_count - 1)))
        backward_on = [s for s in sections if 0 <= slot - 2 * first_back + s < micro_count]
        if backward_on:
            first, index = first_grads.get(slot - first_back, (behind, 0))
            if behind is None:
                grads = first
            else:
                first_time = len(backward_on) == 2 and first_back in backward_on
                grads = exchange(behind, onto_former[-1:] if first_time else onto_former, 1)
            states = []
            for s in backward_on:
                states += list(saved_last if s == first_back else saved[slot - 2 * first_back + 2 * s])
            outs = pl.pallas_call(
                partial(backward_kernel, slot, counts, backward_on, parts, index),
                out_shape=[wide] * parts,
                in_specs=[in_smem, in_vmem] + [pl.BlockSpec(memory_space=pl.ANY)] * (2 * parts)
                + [in_vmem] * 6
                + [pl.BlockSpec(memory_space=pl.ANY)] * len(states),
                out_specs=[in_vmem] * parts,
                scratch_shapes=[
                    pltpu.VMEM((slots, model_dim), jnp.bfloat16),
                    pltpu.VMEM((slots, model_dim + lanes), jnp.bfloat16),
                    pltpu.VMEM((slots, 2 * hidden_dim), jnp.float32),
                    pltpu.VMEM((slots, 2 * hidden_dim), jnp.float32),
                    pltpu.VMEM((slots, model_dim), jnp.float32),
                    pltpu.VMEM((slots, model_dim), jnp.bfloat16),
                    pltpu.VMEM((slots, model_dim), jnp.float32),
                    pltpu.SemaphoreType.DMA((4,)),
                    pltpu.SemaphoreType.DMA((parts,)),
                ],
                compiler_params=params(8),
                cost_estimate=light,
                name=f"expert_backward_{slot}",
            )(sec, gain, *grads, *first, *weights, *states)
            alone = slot < section_count + 1
            home = exchange(outs, staying(backward_on if alone else sections), -1)
            onward = [s for s in backward_on if s > 0]
            has_former = results is not None
            outs = pl.pallas_call(
                partial(backward_router, slot, counts, parts, has_former, onward),
                out_shape=[
                    jax.ShapeDtypeStruct((micro_count, tok_rows, model_dim), jnp.bfloat16),
                    jax.ShapeDtypeStruct((micro_count, tok_rows, lanes), jnp.float32),
                ]
                + [chunk] * (parts if onward else 0),
                in_specs=[in_smem, in_vmem, in_vmem]
                + [in_vmem] * parts
                + [in_hbm] * (2 if has_former else 0)
                + [in_vmem] * len(onward),
                out_specs=[in_hbm] * 2 + [in_vmem] * (parts if onward else 0),
                scratch_shapes=[
                    pltpu.VMEM((tok_rows, model_dim), jnp.bfloat16),
                    pltpu.VMEM((tok_rows, lanes), jnp.float32),
                    pltpu.SemaphoreType.DMA((2,)),
                ],
                input_output_aliases={3 + parts: 0, 4 + parts: 1} if has_former else {},
                compiler_params=params(4),
                cost_estimate=light,
                name=f"route_backward_{slot}",
            )(
                sec,
                take_own,
                place_wide,
                *home,
                *(results if has_former else []),
                *[formers[slot - 2 * first_back + 2 * s] for s in onward],
            )
            results = outs[:2]
            behind = outs[2:]

    return (results[0][None], results[1][None, :, :, :1])


def solution(mesh):
    return jax.shard_map(
        body,
        mesh=mesh,
        in_specs=(
            P("section", "expert", None),
            P("section", "expert", None),
            P("section", None),
            P("section", "expert", None, None),
            P("section", "expert", None, None),
            P("section", "expert", None, None),
            P("section", None, "expert", None),
            P("section", None, "expert", None),
        ),
        out_specs=(P("section", None, "expert", None), P("section", None, "expert", None)),
        check_vma=False,
    )
```

```python
from functools import partial

import jax
import jax.numpy as jnp
from jax import lax
from jax.experimental import pallas as pl
from jax.experimental.pallas import tpu as pltpu
from jax.sharding import PartitionSpec as P

epsilon = 1e-06
both = ("section", "expert")
last_with_last = (((1,), (1,)), ((), ()))

in_vmem = pl.BlockSpec(memory_space=pltpu.VMEM)
in_smem = pl.BlockSpec(memory_space=pltpu.SMEM)
in_hbm = pl.BlockSpec(memory_space=pltpu.HBM)
anywhere = pl.BlockSpec(memory_space=pl.ANY)
lanes = 128


def spans(total, size):
    size = size if total % size == 0 else total
    return [pl.ds(start, size) for start in range(0, total, size)]


def params(mib):
    return pltpu.CompilerParams(vmem_limit_bytes=mib * 2**20)


def product(left, right):
    return jnp.dot(left, right, preferred_element_type=jnp.float32)


def product_t(left, right):
    return lax.dot_general(left, right, last_with_last, preferred_element_type=jnp.float32)


def coded(column, number=None):
    high = column.astype(jnp.bfloat16).astype(jnp.float32)
    left = column - high
    middle = left.astype(jnp.bfloat16).astype(jnp.float32)
    lane = lax.broadcasted_iota(jnp.int32, (column.shape[0], lanes), 1)
    spread = jnp.where(lane == 1, middle, jnp.where(lane == 2, left - middle, 0.0))
    spread = jnp.where(lane == 0, high, spread)
    if number is not None:
        spread = jnp.where(lane == 3, number, spread)
    return spread.astype(jnp.bfloat16)


def decoded(columns):
    lane = lax.broadcasted_iota(jnp.int32, columns.shape, 1)
    values = jnp.where(lane < 3, columns.astype(jnp.float32), 0.0)
    return jnp.sum(values, axis=-1, keepdims=True)


def numbered(columns):
    lane = lax.broadcasted_iota(jnp.int32, columns.shape, 1)
    values = columns.astype(jnp.float32)
    number = jnp.sum(jnp.where(lane == 3, values, 0.0), axis=-1, keepdims=True)
    return (number == (lane + 1).astype(jnp.float32)).astype(jnp.bfloat16)


def load_kernel(core, *refs):
    sec_ref = refs[0]
    mark_ref = refs[-2]
    sems = refs[-1]
    mark_ref[0] = sec_ref[0]

    @pl.when(sec_ref[1] == core)
    def _():
        copies = [
            pltpu.make_async_copy(refs[2 + number], refs[-5 + number], sems.at[number])
            for number in range(3)
        ]
        for copy in copies:
            copy.start()
        for copy in copies:
            copy.wait()


def choose_kernel(steps, after_ref, sec_ref, tokens_ref, cotangent_ref, *out_refs):
    for step, out_ref in zip(steps, out_refs):

        @pl.when(sec_ref[0] == step)
        def _():
            out_ref[...] = tokens_ref[...]

        @pl.when(sec_ref[0] != step)
        def _():
            out_ref[...] = cotangent_ref[...]


def forward_kernel(slot, micro_count, parts, loading, later, last, closing, *refs):
    sec_ref, gain_ref = refs[:2]
    x_refs = refs[2 : 2 + parts]
    given = refs[2 + parts : 8 + parts]
    rest = refs[8 + parts + later :]
    if loading:
        inputs, rest = rest[:2], rest[2:]
    out_refs = [] if closing else rest[:parts]
    save_x, save_gate, save_up, save_rows = rest[len(out_refs) : 4 + len(out_refs)]
    rest = rest[4 + len(out_refs) :]
    if loading:
        choose_kernel([1], None, sec_ref, *inputs, rest[0])
        rest = rest[1:]
    half_refs = [given[0:3], rest[0:3] if loading else given[3:6]]
    copies = []
    if loading:
        normed, hidden, sems = rest[3:]
        copies = [
            pltpu.make_async_copy(given[3 + number], half_refs[1][number], sems.at[number])
            for number in range(3)
        ]
        for copy in copies:
            copy.start()
    else:
        normed, hidden = rest
    micro = slot - sec_ref[0]
    mine = sec_ref[0] == last if closing else sec_ref[0] < last
    active = (micro >= 0) & (micro < micro_count) & mine
    width = gain_ref.shape[1]
    hidden_dim = half_refs[0][0].shape[1]
    rows = x_refs[0].shape[0]

    @pl.when(active)
    def _():
        for part in range(parts):
            values = x_refs[part][:, :width].astype(jnp.float32)
            inv_rms = lax.rsqrt(jnp.mean(values * values, axis=-1, keepdims=True) + epsilon)
            here = pl.ds(part * rows, rows)
            normed[here, :] = (values * inv_rms * gain_ref[...]).astype(jnp.bfloat16)
            save_x[here, :] = x_refs[part][...]
            if out_refs:
                out_refs[part][:, width:] = x_refs[part][:, width:]

    for half in range(2):
        if loading and half == 1:
            copies[0].wait()
            copies[1].wait()

        @pl.when(active)
        def _():
            side = pl.ds(half * hidden_dim, hidden_dim)
            gate_pre = product(normed[...], half_refs[half][0][...])
            up_pre = product(normed[...], half_refs[half][1][...])
            save_gate[:, side] = gate_pre
            save_up[:, side] = up_pre
            hidden[half] = (gate_pre * jax.nn.sigmoid(gate_pre) * up_pre).astype(jnp.bfloat16)

    if loading:
        copies[2].wait()

    @pl.when(active)
    def _():
        route = [decoded(x_refs[part][:, width:]) for part in range(parts)]
        for span in spans(width, 256):
            made = product(hidden[0], half_refs[0][2][:, span])
            made = made + product(hidden[1], half_refs[1][2][:, span])
            save_rows[:, span] = made
            for part in range(len(out_refs)):
                added = route[part] * made[part * rows : (part + 1) * rows]
                values = x_refs[part][:, span].astype(jnp.float32)
                out_refs[part][:, span] = (values + added).astype(jnp.bfloat16)


def backward_kernel(slot, counts, candidates, parts, index, *refs):
    section_count, micro_count = counts
    sec_ref, gain_ref = refs[:2]
    rest = refs[2:]
    arrived = rest[:parts]
    first = rest[parts : 2 * parts]
    rest = rest[2 * parts :]
    half_refs = [rest[0:3], rest[3:6]]
    rest = rest[6:]
    saved = {}
    for section in candidates:
        saved[section] = rest[:4]
        rest = rest[4:]
    out_refs = rest[:parts]
    (grad_buf, x_buf, pre_gate, pre_up, rows_buf, grad_rows, scaled_buf, state_sems, grad_sems) = rest[parts:]
    sec = sec_ref[0]
    micro = slot - 2 * (section_count - 1) + sec
    width = gain_ref.shape[1]
    hidden_dim = half_refs[0][0].shape[1]
    slots = grad_buf.shape[0]
    rows = slots // parts

    @pl.when((micro >= 0) & (micro < micro_count))
    def _():
        def for_section(section, act):
            @pl.when(sec == section)
            def _():
                for part in range(parts):
                    if section == section_count - 1:
                        source = first[part].at[index]
                    else:
                        source = arrived[part]
                    act(pltpu.make_async_copy(
                        source, grad_buf.at[pl.ds(part * rows, rows), :], grad_sems.at[part]
                    ))
                targets = (rows_buf, x_buf, pre_gate, pre_up)
                for number, target in enumerate(targets):
                    act(pltpu.make_async_copy(
                        saved[section][number], target, state_sems.at[number]
                    ))

        for section in candidates:
            for_section(section, lambda copy: copy.start())
        for section in candidates:
            for_section(section, lambda copy: copy.wait())
        route = decoded(x_buf[:, width:])
        gate_grad = jnp.zeros((slots, 1), jnp.float32)
        square = jnp.zeros((slots, 1), jnp.float32)
        for span in spans(width, 512):
            grad_f = grad_buf[:, span].astype(jnp.float32)
            gate_grad += jnp.sum(grad_f * rows_buf[:, span], axis=-1, keepdims=True)
            grad_rows[:, span] = (route * grad_f).astype(jnp.bfloat16)
            values = x_buf[:, span].astype(jnp.float32)
            square += jnp.sum(values * values, axis=-1, keepdims=True)
        gate_columns = coded(gate_grad)
        for part in range(parts):
            out_refs[part][:, width:] = gate_columns[part * rows : (part + 1) * rows]
        inv_rms = lax.rsqrt(square / width + epsilon)
        grads = []
        for half in range(2):
            side = pl.ds(half * hidden_dim, hidden_dim)
            grad_hidden = product_t(half_refs[half][2][...], grad_rows[...]).T
            gate_pre = pre_gate[:, side]
            sigma = jax.nn.sigmoid(gate_pre)
            grad_gate = grad_hidden * pre_up[:, side] * sigma * (1.0 + gate_pre * (1.0 - sigma))
            grad_up = grad_hidden * gate_pre * sigma
            grads.append((grad_gate.astype(jnp.bfloat16), grad_up.astype(jnp.bfloat16)))
        dotted = jnp.zeros((slots, 1), jnp.float32)
        for span in spans(width, 256):
            total = product_t(half_refs[0][0][span, :], grads[0][0])
            total = total + product_t(half_refs[0][1][span, :], grads[0][1])
            total = total + product_t(half_refs[1][0][span, :], grads[1][0])
            total = total + product_t(half_refs[1][1][span, :], grads[1][1])
            scaled = total.T * gain_ref[:, span]
            scaled_buf[:, span] = scaled
            dotted += jnp.sum(x_buf[:, span].astype(jnp.float32) * scaled, axis=-1, keepdims=True)
        back = inv_rms * inv_rms * inv_rms * (dotted / width)
        for span in spans(width, 512):
            grad_in = (
                grad_buf[:, span].astype(jnp.float32)
                + inv_rms * scaled_buf[:, span]
                - x_buf[:, span].astype(jnp.float32) * back
            ).astype(jnp.bfloat16)
            for part in range(parts):
                out_refs[part][:, span] = grad_in[part * rows : (part + 1) * rows]


def forward_router(slot, micro_count, parts, has_first, has_rest, *refs):
    sec_ref, began_ref, route_ref, place_ref = refs[:4]
    rest = refs[4:]
    tokens_ref = rest[0] if has_first else None
    rest = rest[1:] if has_first else rest
    arrived = rest[:parts] if has_rest else None
    rest = rest[parts:] if has_rest else rest
    out_refs = rest[:parts]
    sec = sec_ref[0]
    rest[parts][0] = sec
    micro = slot - sec
    width = out_refs[0].shape[1] - lanes
    rows = out_refs[0].shape[0]

    def put(number, table, source):
        place = place_ref[number].astype(jnp.float32)
        lane = lax.broadcasted_iota(jnp.int32, place.shape, 1)
        token = jnp.sum(place * (lane + 1).astype(jnp.float32), axis=-1, keepdims=True)
        columns = coded(route_ref[number], token)
        for part in range(parts):
            out_refs[part][:, width:] = columns[part * rows : (part + 1) * rows]
        for span in spans(width, 512):
            made = product(table, source(span)).astype(jnp.bfloat16)
            for part in range(parts):
                out_refs[part][:, span] = made[part * rows : (part + 1) * rows]

    if has_first:

        @pl.when(sec == 0)
        def _():
            table = place_ref[slot][:, : tokens_ref.shape[0]]
            put(slot, table, lambda span: tokens_ref[:, span])

    if has_rest:

        @pl.when((sec > 0) & (micro >= 0) & (micro < micro_count))
        def _():
            def source(span):
                return jnp.concatenate([ref[:, span] for ref in arrived], axis=0)

            former = numbered(source(pl.ds(width, lanes)))
            rest[parts + 1][...] = former
            put(micro, product_t(place_ref[micro], former).astype(jnp.bfloat16), source)


def backward_router(slot, counts, parts, has_former, onward, *refs):
    section_count, micro_count = counts
    sec_ref, take_ref, place_ref = refs[:3]
    arrived = refs[3 : 3 + parts]
    rest = refs[3 + parts + (2 if has_former else 0) :]
    formers, rest = rest[: len(onward)], rest[len(onward) :]
    result, gates = rest[:2]
    out_refs = rest[2 : 2 + parts] if onward else []
    ordered, gate_rows, sems = rest[2 + len(out_refs) :]
    sec = sec_ref[0]
    micro = slot - 2 * (section_count - 1) + sec
    width = arrived[0].shape[1] - lanes
    rows = arrived[0].shape[0]

    @pl.when((micro >= 0) & (micro < micro_count))
    def _():
        def source(span):
            return jnp.concatenate([ref[:, span] for ref in arrived], axis=0)

        for section, former in zip(onward, formers):

            @pl.when(sec == section)
            def _():
                table = product_t(former[...], place_ref[micro]).astype(jnp.bfloat16)
                for span in spans(width, 512):
                    made = product(table, source(span)).astype(jnp.bfloat16)
                    for part in range(parts):
                        out_refs[part][:, span] = made[part * rows : (part + 1) * rows]

        for span in spans(width, 512):
            ordered[:, span] = product(take_ref[micro], source(span)).astype(jnp.bfloat16)
        copy = pltpu.make_async_copy(ordered, result.at[micro], sems.at[0])
        copy.start()
        columns = decoded(product(take_ref[micro], source(pl.ds(width, lanes))))
        gate_rows[...] = jnp.broadcast_to(columns, gate_rows.shape)
        gate_copy = pltpu.make_async_copy(gate_rows, gates.at[micro], sems.at[1])
        gate_copy.start()
        copy.wait()
        gate_copy.wait()


def slots_of(route_ids, expert_count, capacity, turn):
    count = route_ids.shape[1]
    before = jnp.arange(count)[None, :] < jnp.arange(count)[:, None]
    alike = (route_ids[:, None, :] == route_ids[:, :, None]) & before
    position = jnp.sum(alike.astype(jnp.int32), axis=-1)
    return lax.rem(route_ids - turn + expert_count, expert_count) * capacity + position


def body(tokens_in, cotangent, norm_gain, w_gate, w_up, w_down, expert_ids, gate_weights):
    section_count = lax.axis_size("section")
    device_count = lax.axis_size("expert")
    section = lax.axis_index("section")
    place = lax.axis_index("expert") // 2
    expert_count = device_count // 2
    micro_count = expert_ids.shape[1]
    tok_rows = expert_ids.shape[2]
    model_dim = tokens_in.shape[2]
    hidden_dim = w_gate.shape[3]
    capacity = 2 * ((tok_rows + expert_count - 1) // expert_count)
    slots = expert_count * capacity
    by_permute = capacity % 16 == 0
    parts = expert_count if by_permute else 1
    rows = slots // parts
    turn = place if by_permute else jnp.int32(0)
    counts = (section_count, micro_count)
    first_back = section_count - 1
    slot_count = micro_count + 2 * (section_count - 1)
    sections = list(range(section_count))

    def exchange(chunks, jobs, direction):
        if by_permute:
            moved = [None] * parts
            for step in sorted(range(parts), key=lambda k: -min(k, parts - k)):
                if step == 0 and all(a == b for a, b in jobs):
                    moved[0] = chunks[0]
                    continue
                pairs = [
                    (
                        a * device_count + 2 * z + core,
                        b * device_count + 2 * ((z + direction * step) % expert_count) + core,
                    )
                    for a, b in jobs
                    for z in range(expert_count)
                    for core in range(2)
                ]
                moved[step] = lax.ppermute(chunks[step], both, sorted(pairs))
            return moved
        (block,) = chunks
        shape = block.shape
        spread = block.reshape(-1, expert_count, capacity, shape[-1])
        groups = [[2 * z + core for z in range(expert_count)] for core in range(2)]
        spread = lax.all_to_all(
            spread, "expert", split_axis=1, concat_axis=1, tiled=True, axis_index_groups=groups
        )
        block = spread.reshape(shape)
        if any(a != b for a, b in jobs):
            block = lax.ppermute(block, "section", jobs)
        return [block]

    def cut(block):
        return [block[:, part * rows : (part + 1) * rows] for part in range(parts)]

    own = (w_gate[0, 0], w_up[0, 0], w_down[0, 0])
    swap = [(i, i ^ 1) for i in range(device_count)]
    other = [lax.ppermute(matrix, "expert", swap) for matrix in own]

    sec = jnp.stack([section, lax.rem(lax.axis_index("expert"), 2)]).astype(jnp.int32)
    gain = norm_gain
    ids = expert_ids[0, :, :, 0]
    onto_next = [(s, s + 1) for s in sections[:-1]]
    onto_former = [(s + 1, s) for s in sections[:-1]]
    numbers = jnp.arange(slots, dtype=jnp.int32)

    slot_own = slots_of(ids, expert_count, capacity, turn)
    padded = jnp.pad(slot_own, ((0, 0), (0, lanes - tok_rows)), constant_values=-1)
    place_wide = (numbers[None, :, None] == padded[:, None, :]).astype(jnp.bfloat16)
    is_own = numbers[None, :, None] == slot_own[:, None, :]
    place_own = is_own.astype(jnp.bfloat16)
    take_own = place_own.transpose(0, 2, 1)

    def staying(members):
        return [(s, s) for s in members]

    route_slots = jnp.sum(jnp.where(is_own, gate_weights[0, :, None, :, 0], 0.0), axis=-1)
    route = route_slots[:, :, None]

    def send_inputs(after):
        steps = list(range(2, section_count))
        sent = pl.pallas_call(
            partial(choose_kernel, steps),
            out_shape=[rows_shape] * len(steps),
            in_specs=[anywhere, in_smem] + [in_vmem] * 2,
            out_specs=[in_vmem] * len(steps),
            compiler_params=params(4),
            cost_estimate=light,
            name="choose_inputs",
        )(after, sec, tokens_in[0], cotangent[0])
        for step, rows_sent in zip(steps, sent):
            travel(step, rows_sent)

    def travel(step, rows_sent):
        came = lax.ppermute(rows_sent, "section", [(step, 0), (step - 1, section_count - 1)])
        tokens_all.append(came)
        cotangent_all[step - 1] = came
        return came

    def send_cotangents(micros):
        packed = jnp.einsum(
            "mjt,mtd->mjd",
            jnp.stack([place_own[m] for m in micros]),
            jnp.stack([cotangent_all[m] for m in micros]),
            preferred_element_type=jnp.float32,
        ).astype(jnp.bfloat16)
        spread = exchange(cut(packed), staying([first_back]), 1)
        for index, m in enumerate(micros):
            first_grads[m] = (spread, index)
        return spread

    cotangent_all = {section_count - 1: cotangent[0]}
    tokens_all = [tokens_in[0]]
    first_grads = {}
    ends = middle = []

    chunk = jax.ShapeDtypeStruct((rows, model_dim), jnp.bfloat16)
    rows_shape = jax.ShapeDtypeStruct((tok_rows, model_dim), jnp.bfloat16)
    mark_shape = jax.ShapeDtypeStruct((1,), jnp.int32)
    matrix_shapes = [jax.ShapeDtypeStruct(m.shape, m.dtype) for m in own]
    wide = jax.ShapeDtypeStruct((rows, model_dim + lanes), jnp.bfloat16)
    light = pl.CostEstimate(flops=0, bytes_accessed=0, transcendentals=0)
    state_shapes = [
        jax.ShapeDtypeStruct((slots, model_dim + lanes), jnp.bfloat16),
        jax.ShapeDtypeStruct((slots, 2 * hidden_dim), jnp.float32),
        jax.ShapeDtypeStruct((slots, 2 * hidden_dim), jnp.float32),
        jax.ShapeDtypeStruct((slots, model_dim), jnp.float32),
    ]

    def load(core, after, matrices, loaded):
        return pl.pallas_call(
            partial(load_kernel, core),
            out_shape=matrix_shapes + [mark_shape],
            in_specs=[in_smem, anywhere] + [in_hbm] * 3 + [in_vmem] * len(loaded),
            out_specs=[in_vmem] * 3 + [in_smem],
            scratch_shapes=[pltpu.SemaphoreType.DMA((3,))],
            input_output_aliases={5 + number: number for number in range(len(loaded))},
            compiler_params=params(42),
            name=f"load_core_{core}",
        )(sec, after, *matrices, *loaded)

    *loaded, began = load(0, place_wide, own, [])
    saved = {}
    formers = {}
    former_shape = jax.ShapeDtypeStruct((slots, lanes), jnp.bfloat16)
    ahead = None
    behind = None
    results = None
    for slot in range(slot_count):
        forward_on = [s for s in sections if 0 <= slot - s < micro_count]
        if forward_on:
            has_first = 0 in forward_on
            has_rest = ahead is not None
            loading = slot == 0
            outs = pl.pallas_call(
                partial(forward_router, slot, micro_count, parts, has_first, has_rest),
                out_shape=[wide] * parts + [mark_shape] + ([former_shape] if has_rest else []),
                in_specs=[in_smem, in_smem, in_vmem, in_vmem]
                + [in_vmem] * ((1 if has_first else 0) + (parts if has_rest else 0)),
                out_specs=[in_vmem] * parts + [in_smem] + ([in_vmem] if has_rest else []),
                compiler_params=params(4),
                cost_estimate=light,
                name=f"route_forward_{slot}",
            )(
                sec,
                began,
                route,
                place_wide,
                *([tokens_all[slot]] if has_first else []),
                *(ahead if has_rest else []),
            )
            busy = slot > section_count
            moved = exchange(outs[:parts], staying(forward_on if busy else sections), 1)
            mark = outs[parts]
            formers[slot] = outs[parts + 1] if has_rest else None
            if loading:
                *own, _ = load(1, mark, own, loaded)
                weights = (*own, *other)
            later = {1: ends, 2: middle}.get(slot, [])
            def expert(closing):
                return pl.pallas_call(
                    partial(
                        forward_kernel,
                        slot,
                        micro_count,
                        parts,
                        loading,
                        len(later),
                        first_back,
                        closing,
                    ),
                    out_shape=([] if closing else [wide] * parts)
                    + state_shapes
                    + ([rows_shape] + matrix_shapes if loading else []),
                    in_specs=[in_smem, in_vmem]
                    + [in_vmem] * parts
                    + [in_vmem] * 3
                    + [in_hbm if loading else in_vmem] * 3
                    + [anywhere] * len(later)
                    + [in_vmem] * (2 if loading else 0),
                    out_specs=[in_vmem]
                    * ((0 if closing else parts) + 4 + (4 if loading else 0)),
                    scratch_shapes=[
                        pltpu.VMEM((slots, model_dim), jnp.bfloat16),
                        pltpu.VMEM((2, slots, hidden_dim), jnp.bfloat16),
                    ]
                    + ([pltpu.SemaphoreType.DMA((3,))] if loading else []),
                    compiler_params=params(28 if loading else 6),
                    cost_estimate=light,
                    name=f"expert_{'closing' if closing else 'forward'}_{slot}",
                )(
                    sec,
                    gain,
                    *moved,
                    *weights,
                    *later,
                    *([tokens_in[0], cotangent[0]] if loading else []),
                )

            def kept(states):
                x_rows, pre_gate, pre_up, made = states
                return (made, x_rows, pre_gate, pre_up)

            ahead = None
            if forward_on[0] < first_back:
                outs = expert(False)
                saved[slot] = kept(outs[parts : parts + 4])
                jobs = onto_next[:-1] if slot < section_count - 2 else onto_next
                ahead = exchange(outs[:parts], jobs, -1)
            if first_back in forward_on:
                saved_last = kept(expert(True))
            if loading:
                weights = (*own, *outs[parts + 5 :])
                came = travel(1, outs[parts + 4])
                ends = send_cotangents([0, section_count - 1])
                send_inputs(came)
                middle = send_cotangents(list(range(1, section_count - 1)))
        backward_on = [s for s in sections if 0 <= slot - 2 * first_back + s < micro_count]
        if backward_on:
            first, index = first_grads.get(slot - first_back, (behind, 0))
            if behind is None:
                grads = first
            else:
                first_time = len(backward_on) == 2 and first_back in backward_on
                grads = exchange(behind, onto_former[-1:] if first_time else onto_former, 1)
            states = []
            for s in backward_on:
                states += list(saved_last if s == first_back else saved[slot - 2 * first_back + 2 * s])
            outs = pl.pallas_call(
                partial(backward_kernel, slot, counts, backward_on, parts, index),
                out_shape=[wide] * parts,
                in_specs=[in_smem, in_vmem] + [pl.BlockSpec(memory_space=pl.ANY)] * (2 * parts)
                + [in_vmem] * 6
                + [pl.BlockSpec(memory_space=pl.ANY)] * len(states),
                out_specs=[in_vmem] * parts,
                scratch_shapes=[
                    pltpu.VMEM((slots, model_dim), jnp.bfloat16),
                    pltpu.VMEM((slots, model_dim + lanes), jnp.bfloat16),
                    pltpu.VMEM((slots, 2 * hidden_dim), jnp.float32),
                    pltpu.VMEM((slots, 2 * hidden_dim), jnp.float32),
                    pltpu.VMEM((slots, model_dim), jnp.float32),
                    pltpu.VMEM((slots, model_dim), jnp.bfloat16),
                    pltpu.VMEM((slots, model_dim), jnp.float32),
                    pltpu.SemaphoreType.DMA((4,)),
                    pltpu.SemaphoreType.DMA((parts,)),
                ],
                compiler_params=params(8),
                cost_estimate=light,
                name=f"expert_backward_{slot}",
            )(sec, gain, *grads, *first, *weights, *states)
            alone = slot < section_count + 1
            home = exchange(outs, staying(backward_on if alone else sections), -1)
            onward = [s for s in backward_on if s > 0]
            has_former = results is not None
            outs = pl.pallas_call(
                partial(backward_router, slot, counts, parts, has_former, onward),
                out_shape=[
                    jax.ShapeDtypeStruct((micro_count, tok_rows, model_dim), jnp.bfloat16),
                    jax.ShapeDtypeStruct((micro_count, tok_rows, lanes), jnp.float32),
                ]
                + [chunk] * (parts if onward else 0),
                in_specs=[in_smem, in_vmem, in_vmem]
                + [in_vmem] * parts
                + [in_hbm] * (2 if has_former else 0)
                + [in_vmem] * len(onward),
                out_specs=[in_hbm] * 2 + [in_vmem] * (parts if onward else 0),
                scratch_shapes=[
                    pltpu.VMEM((tok_rows, model_dim), jnp.bfloat16),
                    pltpu.VMEM((tok_rows, lanes), jnp.float32),
                    pltpu.SemaphoreType.DMA((2,)),
                ],
                input_output_aliases={3 + parts: 0, 4 + parts: 1} if has_former else {},
                compiler_params=params(4),
                cost_estimate=light,
                name=f"route_backward_{slot}",
            )(
                sec,
                take_own,
                place_wide,
                *home,
                *(results if has_former else []),
                *[formers[slot - 2 * first_back + 2 * s] for s in onward],
            )
            results = outs[:2]
            behind = outs[2:]

    return (results[0][None], results[1][None, :, :, :1])


def solution(mesh):
    return jax.shard_map(
        body,
        mesh=mesh,
        in_specs=(
            P("section", "expert", None),
            P("section", "expert", None),
            P("section", None),
            P("section", "expert", None, None),
            P("section", "expert", None, None),
            P("section", "expert", None, None),
            P("section", None, "expert", None),
            P("section", None, "expert", None),
        ),
        out_specs=(P("section", None, "expert", None), P("section", None, "expert", None)),
        check_vma=False,
    )
```

```python
from functools import partial

import jax
import jax.numpy as jnp
from jax import lax
from jax.experimental import pallas as pl
from jax.experimental.pallas import tpu as pltpu
from jax.sharding import PartitionSpec as P

epsilon = 1e-06
both = ("section", "expert")
last_with_last = (((1,), (1,)), ((), ()))

in_vmem = pl.BlockSpec(memory_space=pltpu.VMEM)
in_smem = pl.BlockSpec(memory_space=pltpu.SMEM)
in_hbm = pl.BlockSpec(memory_space=pltpu.HBM)
anywhere = pl.BlockSpec(memory_space=pl.ANY)
lanes = 128


def spans(total, size):
    size = size if total % size == 0 else total
    return [pl.ds(start, size) for start in range(0, total, size)]


def params(mib):
    return pltpu.CompilerParams(vmem_limit_bytes=mib * 2**20)


def product(left, right):
    return jnp.dot(left, right, preferred_element_type=jnp.float32)


def product_t(left, right):
    return lax.dot_general(left, right, last_with_last, preferred_element_type=jnp.float32)


def coded(column, number=None):
    high = column.astype(jnp.bfloat16).astype(jnp.float32)
    left = column - high
    middle = left.astype(jnp.bfloat16).astype(jnp.float32)
    lane = lax.broadcasted_iota(jnp.int32, (column.shape[0], lanes), 1)
    spread = jnp.where(lane == 1, middle, jnp.where(lane == 2, left - middle, 0.0))
    spread = jnp.where(lane == 0, high, spread)
    if number is not None:
        spread = jnp.where(lane == 3, number, spread)
    return spread.astype(jnp.bfloat16)


def decoded(columns):
    lane = lax.broadcasted_iota(jnp.int32, columns.shape, 1)
    values = jnp.where(lane < 3, columns.astype(jnp.float32), 0.0)
    return jnp.sum(values, axis=-1, keepdims=True)


def numbered(columns):
    lane = lax.broadcasted_iota(jnp.int32, columns.shape, 1)
    values = columns.astype(jnp.float32)
    number = jnp.sum(jnp.where(lane == 3, values, 0.0), axis=-1, keepdims=True)
    return (number == (lane + 1).astype(jnp.float32)).astype(jnp.bfloat16)


def load_kernel(core, *refs):
    core_ref = refs[0]
    sems = refs[-1]

    @pl.when(core_ref[0] == core)
    def _():
        copies = [
            pltpu.make_async_copy(refs[2 + number], refs[-4 + number], sems.at[number])
            for number in range(3)
        ]
        for copy in copies:
            copy.start()
        for copy in copies:
            copy.wait()


def choose_kernel(steps, after_ref, sec_ref, tokens_ref, cotangent_ref, *out_refs):
    for step, out_ref in zip(steps, out_refs):

        @pl.when(sec_ref[0] == step)
        def _():
            out_ref[...] = tokens_ref[...]

        @pl.when(sec_ref[0] != step)
        def _():
            out_ref[...] = cotangent_ref[...]


def forward_kernel(slot, micro_count, parts, loading, later, last, closing, *refs):
    sec_ref, gain_ref = refs[:2]
    x_refs = refs[2 : 2 + parts]
    given = refs[2 + parts : 8 + parts]
    rest = refs[8 + parts + later :]
    if loading:
        inputs, rest = rest[:2], rest[2:]
    out_refs = [] if closing else rest[:parts]
    save_x, save_gate, save_up, save_rows = rest[len(out_refs) : 4 + len(out_refs)]
    rest = rest[4 + len(out_refs) :]
    if loading:
        choose_kernel([1], None, sec_ref, *inputs, rest[0])
        rest = rest[1:]
    half_refs = [given[0:3], rest[0:3] if loading else given[3:6]]
    copies = []
    if loading:
        normed, hidden, sems = rest[3:]
        copies = [
            pltpu.make_async_copy(given[3 + number], half_refs[1][number], sems.at[number])
            for number in range(3)
        ]
        for copy in copies:
            copy.start()
    else:
        normed, hidden = rest
    micro = slot - sec_ref[0]
    mine = sec_ref[0] == last if closing else sec_ref[0] < last
    active = (micro >= 0) & (micro < micro_count) & mine
    width = gain_ref.shape[1]
    hidden_dim = half_refs[0][0].shape[1]
    rows = x_refs[0].shape[0]

    @pl.when(active)
    def _():
        for part in range(parts):
            values = x_refs[part][:, :width].astype(jnp.float32)
            inv_rms = lax.rsqrt(jnp.mean(values * values, axis=-1, keepdims=True) + epsilon)
            here = pl.ds(part * rows, rows)
            normed[here, :] = (values * inv_rms * gain_ref[...]).astype(jnp.bfloat16)
            save_x[here, :] = x_refs[part][...]
            if out_refs:
                out_refs[part][:, width:] = x_refs[part][:, width:]

    for half in range(2):
        if loading and half == 1:
            copies[0].wait()
            copies[1].wait()

        @pl.when(active)
        def _():
            side = pl.ds(half * hidden_dim, hidden_dim)
            gate_pre = product(normed[...], half_refs[half][0][...])
            up_pre = product(normed[...], half_refs[half][1][...])
            save_gate[:, side] = gate_pre
            save_up[:, side] = up_pre
            hidden[half] = (gate_pre * jax.nn.sigmoid(gate_pre) * up_pre).astype(jnp.bfloat16)

    if loading:
        copies[2].wait()

    @pl.when(active)
    def _():
        route = [decoded(x_refs[part][:, width:]) for part in range(parts)]
        for span in spans(width, 256):
            made = product(hidden[0], half_refs[0][2][:, span])
            made = made + product(hidden[1], half_refs[1][2][:, span])
            save_rows[:, span] = made
            for part in range(len(out_refs)):
                added = route[part] * made[part * rows : (part + 1) * rows]
                values = x_refs[part][:, span].astype(jnp.float32)
                out_refs[part][:, span] = (values + added).astype(jnp.bfloat16)


def backward_kernel(slot, counts, candidates, parts, index, *refs):
    section_count, micro_count = counts
    sec_ref, gain_ref = refs[:2]
    rest = refs[2:]
    arrived = rest[:parts]
    first = rest[parts : 2 * parts]
    rest = rest[2 * parts :]
    half_refs = [rest[0:3], rest[3:6]]
    rest = rest[6:]
    saved = {}
    for section in candidates:
        saved[section] = rest[:4]
        rest = rest[4:]
    out_refs = rest[:parts]
    (grad_buf, x_buf, pre_gate, pre_up, rows_buf, grad_rows, scaled_buf, state_sems, grad_sems) = rest[parts:]
    sec = sec_ref[0]
    micro = slot - 2 * (section_count - 1) + sec
    width = gain_ref.shape[1]
    hidden_dim = half_refs[0][0].shape[1]
    slots = grad_buf.shape[0]
    rows = slots // parts

    @pl.when((micro >= 0) & (micro < micro_count))
    def _():
        def for_section(section, act):
            @pl.when(sec == section)
            def _():
                for part in range(parts):
                    if section == section_count - 1:
                        source = first[part].at[index]
                    else:
                        source = arrived[part]
                    act(pltpu.make_async_copy(
                        source, grad_buf.at[pl.ds(part * rows, rows), :], grad_sems.at[part]
                    ))
                targets = (rows_buf, x_buf, pre_gate, pre_up)
                for number, target in enumerate(targets):
                    act(pltpu.make_async_copy(
                        saved[section][number], target, state_sems.at[number]
                    ))

        for section in candidates:
            for_section(section, lambda copy: copy.start())
        for section in candidates:
            for_section(section, lambda copy: copy.wait())
        route = decoded(x_buf[:, width:])
        gate_grad = jnp.zeros((slots, 1), jnp.float32)
        square = jnp.zeros((slots, 1), jnp.float32)
        for span in spans(width, 512):
            grad_f = grad_buf[:, span].astype(jnp.float32)
            gate_grad += jnp.sum(grad_f * rows_buf[:, span], axis=-1, keepdims=True)
            grad_rows[:, span] = (route * grad_f).astype(jnp.bfloat16)
            values = x_buf[:, span].astype(jnp.float32)
            square += jnp.sum(values * values, axis=-1, keepdims=True)
        gate_columns = coded(gate_grad)
        for part in range(parts):
            out_refs[part][:, width:] = gate_columns[part * rows : (part + 1) * rows]
        inv_rms = lax.rsqrt(square / width + epsilon)
        grads = []
        for half in range(2):
            side = pl.ds(half * hidden_dim, hidden_dim)
            grad_hidden = product_t(half_refs[half][2][...], grad_rows[...]).T
            gate_pre = pre_gate[:, side]
            sigma = jax.nn.sigmoid(gate_pre)
            grad_gate = grad_hidden * pre_up[:, side] * sigma * (1.0 + gate_pre * (1.0 - sigma))
            grad_up = grad_hidden * gate_pre * sigma
            grads.append((grad_gate.astype(jnp.bfloat16), grad_up.astype(jnp.bfloat16)))
        dotted = jnp.zeros((slots, 1), jnp.float32)
        for span in spans(width, 256):
            total = product_t(half_refs[0][0][span, :], grads[0][0])
            total = total + product_t(half_refs[0][1][span, :], grads[0][1])
            total = total + product_t(half_refs[1][0][span, :], grads[1][0])
            total = total + product_t(half_refs[1][1][span, :], grads[1][1])
            scaled = total.T * gain_ref[:, span]
            scaled_buf[:, span] = scaled
            dotted += jnp.sum(x_buf[:, span].astype(jnp.float32) * scaled, axis=-1, keepdims=True)
        back = inv_rms * inv_rms * inv_rms * (dotted / width)
        for span in spans(width, 512):
            grad_in = (
                grad_buf[:, span].astype(jnp.float32)
                + inv_rms * scaled_buf[:, span]
                - x_buf[:, span].astype(jnp.float32) * back
            ).astype(jnp.bfloat16)
            for part in range(parts):
                out_refs[part][:, span] = grad_in[part * rows : (part + 1) * rows]


def forward_router(slot, micro_count, parts, has_first, has_rest, *refs):
    sec_ref, route_ref, place_ref = refs[:3]
    rest = refs[3:]
    tokens_ref = rest[0] if has_first else None
    rest = rest[1:] if has_first else rest
    arrived = rest[:parts] if has_rest else None
    rest = rest[parts:] if has_rest else rest
    rest = rest[1:] if slot == 0 else rest
    out_refs = rest[:parts]
    sec = sec_ref[0]
    micro = slot - sec
    width = out_refs[0].shape[1] - lanes
    rows = out_refs[0].shape[0]

    def put(number, table, source):
        place = place_ref[number].astype(jnp.float32)
        lane = lax.broadcasted_iota(jnp.int32, place.shape, 1)
        token = jnp.sum(place * (lane + 1).astype(jnp.float32), axis=-1, keepdims=True)
        columns = coded(route_ref[number], token)
        for part in range(parts):
            out_refs[part][:, width:] = columns[part * rows : (part + 1) * rows]
        for span in spans(width, 512):
            made = product(table, source(span)).astype(jnp.bfloat16)
            for part in range(parts):
                out_refs[part][:, span] = made[part * rows : (part + 1) * rows]

    if has_first:

        @pl.when(sec == 0)
        def _():
            table = place_ref[slot][:, : tokens_ref.shape[0]]
            put(slot, table, lambda span: tokens_ref[:, span])

    if has_rest:

        @pl.when((sec > 0) & (micro >= 0) & (micro < micro_count))
        def _():
            def source(span):
                return jnp.concatenate([ref[:, span] for ref in arrived], axis=0)

            former = numbered(source(pl.ds(width, lanes)))
            rest[parts][...] = former
            put(micro, product_t(place_ref[micro], former).astype(jnp.bfloat16), source)


def backward_router(slot, counts, parts, has_former, onward, *refs):
    section_count, micro_count = counts
    sec_ref, take_ref, place_ref = refs[:3]
    arrived = refs[3 : 3 + parts]
    rest = refs[3 + parts + (2 if has_former else 0) :]
    formers, rest = rest[: len(onward)], rest[len(onward) :]
    result, gates = rest[:2]
    out_refs = rest[2 : 2 + parts] if onward else []
    ordered, gate_rows, sems = rest[2 + len(out_refs) :]
    sec = sec_ref[0]
    micro = slot - 2 * (section_count - 1) + sec
    width = arrived[0].shape[1] - lanes
    rows = arrived[0].shape[0]

    @pl.when((micro >= 0) & (micro < micro_count))
    def _():
        def source(span):
            return jnp.concatenate([ref[:, span] for ref in arrived], axis=0)

        for section, former in zip(onward, formers):

            @pl.when(sec == section)
            def _():
                table = product_t(former[...], place_ref[micro]).astype(jnp.bfloat16)
                for span in spans(width, 512):
                    made = product(table, source(span)).astype(jnp.bfloat16)
                    for part in range(parts):
                        out_refs[part][:, span] = made[part * rows : (part + 1) * rows]

        for span in spans(width, 512):
            ordered[:, span] = product(take_ref[micro], source(span)).astype(jnp.bfloat16)
        copy = pltpu.make_async_copy(ordered, result.at[micro], sems.at[0])
        copy.start()
        columns = decoded(product(take_ref[micro], source(pl.ds(width, lanes))))
        gate_rows[...] = jnp.broadcast_to(columns, gate_rows.shape)
        gate_copy = pltpu.make_async_copy(gate_rows, gates.at[micro], sems.at[1])
        gate_copy.start()
        copy.wait()
        gate_copy.wait()


def slots_of(route_ids, expert_count, capacity, turn):
    count = route_ids.shape[1]
    before = jnp.arange(count)[None, :] < jnp.arange(count)[:, None]
    alike = (route_ids[:, None, :] == route_ids[:, :, None]) & before
    position = jnp.sum(alike.astype(jnp.int32), axis=-1)
    return lax.rem(route_ids - turn + expert_count, expert_count) * capacity + position


def body(tokens_in, cotangent, norm_gain, w_gate, w_up, w_down, expert_ids, gate_weights):
    section_count = lax.axis_size("section")
    device_count = lax.axis_size("expert")
    section = lax.axis_index("section")
    place = lax.axis_index("expert") // 2
    expert_count = device_count // 2
    micro_count = expert_ids.shape[1]
    tok_rows = expert_ids.shape[2]
    model_dim = tokens_in.shape[2]
    hidden_dim = w_gate.shape[3]
    capacity = 2 * ((tok_rows + expert_count - 1) // expert_count)
    slots = expert_count * capacity
    by_permute = capacity % 16 == 0
    parts = expert_count if by_permute else 1
    rows = slots // parts
    turn = place if by_permute else jnp.int32(0)
    counts = (section_count, micro_count)
    first_back = section_count - 1
    slot_count = micro_count + 2 * (section_count - 1)
    sections = list(range(section_count))

    def exchange(chunks, jobs, direction):
        if by_permute:
            moved = [None] * parts
            for step in sorted(range(parts), key=lambda k: -min(k, parts - k)):
                if step == 0 and all(a == b for a, b in jobs):
                    moved[0] = chunks[0]
                    continue
                pairs = [
                    (
                        a * device_count + 2 * z + core,
                        b * device_count + 2 * ((z + direction * step) % expert_count) + core,
                    )
                    for a, b in jobs
                    for z in range(expert_count)
                    for core in range(2)
                ]
                moved[step] = lax.ppermute(chunks[step], both, sorted(pairs))
            return moved
        (block,) = chunks
        shape = block.shape
        spread = block.reshape(-1, expert_count, capacity, shape[-1])
        groups = [[2 * z + core for z in range(expert_count)] for core in range(2)]
        spread = lax.all_to_all(
            spread, "expert", split_axis=1, concat_axis=1, tiled=True, axis_index_groups=groups
        )
        block = spread.reshape(shape)
        if any(a != b for a, b in jobs):
            block = lax.ppermute(block, "section", jobs)
        return [block]

    def cut(block):
        return [block[:, part * rows : (part + 1) * rows] for part in range(parts)]

    own = (w_gate[0, 0], w_up[0, 0], w_down[0, 0])
    swap = [(i, i ^ 1) for i in range(device_count)]
    other = [lax.ppermute(matrix, "expert", swap) for matrix in own]

    sec = section.reshape(1).astype(jnp.int32)
    core_index = lax.rem(lax.axis_index("expert"), 2).reshape(1).astype(jnp.int32)
    gain = norm_gain
    ids = expert_ids[0, :, :, 0]
    onto_next = [(s, s + 1) for s in sections[:-1]]
    onto_former = [(s + 1, s) for s in sections[:-1]]
    numbers = jnp.arange(slots, dtype=jnp.int32)

    slot_own = slots_of(ids, expert_count, capacity, turn)
    padded = jnp.pad(slot_own, ((0, 0), (0, lanes - tok_rows)), constant_values=-1)
    place_wide = (numbers[None, :, None] == padded[:, None, :]).astype(jnp.bfloat16)
    is_own = numbers[None, :, None] == slot_own[:, None, :]
    place_own = is_own.astype(jnp.bfloat16)
    take_own = place_own.transpose(0, 2, 1)

    def staying(members):
        return [(s, s) for s in members]

    route_slots = jnp.sum(jnp.where(is_own, gate_weights[0, :, None, :, 0], 0.0), axis=-1)
    route = route_slots[:, :, None]

    def send_inputs(after):
        steps = list(range(2, section_count))
        sent = pl.pallas_call(
            partial(choose_kernel, steps),
            out_shape=[rows_shape] * len(steps),
            in_specs=[anywhere, in_smem] + [in_vmem] * 2,
            out_specs=[in_vmem] * len(steps),
            compiler_params=params(4),
            cost_estimate=light,
            name="choose_inputs",
        )(after, sec, tokens_in[0], cotangent[0])
        for step, rows_sent in zip(steps, sent):
            travel(step, rows_sent)

    def travel(step, rows_sent):
        came = lax.ppermute(rows_sent, "section", [(step, 0), (step - 1, section_count - 1)])
        tokens_all.append(came)
        cotangent_all[step - 1] = came
        return came

    def send_cotangents(micros):
        packed = jnp.einsum(
            "mjt,mtd->mjd",
            jnp.stack([place_own[m] for m in micros]),
            jnp.stack([cotangent_all[m] for m in micros]),
            preferred_element_type=jnp.float32,
        ).astype(jnp.bfloat16)
        spread = exchange(cut(packed), staying([first_back]), 1)
        for index, m in enumerate(micros):
            first_grads[m] = (spread, index)
        return spread

    cotangent_all = {section_count - 1: cotangent[0]}
    tokens_all = [tokens_in[0]]
    first_grads = {}
    ends = middle = []

    chunk = jax.ShapeDtypeStruct((rows, model_dim), jnp.bfloat16)
    rows_shape = jax.ShapeDtypeStruct((tok_rows, model_dim), jnp.bfloat16)
    matrix_shapes = [jax.ShapeDtypeStruct(m.shape, m.dtype) for m in own]
    wide = jax.ShapeDtypeStruct((rows, model_dim + lanes), jnp.bfloat16)
    light = pl.CostEstimate(flops=0, bytes_accessed=0, transcendentals=0)
    state_shapes = [
        jax.ShapeDtypeStruct((slots, model_dim + lanes), jnp.bfloat16),
        jax.ShapeDtypeStruct((slots, 2 * hidden_dim), jnp.float32),
        jax.ShapeDtypeStruct((slots, 2 * hidden_dim), jnp.float32),
        jax.ShapeDtypeStruct((slots, model_dim), jnp.float32),
    ]

    def load(core, after, matrices, loaded):
        return pl.pallas_call(
            partial(load_kernel, core),
            out_shape=matrix_shapes,
            in_specs=[in_smem, anywhere] + [in_hbm] * 3 + [in_vmem] * len(loaded),
            out_specs=[in_vmem] * 3,
            scratch_shapes=[pltpu.SemaphoreType.DMA((3,))],
            input_output_aliases={5 + number: number for number in range(len(loaded))},
            compiler_params=params(42),
            name=f"load_core_{core}",
        )(core_index, after, *matrices, *loaded)

    loaded = load(0, place_wide, own, [])
    saved = {}
    formers = {}
    former_shape = jax.ShapeDtypeStruct((slots, lanes), jnp.bfloat16)
    ahead = None
    behind = None
    results = None
    for slot in range(slot_count):
        forward_on = [s for s in sections if 0 <= slot - s < micro_count]
        if forward_on:
            has_first = 0 in forward_on
            has_rest = ahead is not None
            loading = slot == 0
            outs = pl.pallas_call(
                partial(forward_router, slot, micro_count, parts, has_first, has_rest),
                out_shape=[wide] * parts + ([former_shape] if has_rest else []),
                in_specs=[in_smem, in_vmem, in_vmem]
                + [in_vmem] * ((1 if has_first else 0) + (parts if has_rest else 0))
                + [anywhere] * (1 if loading else 0),
                out_specs=[in_vmem] * parts + ([in_vmem] if has_rest else []),
                compiler_params=params(4),
                cost_estimate=light,
                name=f"route_forward_{slot}",
            )(
                sec,
                route,
                place_wide,
                *([tokens_all[slot]] if has_first else []),
                *(ahead if has_rest else []),
                *(loaded[:1] if loading else []),
            )
            busy = slot > section_count
            moved = exchange(outs[:parts], staying(forward_on if busy else sections), 1)
            formers[slot] = outs[parts] if has_rest else None
            if loading:
                own = load(1, outs[0], own, loaded)
                weights = (*own, *other)
            later = {1: ends, 2: middle}.get(slot, [])
            def expert(closing):
                return pl.pallas_call(
                    partial(
                        forward_kernel,
                        slot,
                        micro_count,
                        parts,
                        loading,
                        len(later),
                        first_back,
                        closing,
                    ),
                    out_shape=([] if closing else [wide] * parts)
                    + state_shapes
                    + ([rows_shape] + matrix_shapes if loading else []),
                    in_specs=[in_smem, in_vmem]
                    + [in_vmem] * parts
                    + [in_vmem] * 3
                    + [in_hbm if loading else in_vmem] * 3
                    + [anywhere] * len(later)
                    + [in_vmem] * (2 if loading else 0),
                    out_specs=[in_vmem]
                    * ((0 if closing else parts) + 4 + (4 if loading else 0)),
                    scratch_shapes=[
                        pltpu.VMEM((slots, model_dim), jnp.bfloat16),
                        pltpu.VMEM((2, slots, hidden_dim), jnp.bfloat16),
                    ]
                    + ([pltpu.SemaphoreType.DMA((3,))] if loading else []),
                    compiler_params=params(28 if loading else 6),
                    cost_estimate=light,
                    name=f"expert_{'closing' if closing else 'forward'}_{slot}",
                )(
                    sec,
                    gain,
                    *moved,
                    *weights,
                    *later,
                    *([tokens_in[0], cotangent[0]] if loading else []),
                )

            def kept(states):
                x_rows, pre_gate, pre_up, made = states
                return (made, x_rows, pre_gate, pre_up)

            ahead = None
            if forward_on[0] < first_back:
                outs = expert(False)
                saved[slot] = kept(outs[parts : parts + 4])
                jobs = onto_next[:-1] if slot < section_count - 2 else onto_next
                ahead = exchange(outs[:parts], jobs, -1)
            if first_back in forward_on:
                saved_last = kept(expert(True))
            if loading:
                weights = (*own, *outs[parts + 5 :])
                came = travel(1, outs[parts + 4])
                ends = send_cotangents([0, section_count - 1])
                send_inputs(came)
                middle = send_cotangents(list(range(1, section_count - 1)))
        backward_on = [s for s in sections if 0 <= slot - 2 * first_back + s < micro_count]
        if backward_on:
            first, index = first_grads.get(slot - first_back, (behind, 0))
            if behind is None:
                grads = first
            else:
                first_time = len(backward_on) == 2 and first_back in backward_on
                grads = exchange(behind, onto_former[-1:] if first_time else onto_former, 1)
            states = []
            for s in backward_on:
                states += list(saved_last if s == first_back else saved[slot - 2 * first_back + 2 * s])
            outs = pl.pallas_call(
                partial(backward_kernel, slot, counts, backward_on, parts, index),
                out_shape=[wide] * parts,
                in_specs=[in_smem, in_vmem] + [pl.BlockSpec(memory_space=pl.ANY)] * (2 * parts)
                + [in_vmem] * 6
                + [pl.BlockSpec(memory_space=pl.ANY)] * len(states),
                out_specs=[in_vmem] * parts,
                scratch_shapes=[
                    pltpu.VMEM((slots, model_dim), jnp.bfloat16),
                    pltpu.VMEM((slots, model_dim + lanes), jnp.bfloat16),
                    pltpu.VMEM((slots, 2 * hidden_dim), jnp.float32),
                    pltpu.VMEM((slots, 2 * hidden_dim), jnp.float32),
                    pltpu.VMEM((slots, model_dim), jnp.float32),
                    pltpu.VMEM((slots, model_dim), jnp.bfloat16),
                    pltpu.VMEM((slots, model_dim), jnp.float32),
                    pltpu.SemaphoreType.DMA((4,)),
                    pltpu.SemaphoreType.DMA((parts,)),
                ],
                compiler_params=params(8),
                cost_estimate=light,
                name=f"expert_backward_{slot}",
            )(sec, gain, *grads, *first, *weights, *states)
            alone = slot < section_count + 1
            home = exchange(outs, staying(backward_on if alone else sections), -1)
            onward = [s for s in backward_on if s > 0]
            has_former = results is not None
            outs = pl.pallas_call(
                partial(backward_router, slot, counts, parts, has_former, onward),
                out_shape=[
                    jax.ShapeDtypeStruct((micro_count, tok_rows, model_dim), jnp.bfloat16),
                    jax.ShapeDtypeStruct((micro_count, tok_rows, lanes), jnp.float32),
                ]
                + [chunk] * (parts if onward else 0),
                in_specs=[in_smem, in_vmem, in_vmem]
                + [in_vmem] * parts
                + [in_hbm] * (2 if has_former else 0)
                + [in_vmem] * len(onward),
                out_specs=[in_hbm] * 2 + [in_vmem] * (parts if onward else 0),
                scratch_shapes=[
                    pltpu.VMEM((tok_rows, model_dim), jnp.bfloat16),
                    pltpu.VMEM((tok_rows, lanes), jnp.float32),
                    pltpu.SemaphoreType.DMA((2,)),
                ],
                input_output_aliases={3 + parts: 0, 4 + parts: 1} if has_former else {},
                compiler_params=params(4),
                cost_estimate=light,
                name=f"route_backward_{slot}",
            )(
                sec,
                take_own,
                place_wide,
                *home,
                *(results if has_former else []),
                *[formers[slot - 2 * first_back + 2 * s] for s in onward],
            )
            results = outs[:2]
            behind = outs[2:]

    return (results[0][None], results[1][None, :, :, :1])


def solution(mesh):
    return jax.shard_map(
        body,
        mesh=mesh,
        in_specs=(
            P("section", "expert", None),
            P("section", "expert", None),
            P("section", None),
            P("section", "expert", None, None),
            P("section", "expert", None, None),
            P("section", "expert", None, None),
            P("section", None, "expert", None),
            P("section", None, "expert", None),
        ),
        out_specs=(P("section", None, "expert", None), P("section", None, "expert", None)),
        check_vma=False,
    )
```

```python
from functools import partial

import jax
import jax.numpy as jnp
from jax import lax
from jax.experimental import pallas as pl
from jax.experimental.pallas import tpu as pltpu
from jax.sharding import PartitionSpec as P

epsilon = 1e-06
both = ("section", "expert")
last_with_last = (((1,), (1,)), ((), ()))

in_vmem = pl.BlockSpec(memory_space=pltpu.VMEM)
in_smem = pl.BlockSpec(memory_space=pltpu.SMEM)
in_hbm = pl.BlockSpec(memory_space=pltpu.HBM)
anywhere = pl.BlockSpec(memory_space=pl.ANY)
lanes = 128


def spans(total, size):
    size = size if total % size == 0 else total
    return [pl.ds(start, size) for start in range(0, total, size)]


def params(mib):
    return pltpu.CompilerParams(vmem_limit_bytes=mib * 2**20)


def product(left, right):
    return jnp.dot(left, right, preferred_element_type=jnp.float32)


def product_t(left, right):
    return lax.dot_general(left, right, last_with_last, preferred_element_type=jnp.float32)


def coded(column, number=None):
    high = column.astype(jnp.bfloat16).astype(jnp.float32)
    left = column - high
    middle = left.astype(jnp.bfloat16).astype(jnp.float32)
    lane = lax.broadcasted_iota(jnp.int32, (column.shape[0], lanes), 1)
    spread = jnp.where(lane == 1, middle, jnp.where(lane == 2, left - middle, 0.0))
    spread = jnp.where(lane == 0, high, spread)
    if number is not None:
        spread = jnp.where(lane == 3, number, spread)
    return spread.astype(jnp.bfloat16)


def decoded(columns):
    lane = lax.broadcasted_iota(jnp.int32, columns.shape, 1)
    values = jnp.where(lane < 3, columns.astype(jnp.float32), 0.0)
    return jnp.sum(values, axis=-1, keepdims=True)


def numbered(columns):
    lane = lax.broadcasted_iota(jnp.int32, columns.shape, 1)
    values = columns.astype(jnp.float32)
    number = jnp.sum(jnp.where(lane == 3, values, 0.0), axis=-1, keepdims=True)
    return (number == (lane + 1).astype(jnp.float32)).astype(jnp.bfloat16)


def load_kernel(after_ref, *refs):
    copies = [
        pltpu.make_async_copy(refs[number], refs[3 + number], refs[6].at[number])
        for number in range(3)
    ]
    for copy in copies:
        copy.start()
    for copy in copies:
        copy.wait()


def choose_kernel(steps, after_ref, sec_ref, tokens_ref, cotangent_ref, *out_refs):
    for step, out_ref in zip(steps, out_refs):

        @pl.when(sec_ref[0] == step)
        def _():
            out_ref[...] = tokens_ref[...]

        @pl.when(sec_ref[0] != step)
        def _():
            out_ref[...] = cotangent_ref[...]


def forward_kernel(slot, micro_count, parts, loading, later, *refs):
    sec_ref, gain_ref = refs[:2]
    x_refs = refs[2 : 2 + parts]
    given = refs[2 + parts : 8 + parts]
    rest = refs[8 + parts + later :]
    if loading:
        inputs, rest = rest[:2], rest[2:]
    out_refs = rest[:parts]
    save_x, save_gate, save_up, save_rows = rest[parts : 4 + parts]
    rest = rest[4 + parts :]
    if loading:
        choose_kernel([1], None, sec_ref, *inputs, rest[0])
        rest = rest[1:]
    half_refs = [given[0:3], rest[0:3] if loading else given[3:6]]
    copies = []
    if loading:
        normed, hidden, sems = rest[3:]
        copies = [
            pltpu.make_async_copy(given[3 + number], half_refs[1][number], sems.at[number])
            for number in range(3)
        ]
        for copy in copies:
            copy.start()
    else:
        normed, hidden = rest
    micro = slot - sec_ref[0]
    active = (micro >= 0) & (micro < micro_count)
    width = gain_ref.shape[1]
    hidden_dim = half_refs[0][0].shape[1]
    rows = x_refs[0].shape[0]

    @pl.when(active)
    def _():
        for part in range(parts):
            values = x_refs[part][:, :width].astype(jnp.float32)
            inv_rms = lax.rsqrt(jnp.mean(values * values, axis=-1, keepdims=True) + epsilon)
            here = pl.ds(part * rows, rows)
            normed[here, :] = (values * inv_rms * gain_ref[...]).astype(jnp.bfloat16)
            save_x[here, :] = x_refs[part][...]
            out_refs[part][:, width:] = x_refs[part][:, width:]

    for half in range(2):
        if loading and half == 1:
            copies[0].wait()
            copies[1].wait()

        @pl.when(active)
        def _():
            side = pl.ds(half * hidden_dim, hidden_dim)
            gate_pre = product(normed[...], half_refs[half][0][...])
            up_pre = product(normed[...], half_refs[half][1][...])
            save_gate[:, side] = gate_pre
            save_up[:, side] = up_pre
            hidden[half] = (gate_pre * jax.nn.sigmoid(gate_pre) * up_pre).astype(jnp.bfloat16)

    if loading:
        copies[2].wait()

    @pl.when(active)
    def _():
        route = [decoded(x_refs[part][:, width:]) for part in range(parts)]
        for span in spans(width, 256):
            made = product(hidden[0], half_refs[0][2][:, span])
            made = made + product(hidden[1], half_refs[1][2][:, span])
            save_rows[:, span] = made
            for part in range(parts):
                added = route[part] * made[part * rows : (part + 1) * rows]
                values = x_refs[part][:, span].astype(jnp.float32)
                out_refs[part][:, span] = (values + added).astype(jnp.bfloat16)


def backward_kernel(slot, counts, candidates, parts, index, *refs):
    section_count, micro_count = counts
    sec_ref, gain_ref = refs[:2]
    rest = refs[2:]
    arrived = rest[:parts]
    first = rest[parts : 2 * parts]
    rest = rest[2 * parts :]
    half_refs = [rest[0:3], rest[3:6]]
    rest = rest[6:]
    saved = {}
    for section in candidates:
        saved[section] = rest[:4]
        rest = rest[4:]
    out_refs = rest[:parts]
    (grad_buf, x_buf, pre_gate, pre_up, rows_buf, grad_rows, scaled_buf, state_sems, grad_sems) = rest[parts:]
    sec = sec_ref[0]
    micro = slot - 2 * (section_count - 1) + sec
    width = gain_ref.shape[1]
    hidden_dim = half_refs[0][0].shape[1]
    slots = grad_buf.shape[0]
    rows = slots // parts

    @pl.when((micro >= 0) & (micro < micro_count))
    def _():
        def for_section(section, act):
            @pl.when(sec == section)
            def _():
                for part in range(parts):
                    if section == section_count - 1:
                        source = first[part].at[index]
                    else:
                        source = arrived[part]
                    act(pltpu.make_async_copy(
                        source, grad_buf.at[pl.ds(part * rows, rows), :], grad_sems.at[part]
                    ))
                targets = (rows_buf, x_buf, pre_gate, pre_up)
                for number, target in enumerate(targets):
                    act(pltpu.make_async_copy(
                        saved[section][number], target, state_sems.at[number]
                    ))

        for section in candidates:
            for_section(section, lambda copy: copy.start())
        for section in candidates:
            for_section(section, lambda copy: copy.wait())
        route = decoded(x_buf[:, width:])
        gate_grad = jnp.zeros((slots, 1), jnp.float32)
        square = jnp.zeros((slots, 1), jnp.float32)
        for span in spans(width, 512):
            grad_f = grad_buf[:, span].astype(jnp.float32)
            gate_grad += jnp.sum(grad_f * rows_buf[:, span], axis=-1, keepdims=True)
            grad_rows[:, span] = (route * grad_f).astype(jnp.bfloat16)
            values = x_buf[:, span].astype(jnp.float32)
            square += jnp.sum(values * values, axis=-1, keepdims=True)
        gate_columns = coded(gate_grad)
        for part in range(parts):
            out_refs[part][:, width:] = gate_columns[part * rows : (part + 1) * rows]
        inv_rms = lax.rsqrt(square / width + epsilon)
        grads = []
        for half in range(2):
            side = pl.ds(half * hidden_dim, hidden_dim)
            grad_hidden = product_t(half_refs[half][2][...], grad_rows[...]).T
            gate_pre = pre_gate[:, side]
            sigma = jax.nn.sigmoid(gate_pre)
            grad_gate = grad_hidden * pre_up[:, side] * sigma * (1.0 + gate_pre * (1.0 - sigma))
            grad_up = grad_hidden * gate_pre * sigma
            grads.append((grad_gate.astype(jnp.bfloat16), grad_up.astype(jnp.bfloat16)))
        dotted = jnp.zeros((slots, 1), jnp.float32)
        for span in spans(width, 256):
            total = product_t(half_refs[0][0][span, :], grads[0][0])
            total = total + product_t(half_refs[0][1][span, :], grads[0][1])
            total = total + product_t(half_refs[1][0][span, :], grads[1][0])
            total = total + product_t(half_refs[1][1][span, :], grads[1][1])
            scaled = total.T * gain_ref[:, span]
            scaled_buf[:, span] = scaled
            dotted += jnp.sum(x_buf[:, span].astype(jnp.float32) * scaled, axis=-1, keepdims=True)
        back = inv_rms * inv_rms * inv_rms * (dotted / width)
        for span in spans(width, 512):
            grad_in = (
                grad_buf[:, span].astype(jnp.float32)
                + inv_rms * scaled_buf[:, span]
                - x_buf[:, span].astype(jnp.float32) * back
            ).astype(jnp.bfloat16)
            for part in range(parts):
                out_refs[part][:, span] = grad_in[part * rows : (part + 1) * rows]


def forward_router(slot, micro_count, parts, has_first, has_rest, *refs):
    sec_ref, route_ref, place_ref = refs[:3]
    rest = refs[3:]
    tokens_ref = rest[0] if has_first else None
    rest = rest[1:] if has_first else rest
    arrived = rest[:parts] if has_rest else None
    rest = rest[parts:] if has_rest else rest
    out_refs = rest[:parts]
    sec = sec_ref[0]
    micro = slot - sec
    width = out_refs[0].shape[1] - lanes
    rows = out_refs[0].shape[0]

    def put(number, table, source):
        place = place_ref[number].astype(jnp.float32)
        lane = lax.broadcasted_iota(jnp.int32, place.shape, 1)
        token = jnp.sum(place * (lane + 1).astype(jnp.float32), axis=-1, keepdims=True)
        columns = coded(route_ref[number], token)
        for part in range(parts):
            out_refs[part][:, width:] = columns[part * rows : (part + 1) * rows]
        for span in spans(width, 512):
            made = product(table, source(span)).astype(jnp.bfloat16)
            for part in range(parts):
                out_refs[part][:, span] = made[part * rows : (part + 1) * rows]

    if has_first:

        @pl.when(sec == 0)
        def _():
            table = place_ref[slot][:, : tokens_ref.shape[0]]
            put(slot, table, lambda span: tokens_ref[:, span])

    if has_rest:

        @pl.when((sec > 0) & (micro >= 0) & (micro < micro_count))
        def _():
            def source(span):
                return jnp.concatenate([ref[:, span] for ref in arrived], axis=0)

            former = numbered(source(pl.ds(width, lanes)))
            rest[parts][...] = former
            put(micro, product_t(place_ref[micro], former).astype(jnp.bfloat16), source)


def backward_router(slot, counts, parts, has_former, onward, *refs):
    section_count, micro_count = counts
    sec_ref, take_ref, place_ref = refs[:3]
    arrived = refs[3 : 3 + parts]
    rest = refs[3 + parts + (2 if has_former else 0) :]
    formers, rest = rest[: len(onward)], rest[len(onward) :]
    result, gates = rest[:2]
    out_refs = rest[2 : 2 + parts] if onward else []
    ordered, gate_rows, sems = rest[2 + len(out_refs) :]
    sec = sec_ref[0]
    micro = slot - 2 * (section_count - 1) + sec
    width = arrived[0].shape[1] - lanes
    rows = arrived[0].shape[0]

    @pl.when((micro >= 0) & (micro < micro_count))
    def _():
        def source(span):
            return jnp.concatenate([ref[:, span] for ref in arrived], axis=0)

        for section, former in zip(onward, formers):

            @pl.when(sec == section)
            def _():
                table = product_t(former[...], place_ref[micro]).astype(jnp.bfloat16)
                for span in spans(width, 512):
                    made = product(table, source(span)).astype(jnp.bfloat16)
                    for part in range(parts):
                        out_refs[part][:, span] = made[part * rows : (part + 1) * rows]

        for span in spans(width, 512):
            ordered[:, span] = product(take_ref[micro], source(span)).astype(jnp.bfloat16)
        copy = pltpu.make_async_copy(ordered, result.at[micro], sems.at[0])
        copy.start()
        columns = decoded(product(take_ref[micro], source(pl.ds(width, lanes))))
        gate_rows[...] = jnp.broadcast_to(columns, gate_rows.shape)
        gate_copy = pltpu.make_async_copy(gate_rows, gates.at[micro], sems.at[1])
        gate_copy.start()
        copy.wait()
        gate_copy.wait()


def slots_of(route_ids, expert_count, capacity, turn):
    count = route_ids.shape[1]
    before = jnp.arange(count)[None, :] < jnp.arange(count)[:, None]
    alike = (route_ids[:, None, :] == route_ids[:, :, None]) & before
    position = jnp.sum(alike.astype(jnp.int32), axis=-1)
    return lax.rem(route_ids - turn + expert_count, expert_count) * capacity + position


def body(tokens_in, cotangent, norm_gain, w_gate, w_up, w_down, expert_ids, gate_weights):
    section_count = lax.axis_size("section")
    device_count = lax.axis_size("expert")
    section = lax.axis_index("section")
    place = lax.axis_index("expert") // 2
    expert_count = device_count // 2
    micro_count = expert_ids.shape[1]
    tok_rows = expert_ids.shape[2]
    model_dim = tokens_in.shape[2]
    hidden_dim = w_gate.shape[3]
    capacity = 2 * ((tok_rows + expert_count - 1) // expert_count)
    slots = expert_count * capacity
    by_permute = capacity % 16 == 0
    parts = expert_count if by_permute else 1
    rows = slots // parts
    turn = place if by_permute else jnp.int32(0)
    counts = (section_count, micro_count)
    first_back = section_count - 1
    slot_count = micro_count + 2 * (section_count - 1)
    sections = list(range(section_count))

    def exchange(chunks, jobs, direction):
        if by_permute:
            moved = [None] * parts
            for step in sorted(range(parts), key=lambda k: -min(k, parts - k)):
                if step == 0 and all(a == b for a, b in jobs):
                    moved[0] = chunks[0]
                    continue
                pairs = [
                    (
                        a * device_count + 2 * z + core,
                        b * device_count + 2 * ((z + direction * step) % expert_count) + core,
                    )
                    for a, b in jobs
                    for z in range(expert_count)
                    for core in range(2)
                ]
                moved[step] = lax.ppermute(chunks[step], both, sorted(pairs))
            return moved
        (block,) = chunks
        shape = block.shape
        spread = block.reshape(-1, expert_count, capacity, shape[-1])
        groups = [[2 * z + core for z in range(expert_count)] for core in range(2)]
        spread = lax.all_to_all(
            spread, "expert", split_axis=1, concat_axis=1, tiled=True, axis_index_groups=groups
        )
        block = spread.reshape(shape)
        if any(a != b for a, b in jobs):
            block = lax.ppermute(block, "section", jobs)
        return [block]

    def cut(block):
        return [block[:, part * rows : (part + 1) * rows] for part in range(parts)]

    own = (w_gate[0, 0], w_up[0, 0], w_down[0, 0])
    swap = [(i, i ^ 1) for i in range(device_count)]
    other = [lax.ppermute(matrix, "expert", swap) for matrix in own]

    sec = section.reshape(1).astype(jnp.int32)
    gain = norm_gain
    ids = expert_ids[0, :, :, 0]
    onto_next = [(s, s + 1) for s in sections[:-1]]
    onto_former = [(s + 1, s) for s in sections[:-1]]
    numbers = jnp.arange(slots, dtype=jnp.int32)

    slot_own = slots_of(ids, expert_count, capacity, turn)
    padded = jnp.pad(slot_own, ((0, 0), (0, lanes - tok_rows)), constant_values=-1)
    place_wide = (numbers[None, :, None] == padded[:, None, :]).astype(jnp.bfloat16)
    is_own = numbers[None, :, None] == slot_own[:, None, :]
    place_own = is_own.astype(jnp.bfloat16)
    take_own = place_own.transpose(0, 2, 1)

    def staying(members):
        return [(s, s) for s in members]

    route_slots = jnp.sum(jnp.where(is_own, gate_weights[0, :, None, :, 0], 0.0), axis=-1)
    route = route_slots[:, :, None]

    def send_inputs(after):
        steps = list(range(2, section_count))
        sent = pl.pallas_call(
            partial(choose_kernel, steps),
            out_shape=[rows_shape] * len(steps),
            in_specs=[anywhere, in_smem] + [in_vmem] * 2,
            out_specs=[in_vmem] * len(steps),
            compiler_params=params(4),
            cost_estimate=light,
            name="choose_inputs",
        )(after, sec, tokens_in[0], cotangent[0])
        for step, rows_sent in zip(steps, sent):
            travel(step, rows_sent)

    def travel(step, rows_sent):
        came = lax.ppermute(rows_sent, "section", [(step, 0), (step - 1, section_count - 1)])
        tokens_all.append(came)
        cotangent_all[step - 1] = came
        return came

    def send_cotangents(micros):
        packed = jnp.einsum(
            "mjt,mtd->mjd",
            jnp.stack([place_own[m] for m in micros]),
            jnp.stack([cotangent_all[m] for m in micros]),
            preferred_element_type=jnp.float32,
        ).astype(jnp.bfloat16)
        spread = exchange(cut(packed), staying([first_back]), 1)
        for index, m in enumerate(micros):
            first_grads[m] = (spread, index)
        return spread

    cotangent_all = {section_count - 1: cotangent[0]}
    tokens_all = [tokens_in[0]]
    first_grads = {}
    ends = middle = []

    chunk = jax.ShapeDtypeStruct((rows, model_dim), jnp.bfloat16)
    rows_shape = jax.ShapeDtypeStruct((tok_rows, model_dim), jnp.bfloat16)
    matrix_shapes = [jax.ShapeDtypeStruct(m.shape, m.dtype) for m in own]
    wide = jax.ShapeDtypeStruct((rows, model_dim + lanes), jnp.bfloat16)
    light = pl.CostEstimate(flops=0, bytes_accessed=0, transcendentals=0)
    state_shapes = [
        jax.ShapeDtypeStruct((slots, model_dim + lanes), jnp.bfloat16),
        jax.ShapeDtypeStruct((slots, 2 * hidden_dim), jnp.float32),
        jax.ShapeDtypeStruct((slots, 2 * hidden_dim), jnp.float32),
        jax.ShapeDtypeStruct((slots, model_dim), jnp.float32),
    ]

    saved = {}
    formers = {}
    former_shape = jax.ShapeDtypeStruct((slots, lanes), jnp.bfloat16)
    ahead = None
    behind = None
    results = None
    for slot in range(slot_count):
        forward_on = [s for s in sections if 0 <= slot - s < micro_count]
        if forward_on:
            has_first = 0 in forward_on
            has_rest = ahead is not None
            loading = slot == 0
            outs = pl.pallas_call(
                partial(forward_router, slot, micro_count, parts, has_first, has_rest),
                out_shape=[wide] * parts + ([former_shape] if has_rest else []),
                in_specs=[in_smem, in_vmem, in_vmem]
                + [in_vmem] * ((1 if has_first else 0) + (parts if has_rest else 0)),
                out_specs=[in_vmem] * parts + ([in_vmem] if has_rest else []),
                compiler_params=params(4),
                cost_estimate=light,
                name=f"route_forward_{slot}",
            )(
                sec,
                route,
                place_wide,
                *([tokens_all[slot]] if has_first else []),
                *(ahead if has_rest else []),
            )
            busy = slot > section_count
            moved = exchange(outs[:parts], staying(forward_on if busy else sections), 1)
            formers[slot] = outs[parts] if has_rest else None
            if loading:
                own = pl.pallas_call(
                    load_kernel,
                    out_shape=matrix_shapes,
                    in_specs=[anywhere] + [in_hbm] * 3,
                    out_specs=[in_vmem] * 3,
                    scratch_shapes=[pltpu.SemaphoreType.DMA((3,))],
                    compiler_params=params(42),
                    name="load_weights",
                )(outs[0], *own)
                weights = (*own, *other)
            later = {1: ends, 2: middle}.get(slot, [])
            outs = pl.pallas_call(
                partial(forward_kernel, slot, micro_count, parts, loading, len(later)),
                out_shape=[wide] * parts
                + state_shapes
                + ([rows_shape] + matrix_shapes if loading else []),
                in_specs=[in_smem, in_vmem]
                + [in_vmem] * parts
                + [in_vmem] * 3
                + [in_hbm if loading else in_vmem] * 3
                + [anywhere] * len(later)
                + [in_vmem] * (2 if loading else 0),
                out_specs=[in_vmem] * (parts + 4 + (4 if loading else 0)),
                scratch_shapes=[
                    pltpu.VMEM((slots, model_dim), jnp.bfloat16),
                    pltpu.VMEM((2, slots, hidden_dim), jnp.bfloat16),
                ]
                + ([pltpu.SemaphoreType.DMA((3,))] if loading else []),
                compiler_params=params(28 if loading else 6),
                cost_estimate=light,
                name=f"expert_forward_{slot}",
            )(sec, gain, *moved, *weights, *later, *([tokens_in[0], cotangent[0]] if loading else []))
            x_rows, pre_gate, pre_up, made = outs[parts : parts + 4]
            saved[slot] = (made, x_rows, pre_gate, pre_up)
            more = any(s + 1 < section_count for s in forward_on)
            jobs = onto_next[:-1] if slot < section_count - 2 else onto_next
            ahead = exchange(outs[:parts], jobs, -1) if more else None
            if loading:
                weights = (*own, *outs[parts + 5 :])
                came = travel(1, outs[parts + 4])
                ends = send_cotangents([0, section_count - 1])
                send_inputs(came)
                middle = send_cotangents(list(range(1, section_count - 1)))
        backward_on = [s for s in sections if 0 <= slot - 2 * first_back + s < micro_count]
        if backward_on:
            first, index = first_grads.get(slot - first_back, (behind, 0))
            if behind is None:
                grads = first
            else:
                first_time = len(backward_on) == 2 and first_back in backward_on
                grads = exchange(behind, onto_former[-1:] if first_time else onto_former, 1)
            states = []
            for s in backward_on:
                states += list(saved[slot - 2 * first_back + 2 * s])
            outs = pl.pallas_call(
                partial(backward_kernel, slot, counts, backward_on, parts, index),
                out_shape=[wide] * parts,
                in_specs=[in_smem, in_vmem] + [pl.BlockSpec(memory_space=pl.ANY)] * (2 * parts)
                + [in_vmem] * 6
                + [pl.BlockSpec(memory_space=pl.ANY)] * len(states),
                out_specs=[in_vmem] * parts,
                scratch_shapes=[
                    pltpu.VMEM((slots, model_dim), jnp.bfloat16),
                    pltpu.VMEM((slots, model_dim + lanes), jnp.bfloat16),
                    pltpu.VMEM((slots, 2 * hidden_dim), jnp.float32),
                    pltpu.VMEM((slots, 2 * hidden_dim), jnp.float32),
                    pltpu.VMEM((slots, model_dim), jnp.float32),
                    pltpu.VMEM((slots, model_dim), jnp.bfloat16),
                    pltpu.VMEM((slots, model_dim), jnp.float32),
                    pltpu.SemaphoreType.DMA((4,)),
                    pltpu.SemaphoreType.DMA((parts,)),
                ],
                compiler_params=params(8),
                cost_estimate=light,
                name=f"expert_backward_{slot}",
            )(sec, gain, *grads, *first, *weights, *states)
            alone = slot < section_count + 1
            home = exchange(outs, staying(backward_on if alone else sections), -1)
            onward = [s for s in backward_on if s > 0]
            has_former = results is not None
            outs = pl.pallas_call(
                partial(backward_router, slot, counts, parts, has_former, onward),
                out_shape=[
                    jax.ShapeDtypeStruct((micro_count, tok_rows, model_dim), jnp.bfloat16),
                    jax.ShapeDtypeStruct((micro_count, tok_rows, lanes), jnp.float32),
                ]
                + [chunk] * (parts if onward else 0),
                in_specs=[in_smem, in_vmem, in_vmem]
                + [in_vmem] * parts
                + [in_hbm] * (2 if has_former else 0)
                + [in_vmem] * len(onward),
                out_specs=[in_hbm] * 2 + [in_vmem] * (parts if onward else 0),
                scratch_shapes=[
                    pltpu.VMEM((tok_rows, model_dim), jnp.bfloat16),
                    pltpu.VMEM((tok_rows, lanes), jnp.float32),
                    pltpu.SemaphoreType.DMA((2,)),
                ],
                input_output_aliases={3 + parts: 0, 4 + parts: 1} if has_former else {},
                compiler_params=params(4),
                cost_estimate=light,
                name=f"route_backward_{slot}",
            )(
                sec,
                take_own,
                place_wide,
                *home,
                *(results if has_former else []),
                *[formers[slot - 2 * first_back + 2 * s] for s in onward],
            )
            results = outs[:2]
            behind = outs[2:]

    return (results[0][None], results[1][None, :, :, :1])


def solution(mesh):
    return jax.shard_map(
        body,
        mesh=mesh,
        in_specs=(
            P("section", "expert", None),
            P("section", "expert", None),
            P("section", None),
            P("section", "expert", None, None),
            P("section", "expert", None, None),
            P("section", "expert", None, None),
            P("section", None, "expert", None),
            P("section", None, "expert", None),
        ),
        out_specs=(P("section", None, "expert", None), P("section", None, "expert", None)),
        check_vma=False,
    )
```
